32 devices in a mesh: stack: 2 (over y), acq: 4 (over x, core), rng: 4 (over z).
Axes of the slice: x: 2, y: 2, z: 4, core: 2. Of those that a mesh axis runs over, the one named last changes fastest.
Arguments:
- images: bfloat16 [2, 16, 128, 1024], P(None, ('stack', 'acq'), None, 'rng'), parts along dimension 1, may hold values from -16 to 16
- pairing: int32 [3, 8], replicated, may hold values from 0 to 7, as said below
- tile_offsets: int32 [3, 2], replicated, may hold values from 0 to 31, as said below
Outputs:
- coherence: float32 [3, 16, 64, 1024], P(None, ('stack', 'acq'), None, 'rng'), parts along dimension 1
- filtered: bfloat16 [2, 3, 16, 64, 1024], P(None, None, ('stack', 'acq'), None, 'rng'), parts along dimension 2
The draws below stay inside these ranges and needn't reach their ends.
There are 2 independent parts, one for each index of `stack`. The reference program is written for one: setup_inputs(seed, part) draws one part's arguments, and reference() takes and returns one part's arrays. A program takes and returns all parts, laid end to end along the dimension named above; an argument that names none is the same for every part. Nothing has to cross between parts.
Inputs may be any that keep to these rules, and one draw needn't show every extreme that they name: In matching m, the partner of acquisition a lies in group (a // 2) XOR (m + 1), and the pairing is an involution. `tile_offsets`: both ends occur in every draw.
All inputs are finite; a program needn't handle non-finite values.
Results may differ from the reference program's by a relative error of at most 0.001.
Values may be sent and summed in bfloat16 or wider, within the bound.
A program may use at most 64 MiB of HBM per device.

```python
import jax
import jax.numpy as jnp
from jax import lax

LINES = 128
MATCH = 3
REACH = 32
PATCH = 32
HALF = 64
RANGE = 1024
ACQS = 8


def draw_images(key, part):
    folded = jax.random.fold_in(key, 11)
    subkeys = jax.random.split(folded, 7)
    scene_real = jax.random.normal(subkeys[0], (LINES, RANGE), jnp.float32)
    scene_imag = jax.random.normal(subkeys[1], (LINES, RANGE), jnp.float32)
    noise = jax.random.normal(subkeys[2], (2, ACQS, LINES, RANGE), jnp.float32)
    keeping = jax.random.uniform(subkeys[3], (ACQS, 1, 1), jnp.float32, 0.4, 0.9)
    line_rate = jax.random.uniform(subkeys[4], (ACQS, 1, 1), jnp.float32, -0.04, 0.04)
    cell_rate = jax.random.uniform(subkeys[5], (ACQS, 1, 1), jnp.float32, -0.04, 0.04)
    starting = jax.random.uniform(subkeys[6], (ACQS, 1, 1), jnp.float32, -jnp.pi, jnp.pi)
    line_index = jnp.arange(LINES, dtype=jnp.float32)[None, :, None]
    cell_index = jnp.arange(RANGE, dtype=jnp.float32)[None, None, :]
    phases = line_rate * line_index + cell_rate * cell_index + starting
    common = jnp.sqrt(keeping)
    private = jnp.sqrt(1.0 - keeping)
    cosines = jnp.cos(phases)
    sines = jnp.sin(phases)
    real_part = (common * (scene_real * cosines - scene_imag * sines) + private * noise[0]) * 0.7071
    imag_part = (common * (scene_real * sines + scene_imag * cosines) + private * noise[1]) * 0.7071
    return jnp.clip(jnp.stack([real_part, imag_part]), -16.0, 16.0).astype(jnp.bfloat16)


def draw_pairing(key, part):
    crossing = jax.random.randint(jax.random.fold_in(key, 21), (MATCH, ACQS // 2), 0, 2)
    acquired = jnp.arange(ACQS)
    grouped = acquired // 2
    member = acquired % 2
    matched = []
    for matching in range(MATCH):
        partner_group = jnp.bitwise_xor(grouped, matching + 1)
        lowest = jnp.minimum(grouped, partner_group)
        flipped = crossing[matching][lowest]
        matched.append(2 * partner_group + jnp.bitwise_xor(member, flipped))
    return jnp.stack(matched).astype(jnp.int32)


def draw_tile_offsets(key, part):
    folded = jax.random.fold_in(key, 31)
    picks = jax.random.randint(jax.random.fold_in(folded, 1), (2 * MATCH,), 0, PATCH)
    highest = jax.random.randint(jax.random.fold_in(folded, 2), (), 0, 2 * MATCH)
    lowest = (highest + 1 + jax.random.randint(jax.random.fold_in(folded, 3), (), 0, 2 * MATCH - 1)) % (2 * MATCH)
    counter = jnp.arange(2 * MATCH)
    picks = jnp.where(counter == highest, PATCH - 1, jnp.where(counter == lowest, 0, picks))
    return picks.reshape(MATCH, 2).astype(jnp.int32)


def setup_inputs(seed: int = 0, part: int = 0) -> dict:
    splits = jax.random.split(jax.random.key(seed), 4)
    part_keys = jax.random.split(jax.random.fold_in(splits[3], part), 4)
    images = draw_images(jax.random.fold_in(jax.random.fold_in(splits[3], part), 71), part)
    pairing = draw_pairing(jax.random.fold_in(splits[3], 71), part)
    tile_offsets = draw_tile_offsets(jax.random.fold_in(splits[3], 71), part)
    return dict(images=images, pairing=pairing, tile_offsets=tile_offsets)


EPSILON = 1e-06
HIGHEST = lax.Precision.HIGHEST

def gauss_band(height, breadth, offset, float_type):
    spread = jnp.arange(height)[:, None] - jnp.arange(breadth)[None, :] - offset
    width_scale = REACH / 8.0
    weights = jnp.exp(-(spread * spread).astype(float_type) / (2.0 * width_scale * width_scale))
    return jnp.where(jnp.abs(spread) <= REACH, weights, jnp.zeros_like(weights))

def dft_tables(float_type):
    counter = jnp.arange(PATCH)
    angles = 2.0 * jnp.pi / PATCH * (counter[:, None] * counter[None, :] % PATCH).astype(float_type)
    return (jnp.cos(angles), jnp.sin(angles))

def transform(table, field):
    return jnp.einsum('uy,aybx->aubx', table, field, precision=HIGHEST)

def transform_cols(table, field):
    return jnp.einsum('vx,aubx->aubv', table, field, precision=HIGHEST)

def patch_filter(real_part, imag_part, row_offset, col_offset):
    height = real_part.shape[0]
    breadth = real_part.shape[1] - 2 * REACH
    row_count = height // PATCH + 1
    col_count = breadth // PATCH + 1
    cosine_table, sine_table = dft_tables(real_part.dtype)

    def to_tiles(field):
        padded = jnp.pad(field, ((REACH, REACH), (0, 0)))
        window = lax.dynamic_slice(padded, (row_offset, col_offset), (height + PATCH, breadth + PATCH))
        return window.reshape(row_count, PATCH, col_count, PATCH)
    tile_real = to_tiles(real_part)
    tile_imag = to_tiles(imag_part)
    rowwise_real = transform(cosine_table, tile_real) + transform(sine_table, tile_imag)
    rowwise_imag = transform(cosine_table, tile_imag) - transform(sine_table, tile_real)
    freq_real = transform_cols(cosine_table, rowwise_real) + transform_cols(sine_table, rowwise_imag)
    freq_imag = transform_cols(cosine_table, rowwise_imag) - transform_cols(sine_table, rowwise_real)
    magnitude = jnp.sqrt(jnp.sqrt(freq_real * freq_real + freq_imag * freq_imag + EPSILON))
    scaling = magnitude / (lax.optimization_barrier(jnp.mean(magnitude, axis=(1, 3), keepdims=True)) + EPSILON)
    weighted_real = freq_real * scaling
    weighted_imag = freq_imag * scaling
    back_real = transform(cosine_table, weighted_real) - transform(sine_table, weighted_imag)
    back_imag = transform(cosine_table, weighted_imag) + transform(sine_table, weighted_real)
    final_real = (transform_cols(cosine_table, back_real) - transform_cols(sine_table, back_imag)) / (PATCH * PATCH)
    final_imag = (transform_cols(cosine_table, back_imag) + transform_cols(sine_table, back_real)) / (PATCH * PATCH)
    final_real = final_real.reshape(height + PATCH, breadth + PATCH)
    final_imag = final_imag.reshape(height + PATCH, breadth + PATCH)
    starts = (PATCH - row_offset, PATCH - col_offset)
    return (lax.dynamic_slice(final_real, starts, (height, breadth)), lax.dynamic_slice(final_imag, starts, (height, breadth)))

def pair_fields(local_image, remote_image):
    local_real, local_imag = (local_image[0], local_image[1])
    remote_real, remote_imag = (remote_image[0], remote_image[1])
    return jnp.stack([local_real * remote_real + local_imag * remote_imag, local_imag * remote_real - local_real * remote_imag, local_real * local_real + local_imag * local_imag, remote_real * remote_real + remote_imag * remote_imag], axis=-3)

def coherence_of(smoothed):
    inter_real = smoothed[..., 0, :, :]
    inter_imag = smoothed[..., 1, :, :]
    return (inter_real * inter_real + inter_imag * inter_imag) / (smoothed[..., 2, :, :] * smoothed[..., 3, :, :] + EPSILON)

def smooth_range(fields):
    field_count, height, breadth = fields.shape
    blocks = breadth // 128
    padded = jnp.pad(fields, ((0, 0), (0, 0), (REACH, 128 - REACH)))
    tiled_view = padded.reshape(field_count, height, blocks + 1, 128)
    window = jnp.concatenate([tiled_view[:, :, :-1], tiled_view[:, :, 1:, :2 * REACH]], axis=3)
    matrix = gauss_band(128 + 2 * REACH, 128, REACH, fields.dtype)
    smoothed = jnp.einsum('fhbj,jc->fhbc', window, matrix, precision=HIGHEST)
    return smoothed.reshape(field_count, height, breadth)

def reference(images, pairing, tile_offsets):
    coherence_rows = []
    filtered_rows = []
    for matching in range(MATCH):
        for acquired in range(ACQS):
            partner = pairing[matching, acquired]
            grouped = acquired // 2
            upper_half = 1 if grouped > grouped ^ matching + 1 else 0
            first_line = upper_half * HALF
            local_image = images[:, acquired, first_line:first_line + HALF].astype(jnp.float32)
            remote_image = lax.dynamic_index_in_dim(images, partner, 1, keepdims=False)[:, first_line:first_line + HALF].astype(jnp.float32)
            fields = pair_fields(local_image, remote_image)
            range_smoothed = smooth_range(fields)
            azimuth = gauss_band(HALF, HALF, 0, fields.dtype)
            smoothed = jnp.einsum('ih,fhc->fic', azimuth, range_smoothed, precision=HIGHEST)
            coherence_rows.append(coherence_of(smoothed))
            padded = jnp.pad(fields[:2], ((0, 0), (0, 0), (REACH, REACH)))
            filtered_real, filtered_imag = patch_filter(padded[0], padded[1], tile_offsets[matching, 0], tile_offsets[matching, 1])
            filtered_rows.append(jnp.stack([filtered_real, filtered_imag]))
    coherence = jnp.stack(coherence_rows).reshape(MATCH, ACQS, HALF, RANGE)
    filtered = jnp.stack(filtered_rows).reshape(MATCH, ACQS, 2, HALF, RANGE).transpose(2, 0, 1, 3, 4).astype(jnp.bfloat16)
    return (coherence, filtered)
```

```python
import functools

import jax
import jax.numpy as jnp
import ml_dtypes
import numpy as np
from jax import lax
from jax.experimental import pallas as pl
from jax.experimental.pallas import tpu as pltpu
from jax.sharding import PartitionSpec as P

MATCH = 3
REACH = 32
PATCH = 32
EPSILON = 1e-06
LANES = 128
MESH = pl.DeviceIdType.MESH
BF16 = jnp.bfloat16
F32 = jnp.float32


def halves(table):
    high = table.astype(ml_dtypes.bfloat16)
    low = (table - high.astype(np.float64)).astype(ml_dtypes.bfloat16)
    return high, low


def gauss(distance):
    weights = np.exp(-(distance.astype(np.float64) ** 2) / (2.0 * (REACH / 8.0) ** 2))
    return np.where(np.abs(distance) <= REACH, weights, 0.0)


def range_table(breadth):
    lane = np.arange(breadth + LANES)
    cell = np.where(lane >= breadth + LANES - REACH, lane - breadth - LANES, lane)
    used = cell < breadth + REACH
    weights = gauss(cell[:, None] - np.arange(breadth)[None, :])
    return np.stack(halves(weights * used[:, None]))


def azimuth_table(height):
    line = np.arange(height)
    return np.stack(halves(gauss(line[:, None] - line[None, :])))


def column_tables():
    counter = np.arange(PATCH)
    angles = 2.0 * np.pi / PATCH * (counter[:, None] * counter[None, :] % PATCH)
    eye = np.eye(LANES // PATCH)
    cosine, sine = np.kron(eye, np.cos(angles)), np.kron(eye, np.sin(angles))
    there = np.block([[cosine, -sine], [sine, cosine]])
    back = np.block([[cosine, sine], [-sine, cosine]])
    return np.stack(halves(there) + halves(back))


def row_tables(height):
    count = height // PATCH + 1
    line = np.arange(height)
    offset = np.arange(PATCH)[:, None, None, None]
    where = line[None, None, None, :] - offset
    inside = (where + PATCH) // PATCH == np.arange(count)[None, :, None, None]
    frequency = np.arange(PATCH)[None, None, :, None]
    angles = 2.0 * np.pi / PATCH * (frequency * where % PATCH)
    shape = (PATCH, count * PATCH, height)
    cosine = (np.cos(angles) * inside).reshape(shape)
    sine = (np.sin(angles) * inside).reshape(shape)
    there = np.concatenate(
        [np.concatenate([cosine, sine], 2), np.concatenate([-sine, cosine], 2)], 1
    )
    back = there.transpose(0, 2, 1) / (PATCH * PATCH)
    return np.concatenate(halves(there), 2), np.concatenate(halves(back), 2)


def exchange_kernel(
    images, mains, lefts, rights, own_left, own_right, heads, tails, send_sem, recv_sem
):
    stack, group, strip = lax.axis_index("stack"), lax.axis_index("acq"), lax.axis_index("rng")
    strips = lax.axis_size("rng")
    height = images.shape[2] // 2
    breadth = images.shape[3]
    near, far = jnp.bitwise_xor(group, 1), jnp.bitwise_xor(group, 2)
    has_left, has_right = strip > 0, strip < strips - 1

    barrier = pltpu.get_barrier_semaphore()

    def greet(g, r):
        pl.semaphore_signal(barrier, inc=1, device_id=(stack, g, r), device_id_type=MESH)

    greet(near, strip)
    greet(far, strip)

    @pl.when(has_left)
    def _():
        for g in (group, near, far):
            greet(g, strip - 1)

    @pl.when(has_right)
    def _():
        for g in (group, near, far):
            greet(g, strip + 1)

    lane = lax.broadcasted_iota(jnp.int32, (2 * height, LANES), 1) // REACH
    head = jnp.zeros((2 * height, LANES), F32)
    tail = jnp.zeros((2 * height, LANES), F32)
    for part in range(2):
        for member in range(2):
            place = 2 * part + member
            first = images[part, member, :, :LANES].astype(F32)
            last = images[part, member, :, breadth - LANES :].astype(F32)
            if place:
                first = pltpu.roll(first, REACH * place, 1)
            if place != 3:
                last = pltpu.roll(last, REACH * (place + 1), 1)
            head = jnp.where(lane == place, first, head)
            tail = jnp.where(lane == place, last, tail)
    heads[...] = head.astype(BF16)
    tails[...] = tail.astype(BF16)

    pl.semaphore_wait(
        barrier, 2 + 3 * has_left.astype(jnp.int32) + 3 * has_right.astype(jnp.int32)
    )

    def copy(source, target, index, g, r):
        return pltpu.make_async_remote_copy(
            src_ref=source,
            dst_ref=target,
            send_sem=send_sem.at[index],
            recv_sem=recv_sem.at[index],
            device_id=(stack, g, r),
            device_id_type=MESH,
        )

    def rows(g):
        return pl.ds(pl.multiple_of((g > group).astype(jnp.int32) * height, height), height)

    main_far = copy(images.at[:, :, rows(far), :], mains.at[1], 0, far, strip)
    main_near = copy(images.at[:, :, rows(near), :], mains.at[0], 1, near, strip)
    main_far.start()
    right_far = copy(heads.at[rows(far), :], rights.at[1], 2, far, strip - 1)
    right_near = copy(heads.at[rows(near), :], rights.at[0], 3, near, strip - 1)
    right_own = copy(heads, own_right, 4, group, strip - 1)
    left_far = copy(tails.at[rows(far), :], lefts.at[1], 5, far, strip + 1)
    left_near = copy(tails.at[rows(near), :], lefts.at[0], 6, near, strip + 1)
    left_own = copy(tails, own_left, 7, group, strip + 1)

    @pl.when(has_left)
    def _():
        right_far.start()
        right_near.start()
        right_own.start()

    @pl.when(has_right)
    def _():
        left_far.start()
        left_near.start()
        left_own.start()

    main_near.start()

    main_on = copy(mains.at[1], mains.at[2], 8, near, strip)
    right_on = copy(rights.at[1], rights.at[2], 9, near, strip)
    left_on = copy(lefts.at[1], lefts.at[2], 10, near, strip)

    @pl.when(has_right)
    def _():
        right_far.wait_recv()
        right_on.start()

    @pl.when(has_left)
    def _():
        left_far.wait_recv()
        left_on.start()

    main_far.wait_recv()
    main_on.start()
    main_near.wait()
    main_far.wait_send()

    @pl.when(has_left)
    def _():
        right_far.wait_send()
        right_near.wait_send()
        right_own.wait_send()
        left_near.wait_recv()
        left_own.wait_recv()
        left_on.wait()

    @pl.when(has_right)
    def _():
        left_far.wait_send()
        left_near.wait_send()
        left_own.wait_send()
        right_near.wait_recv()
        right_own.wait_recv()
        right_on.wait()

    main_on.wait()


def exchange(images):
    height, breadth = images.shape[2] // 2, images.shape[3]
    shapes = (
        (MATCH, 2, 2, height, breadth),
        (MATCH, height, LANES),
        (MATCH, height, LANES),
        (2 * height, LANES),
        (2 * height, LANES),
    )
    return pl.pallas_call(
        exchange_kernel,
        out_shape=[jax.ShapeDtypeStruct(shape, BF16) for shape in shapes],
        in_specs=[pl.BlockSpec(memory_space=pltpu.VMEM)],
        out_specs=[pl.BlockSpec(memory_space=pl.ANY)] * 5,
        scratch_shapes=[
            pltpu.VMEM((2 * height, LANES), BF16),
            pltpu.VMEM((2 * height, LANES), BF16),
            pltpu.SemaphoreType.DMA((11,)),
            pltpu.SemaphoreType.DMA((11,)),
        ],
        compiler_params=pltpu.CompilerParams(collective_id=0, has_side_effects=True),
        name="exchange",
    )(images)


def split(value):
    high = value.astype(BF16)
    return high, (value - high.astype(F32)).astype(BF16)


def times_table(value, high, low):
    value_high, value_low = split(value)
    return jnp.dot(
        jnp.concatenate([value_high, value_low, value_high], 1),
        jnp.concatenate([high, high, low], 0),
        preferred_element_type=F32,
    )


def table_times(high, low, value):
    value_high, value_low = split(value)
    return jnp.dot(
        jnp.concatenate([high, high, low], 1),
        jnp.concatenate([value_high, value_low, value_high], 0),
        preferred_element_type=F32,
    )


def pair_kernel(
    pairing,
    offsets,
    images,
    own_left,
    own_right,
    mains,
    lefts,
    rights,
    range_band,
    azimuth_band,
    columns,
    rows_there,
    rows_back,
    coherence,
    filtered,
):
    matching = pl.program_id(0)
    group, strip = lax.axis_index("acq"), lax.axis_index("rng")
    has_left, has_right = strip > 0, strip < lax.axis_size("rng") - 1
    height, breadth = mains.shape[3], mains.shape[4]
    wide = breadth + LANES
    upper = (group > jnp.bitwise_xor(group, matching + 1)).astype(jnp.int32)
    lines = pl.ds(pl.multiple_of(upper * height, height), height)
    lane = lax.broadcasted_iota(jnp.int32, (height, LANES), 1)
    at_right = jnp.logical_and(lane < REACH, has_right)
    at_left = jnp.logical_and(lane >= LANES - REACH, has_left)

    def widened(main, left, right, place):
        right = pltpu.roll(right, lax.rem(LANES - REACH * place, LANES), 1)
        left = pltpu.roll(left, lax.rem(2 * LANES - REACH - REACH * place, LANES), 1)
        rim = jnp.where(at_right, right, jnp.where(at_left, left, 0.0))
        return jnp.concatenate([main.astype(F32), rim], 1)

    my_left, my_right = own_left[lines, :].astype(F32), own_right[lines, :].astype(F32)
    their_left, their_right = lefts[0].astype(F32), rights[0].astype(F32)

    fields = []
    for member in range(2):
        partner = lax.rem(pairing[matching, 2 * group + member], 2)
        mine = [
            widened(images[part, member, lines, :], my_left, my_right, 2 * part + member)
            for part in range(2)
        ]
        theirs = [
            widened(mains[0, part, partner], their_left, their_right, 2 * part + partner)
            for part in range(2)
        ]
        fields.append(
            [
                mine[0] * theirs[0] + mine[1] * theirs[1],
                mine[1] * theirs[0] - mine[0] * theirs[1],
                mine[0] * mine[0] + mine[1] * mine[1],
                theirs[0] * theirs[0] + theirs[1] * theirs[1],
            ]
        )

    smoothed = times_table(
        jnp.concatenate(fields[0] + fields[1], 0), range_band[0], range_band[1]
    )
    for member in range(2):
        real, imag, mine, theirs = [
            table_times(
                azimuth_band[0],
                azimuth_band[1],
                smoothed[(4 * member + f) * height : (4 * member + f + 1) * height],
            )
            for f in range(4)
        ]
        coherence[0, member] = (real * real + imag * imag) / (mine * theirs + EPSILON)

    groups = breadth // LANES
    blocks = 2 * groups + 1
    count = height // PATCH + 1
    shift = REACH - offsets[matching, 1]
    windows = [
        [pltpu.roll(fields[member][part], shift, 1) for part in range(2)] for member in range(2)
    ]
    cells = []
    for member in range(2):
        for block in range(groups):
            cells.append(
                jnp.concatenate(
                    [w[:, block * LANES : (block + 1) * LANES] for w in windows[member]], 1
                )
            )
    cells.append(
        jnp.concatenate(
            [
                jnp.where(
                    lane < PATCH,
                    windows[0][part][:, breadth:],
                    pltpu.roll(windows[1][part][:, breadth:], PATCH, 1),
                )
                for part in range(2)
            ],
            1,
        )
    )
    rowwise = times_table(jnp.concatenate(cells, 0), columns[0], columns[1])

    def upright(value):
        return jnp.concatenate(
            [
                jnp.concatenate(
                    [
                        value[b * height : (b + 1) * height, :LANES],
                        value[b * height : (b + 1) * height, LANES:],
                    ],
                    0,
                )
                for b in range(blocks)
            ],
            1,
        )

    def flat(value):
        return jnp.concatenate(
            [
                jnp.concatenate(
                    [
                        value[:height, b * LANES : (b + 1) * LANES],
                        value[height:, b * LANES : (b + 1) * LANES],
                    ],
                    1,
                )
                for b in range(blocks)
            ],
            0,
        )

    deep = 2 * height
    frequency = table_times(
        rows_there[0, :, :deep], rows_there[0, :, deep:], upright(rowwise)
    )
    high = count * PATCH
    real, imag = frequency[:high], frequency[high:]
    magnitude = lax.rsqrt(lax.rsqrt(real * real + imag * imag + EPSILON))
    sums = [
        jnp.sum(magnitude[j * PATCH : (j + 1) * PATCH], axis=0, keepdims=True)
        for j in range(count)
    ]
    sums = jnp.concatenate(
        [s[:, b * LANES : (b + 1) * LANES] for b in range(blocks) for s in sums]
        + [jnp.zeros((-blocks * count % 8, LANES), F32)] * (blocks * count % 8 != 0),
        0,
    )
    first = lax.broadcasted_iota(jnp.int32, (LANES, LANES), 0) // PATCH
    second = lax.broadcasted_iota(jnp.int32, (LANES, LANES), 1) // PATCH
    ones = (first == second).astype(F32).astype(BF16)
    sums_high, sums_low = split(sums)
    total = jnp.dot(
        jnp.concatenate([sums_high, sums_low], 1),
        jnp.concatenate([ones, ones], 0),
        preferred_element_type=F32,
    )
    inverse = 1.0 / (total * (1.0 / (PATCH * PATCH)) + EPSILON)
    scaling = jnp.concatenate(
        [
            jnp.concatenate(
                [
                    magnitude[j * PATCH : (j + 1) * PATCH, b * LANES : (b + 1) * LANES]
                    * inverse[b * count + j : b * count + j + 1]
                    for j in range(count)
                ],
                0,
            )
            for b in range(blocks)
        ],
        1,
    )
    weighted = jnp.concatenate([real * scaling, imag * scaling], 0)
    deep = 2 * high
    back = table_times(rows_back[0, :, :deep], rows_back[0, :, deep:], weighted)
    final = times_table(flat(back), columns[2], columns[3])
    rim = final[2 * groups * height :]
    for member in range(2):
        for part in range(2):
            pieces = [
                final[b * height : (b + 1) * height, part * LANES : (part + 1) * LANES]
                for b in range(member * groups, (member + 1) * groups)
            ]
            last = rim[:, part * LANES : (part + 1) * LANES]
            if member:
                last = pltpu.roll(last, LANES - PATCH, 1)
            whole = pltpu.roll(jnp.concatenate(pieces + [last], 1), wide - shift, 1)
            filtered[part, 0, member] = whole[:, :breadth].astype(BF16)


def per_device(images, pairing, tile_offsets):
    height, breadth = images.shape[2] // 2, images.shape[3]
    mains, lefts, rights, own_left, own_right = exchange(images)
    range_band = jnp.asarray(range_table(breadth))
    azimuth_band = jnp.asarray(azimuth_table(height))
    columns = jnp.asarray(column_tables())
    rows_there, rows_back = (jnp.asarray(t) for t in row_tables(height))

    def whole(array):
        return pl.BlockSpec(array.shape, lambda m, pairs, offs: (0,) * array.ndim)

    def matched(array):
        rest = array.shape[1:]
        return pl.BlockSpec((1,) + rest, lambda m, pairs, offs: (m,) + (0,) * len(rest))

    def placed(array):
        rest = array.shape[1:]
        return pl.BlockSpec((1,) + rest, lambda m, pairs, offs: (offs[m, 0], 0, 0))

    return pl.pallas_call(
        pair_kernel,
        grid_spec=pltpu.PrefetchScalarGridSpec(
            num_scalar_prefetch=2,
            grid=(MATCH,),
            in_specs=[
                whole(images),
                whole(own_left),
                whole(own_right),
                matched(mains),
                matched(lefts),
                matched(rights),
                whole(range_band),
                whole(azimuth_band),
                whole(columns),
                placed(rows_there),
                placed(rows_back),
            ],
            out_specs=[
                pl.BlockSpec((1, 2, height, breadth), lambda m, pairs, offs: (m, 0, 0, 0)),
                pl.BlockSpec((2, 1, 2, height, breadth), lambda m, pairs, offs: (0, m, 0, 0, 0)),
            ],
        ),
        out_shape=[
            jax.ShapeDtypeStruct((MATCH, 2, height, breadth), F32),
            jax.ShapeDtypeStruct((2, MATCH, 2, height, breadth), BF16),
        ],
        compiler_params=pltpu.CompilerParams(vmem_limit_bytes=48 * 2**20),
        name="pairs",
    )(
        pairing,
        tile_offsets,
        images,
        own_left,
        own_right,
        mains,
        lefts,
        rights,
        range_band,
        azimuth_band,
        columns,
        rows_there,
        rows_back,
    )


def solution(mesh):
    in_specs = (P(None, ("stack", "acq"), None, "rng"), P(), P())
    out_specs = (
        P(None, ("stack", "acq"), None, "rng"),
        P(None, None, ("stack", "acq"), None, "rng"),
    )
    return jax.shard_map(
        per_device, mesh=mesh, in_specs=in_specs, out_specs=out_specs, check_vma=False
    )
```

```python
import functools

import jax
import jax.numpy as jnp
import ml_dtypes
import numpy as np
from jax import lax
from jax.experimental import pallas as pl
from jax.experimental.pallas import tpu as pltpu
from jax.sharding import PartitionSpec as P

MATCH = 3
REACH = 32
PATCH = 32
EPSILON = 1e-06
LANES = 128
MESH = pl.DeviceIdType.MESH
BF16 = jnp.bfloat16
F32 = jnp.float32


def halves(table):
    high = table.astype(ml_dtypes.bfloat16)
    low = (table - high.astype(np.float64)).astype(ml_dtypes.bfloat16)
    return high, low


def gauss(distance):
    weights = np.exp(-(distance.astype(np.float64) ** 2) / (2.0 * (REACH / 8.0) ** 2))
    return np.where(np.abs(distance) <= REACH, weights, 0.0)


def range_table(breadth):
    lane = np.arange(breadth + LANES)
    cell = np.where(lane >= breadth + LANES - REACH, lane - breadth - LANES, lane)
    used = cell < breadth + REACH
    weights = gauss(cell[:, None] - np.arange(breadth)[None, :])
    return np.stack(halves(weights * used[:, None]))


def azimuth_table(height):
    line = np.arange(height)
    return np.stack(halves(gauss(line[:, None] - line[None, :])))


def column_tables():
    counter = np.arange(PATCH)
    angles = 2.0 * np.pi / PATCH * (counter[:, None] * counter[None, :] % PATCH)
    eye = np.eye(LANES // PATCH)
    cosine, sine = np.kron(eye, np.cos(angles)), np.kron(eye, np.sin(angles))
    there = np.block([[cosine, -sine], [sine, cosine]])
    back = np.block([[cosine, sine], [-sine, cosine]])
    return np.stack(halves(there) + halves(back))


def row_tables(height):
    count = height // PATCH + 1
    line = np.arange(height)
    offset = np.arange(PATCH)[:, None, None, None]
    where = line[None, None, None, :] - offset
    inside = (where + PATCH) // PATCH == np.arange(count)[None, :, None, None]
    frequency = np.arange(PATCH)[None, None, :, None]
    angles = 2.0 * np.pi / PATCH * (frequency * where % PATCH)
    shape = (PATCH, count * PATCH, height)
    cosine = (np.cos(angles) * inside).reshape(shape)
    sine = (np.sin(angles) * inside).reshape(shape)
    there = np.concatenate(
        [np.concatenate([cosine, sine], 2), np.concatenate([-sine, cosine], 2)], 1
    )
    back = there.transpose(0, 2, 1) / (PATCH * PATCH)
    return np.concatenate(halves(there), 2), np.concatenate(halves(back), 2)


def exchange_kernel(
    images, mains, lefts, rights, own_left, own_right, heads, tails, send_sem, recv_sem
):
    stack, group, strip = lax.axis_index("stack"), lax.axis_index("acq"), lax.axis_index("rng")
    strips = lax.axis_size("rng")
    height = images.shape[2] // 2
    breadth = images.shape[3]
    near, far = jnp.bitwise_xor(group, 1), jnp.bitwise_xor(group, 2)
    has_left, has_right = strip > 0, strip < strips - 1

    barrier = pltpu.get_barrier_semaphore()

    def greet(g, r):
        pl.semaphore_signal(barrier, inc=1, device_id=(stack, g, r), device_id_type=MESH)

    greet(near, strip)
    greet(far, strip)

    @pl.when(has_left)
    def _():
        for g in (group, near, far):
            greet(g, strip - 1)

    @pl.when(has_right)
    def _():
        for g in (group, near, far):
            greet(g, strip + 1)

    lane = lax.broadcasted_iota(jnp.int32, (2 * height, LANES), 1) // REACH
    head = jnp.zeros((2 * height, LANES), F32)
    tail = jnp.zeros((2 * height, LANES), F32)
    for part in range(2):
        for member in range(2):
            place = 2 * part + member
            first = images[part, member, :, :LANES].astype(F32)
            last = images[part, member, :, breadth - LANES :].astype(F32)
            if place:
                first = pltpu.roll(first, REACH * place, 1)
            if place != 3:
                last = pltpu.roll(last, REACH * (place + 1), 1)
            head = jnp.where(lane == place, first, head)
            tail = jnp.where(lane == place, last, tail)
    heads[...] = head.astype(BF16)
    tails[...] = tail.astype(BF16)

    pl.semaphore_wait(
        barrier, 2 + 3 * has_left.astype(jnp.int32) + 3 * has_right.astype(jnp.int32)
    )

    def copy(source, target, index, g, r):
        return pltpu.make_async_remote_copy(
            src_ref=source,
            dst_ref=target,
            send_sem=send_sem.at[index],
            recv_sem=recv_sem.at[index],
            device_id=(stack, g, r),
            device_id_type=MESH,
        )

    def rows(g):
        return pl.ds(pl.multiple_of((g > group).astype(jnp.int32) * height, height), height)

    main_far = copy(images.at[:, :, rows(far), :], mains.at[1], 0, far, strip)
    main_near = copy(images.at[:, :, rows(near), :], mains.at[0], 1, near, strip)
    main_far.start()
    right_far = copy(heads.at[rows(far), :], rights.at[1], 2, far, strip - 1)
    right_near = copy(heads.at[rows(near), :], rights.at[0], 3, near, strip - 1)
    right_own = copy(heads, own_right, 4, group, strip - 1)
    left_far = copy(tails.at[rows(far), :], lefts.at[1], 5, far, strip + 1)
    left_near = copy(tails.at[rows(near), :], lefts.at[0], 6, near, strip + 1)
    left_own = copy(tails, own_left, 7, group, strip + 1)

    @pl.when(has_left)
    def _():
        right_far.start()
        right_near.start()
        right_own.start()

    @pl.when(has_right)
    def _():
        left_far.start()
        left_near.start()
        left_own.start()

    main_near.start()

    main_on = copy(mains.at[1], mains.at[2], 8, near, strip)
    right_on = copy(rights.at[1], rights.at[2], 9, near, strip)
    left_on = copy(lefts.at[1], lefts.at[2], 10, near, strip)

    @pl.when(has_right)
    def _():
        right_far.wait_recv()
        right_on.start()

    @pl.when(has_left)
    def _():
        left_far.wait_recv()
        left_on.start()

    main_far.wait_recv()
    main_on.start()
    main_near.wait()
    main_far.wait_send()

    @pl.when(has_left)
    def _():
        right_far.wait_send()
        right_near.wait_send()
        right_own.wait_send()
        left_near.wait_recv()
        left_own.wait_recv()
        left_on.wait()

    @pl.when(has_right)
    def _():
        left_far.wait_send()
        left_near.wait_send()
        left_own.wait_send()
        right_near.wait_recv()
        right_own.wait_recv()
        right_on.wait()

    main_on.wait()


def exchange(images):
    height, breadth = images.shape[2] // 2, images.shape[3]
    shapes = (
        (MATCH, 2, 2, height, breadth),
        (MATCH, height, LANES),
        (MATCH, height, LANES),
        (2 * height, LANES),
        (2 * height, LANES),
    )
    return pl.pallas_call(
        exchange_kernel,
        out_shape=[jax.ShapeDtypeStruct(shape, BF16) for shape in shapes],
        in_specs=[pl.BlockSpec(memory_space=pltpu.VMEM)],
        out_specs=[pl.BlockSpec(memory_space=pl.ANY)] * 5,
        scratch_shapes=[
            pltpu.VMEM((2 * height, LANES), BF16),
            pltpu.VMEM((2 * height, LANES), BF16),
            pltpu.SemaphoreType.DMA((11,)),
            pltpu.SemaphoreType.DMA((11,)),
        ],
        compiler_params=pltpu.CompilerParams(collective_id=0, has_side_effects=True, vmem_limit_bytes=63 * 2**20),
        name="exchange",
    )(images)


def split(value):
    high = value.astype(BF16)
    return high, (value - high.astype(F32)).astype(BF16)


def times_table(value, high, low):
    value_high, value_low = split(value)
    return jnp.dot(
        jnp.concatenate([value_high, value_low, value_high], 1),
        jnp.concatenate([high, high, low], 0),
        preferred_element_type=F32,
    )


def table_times(high, low, value):
    value_high, value_low = split(value)
    return jnp.dot(
        jnp.concatenate([high, high, low], 1),
        jnp.concatenate([value_high, value_low, value_high], 0),
        preferred_element_type=F32,
    )


def pair_kernel(
    pairing,
    offsets,
    images,
    own_left,
    own_right,
    mains,
    lefts,
    rights,
    range_band,
    azimuth_band,
    columns,
    rows_there,
    rows_back,
    coherence,
    filtered,
):
    matching = pl.program_id(0)
    group, strip = lax.axis_index("acq"), lax.axis_index("rng")
    has_left, has_right = strip > 0, strip < lax.axis_size("rng") - 1
    height, breadth = mains.shape[3], mains.shape[4]
    wide = breadth + LANES
    upper = (group > jnp.bitwise_xor(group, matching + 1)).astype(jnp.int32)
    lines = pl.ds(pl.multiple_of(upper * height, height), height)
    lane = lax.broadcasted_iota(jnp.int32, (height, LANES), 1)
    at_right = jnp.logical_and(lane < REACH, has_right)
    at_left = jnp.logical_and(lane >= LANES - REACH, has_left)

    def widened(main, left, right, place):
        right = pltpu.roll(right, lax.rem(LANES - REACH * place, LANES), 1)
        left = pltpu.roll(left, lax.rem(2 * LANES - REACH - REACH * place, LANES), 1)
        rim = jnp.where(at_right, right, jnp.where(at_left, left, 0.0))
        return jnp.concatenate([main.astype(F32), rim], 1)

    my_left, my_right = own_left[lines, :].astype(F32), own_right[lines, :].astype(F32)
    their_left, their_right = lefts[0].astype(F32), rights[0].astype(F32)

    fields = []
    for member in range(2):
        partner = lax.rem(pairing[matching, 2 * group + member], 2)
        mine = [
            widened(images[part, member, lines, :], my_left, my_right, 2 * part + member)
            for part in range(2)
        ]
        theirs = [
            widened(mains[0, part, partner], their_left, their_right, 2 * part + partner)
            for part in range(2)
        ]
        fields.append(
            [
                mine[0] * theirs[0] + mine[1] * theirs[1],
                mine[1] * theirs[0] - mine[0] * theirs[1],
                mine[0] * mine[0] + mine[1] * mine[1],
                theirs[0] * theirs[0] + theirs[1] * theirs[1],
            ]
        )

    smoothed = times_table(
        jnp.concatenate(fields[0] + fields[1], 0), range_band[0], range_band[1]
    )
    for member in range(2):
        real, imag, mine, theirs = [
            table_times(
                azimuth_band[0],
                azimuth_band[1],
                smoothed[(4 * member + f) * height : (4 * member + f + 1) * height],
            )
            for f in range(4)
        ]
        coherence[0, member] = (real * real + imag * imag) / (mine * theirs + EPSILON)

    groups = breadth // LANES
    blocks = 2 * groups + 1
    count = height // PATCH + 1
    shift = REACH - offsets[1, matching]
    windows = [
        [pltpu.roll(fields[member][part], shift, 1) for part in range(2)] for member in range(2)
    ]
    cells = []
    for member in range(2):
        for block in range(groups):
            cells.append(
                jnp.concatenate(
                    [w[:, block * LANES : (block + 1) * LANES] for w in windows[member]], 1
                )
            )
    cells.append(
        jnp.concatenate(
            [
                jnp.where(
                    lane < PATCH,
                    windows[0][part][:, breadth:],
                    pltpu.roll(windows[1][part][:, breadth:], PATCH, 1),
                )
                for part in range(2)
            ],
            1,
        )
    )
    rowwise = times_table(jnp.concatenate(cells, 0), columns[0], columns[1])

    def upright(value):
        return jnp.concatenate(
            [
                jnp.concatenate(
                    [
                        value[b * height : (b + 1) * height, :LANES],
                        value[b * height : (b + 1) * height, LANES:],
                    ],
                    0,
                )
                for b in range(blocks)
            ],
            1,
        )

    def flat(value):
        return jnp.concatenate(
            [
                jnp.concatenate(
                    [
                        value[:height, b * LANES : (b + 1) * LANES],
                        value[height:, b * LANES : (b + 1) * LANES],
                    ],
                    1,
                )
                for b in range(blocks)
            ],
            0,
        )

    deep = 2 * height
    frequency = table_times(
        rows_there[0, :, :deep], rows_there[0, :, deep:], upright(rowwise)
    )
    high = count * PATCH
    real, imag = frequency[:high], frequency[high:]
    magnitude = lax.rsqrt(lax.rsqrt(real * real + imag * imag + EPSILON))
    sums = [
        jnp.sum(magnitude[j * PATCH : (j + 1) * PATCH], axis=0, keepdims=True)
        for j in range(count)
    ]
    sums = jnp.concatenate(
        [s[:, b * LANES : (b + 1) * LANES] for b in range(blocks) for s in sums]
        + [jnp.zeros((-blocks * count % 8, LANES), F32)] * (blocks * count % 8 != 0),
        0,
    )
    first = lax.broadcasted_iota(jnp.int32, (LANES, LANES), 0) // PATCH
    second = lax.broadcasted_iota(jnp.int32, (LANES, LANES), 1) // PATCH
    ones = (first == second).astype(F32).astype(BF16)
    sums_high, sums_low = split(sums)
    total = jnp.dot(
        jnp.concatenate([sums_high, sums_low], 1),
        jnp.concatenate([ones, ones], 0),
        preferred_element_type=F32,
    )
    inverse = 1.0 / (total * (1.0 / (PATCH * PATCH)) + EPSILON)
    scaling = jnp.concatenate(
        [
            jnp.concatenate(
                [
                    magnitude[j * PATCH : (j + 1) * PATCH, b * LANES : (b + 1) * LANES]
                    * inverse[b * count + j : b * count + j + 1]
                    for j in range(count)
                ],
                0,
            )
            for b in range(blocks)
        ],
        1,
    )
    weighted = jnp.concatenate([real * scaling, imag * scaling], 0)
    deep = 2 * high
    back = table_times(rows_back[0, :, :deep], rows_back[0, :, deep:], weighted)
    final = times_table(flat(back), columns[2], columns[3])
    rim = final[2 * groups * height :]
    for member in range(2):
        for part in range(2):
            pieces = [
                final[b * height : (b + 1) * height, part * LANES : (part + 1) * LANES]
                for b in range(member * groups, (member + 1) * groups)
            ]
            last = rim[:, part * LANES : (part + 1) * LANES]
            if member:
                last = pltpu.roll(last, LANES - PATCH, 1)
            whole = pltpu.roll(jnp.concatenate(pieces + [last], 1), wide - shift, 1)
            filtered[part, 0, member] = whole[:, :breadth].astype(BF16)


def per_device(images, pairing, tile_offsets):
    height, breadth = images.shape[2] // 2, images.shape[3]
    mains, lefts, rights, own_left, own_right = exchange(images)
    range_band = jnp.asarray(range_table(breadth))
    azimuth_band = jnp.asarray(azimuth_table(height))
    columns = jnp.asarray(column_tables())
    rows_there, rows_back = (jnp.asarray(t) for t in row_tables(height))

    def whole(array):
        return pl.BlockSpec(array.shape, lambda m, pairs, offs: (0,) * array.ndim)

    def matched(array):
        rest = array.shape[1:]
        return pl.BlockSpec((1,) + rest, lambda m, pairs, offs: (m,) + (0,) * len(rest))

    def placed(array):
        rest = array.shape[1:]
        return pl.BlockSpec((1,) + rest, lambda m, pairs, offs: (offs[0, m], 0, 0))

    return pl.pallas_call(
        pair_kernel,
        grid_spec=pltpu.PrefetchScalarGridSpec(
            num_scalar_prefetch=2,
            grid=(MATCH,),
            in_specs=[
                whole(images),
                whole(own_left),
                whole(own_right),
                matched(mains),
                matched(lefts),
                matched(rights),
                whole(range_band),
                whole(azimuth_band),
                whole(columns),
                placed(rows_there),
                placed(rows_back),
            ],
            out_specs=[
                pl.BlockSpec((1, 2, height, breadth), lambda m, pairs, offs: (m, 0, 0, 0)),
                pl.BlockSpec((2, 1, 2, height, breadth), lambda m, pairs, offs: (0, m, 0, 0, 0)),
            ],
        ),
        out_shape=[
            jax.ShapeDtypeStruct((MATCH, 2, height, breadth), F32),
            jax.ShapeDtypeStruct((2, MATCH, 2, height, breadth), BF16),
        ],
        compiler_params=pltpu.CompilerParams(vmem_limit_bytes=63 * 2**20),
        name="pairs",
    )(
        pairing,
        tile_offsets.T,
        images,
        own_left,
        own_right,
        mains,
        lefts,
        rights,
        range_band,
        azimuth_band,
        columns,
        rows_there,
        rows_back,
    )


def solution(mesh):
    in_specs = (P(None, ("stack", "acq"), None, "rng"), P(), P())
    out_specs = (
        P(None, ("stack", "acq"), None, "rng"),
        P(None, None, ("stack", "acq"), None, "rng"),
    )
    return jax.shard_map(
        per_device, mesh=mesh, in_specs=in_specs, out_specs=out_specs, check_vma=False
    )
```

```python
import functools

import jax
import jax.numpy as jnp
import ml_dtypes
import numpy as np
from jax import lax
from jax.experimental import pallas as pl
from jax.experimental.pallas import tpu as pltpu
from jax.sharding import PartitionSpec as P

MATCH = 3
REACH = 32
PATCH = 32
EPSILON = 1e-06
LANES = 128
MESH = pl.DeviceIdType.MESH
BF16 = jnp.bfloat16
F32 = jnp.float32


def halves(table):
    high = table.astype(ml_dtypes.bfloat16)
    low = (table - high.astype(np.float64)).astype(ml_dtypes.bfloat16)
    return high, low


def gauss(distance):
    weights = np.exp(-(distance.astype(np.float64) ** 2) / (2.0 * (REACH / 8.0) ** 2))
    return np.where(np.abs(distance) <= REACH, weights, 0.0)


def range_table(breadth):
    lane = np.arange(breadth + LANES)
    cell = np.where(lane >= breadth + LANES - REACH, lane - breadth - LANES, lane)
    used = cell < breadth + REACH
    weights = gauss(cell[:, None] - np.arange(breadth)[None, :])
    return np.stack(halves(weights * used[:, None]))


def azimuth_table(height):
    line = np.arange(height)
    return np.stack(halves(gauss(line[:, None] - line[None, :])))


def column_tables():
    counter = np.arange(PATCH)
    angles = 2.0 * np.pi / PATCH * (counter[:, None] * counter[None, :] % PATCH)
    eye = np.eye(LANES // PATCH)
    cosine, sine = np.kron(eye, np.cos(angles)), np.kron(eye, np.sin(angles))
    there = np.block([[cosine, -sine], [sine, cosine]])
    back = np.block([[cosine, sine], [-sine, cosine]])
    return np.stack(halves(there) + halves(back))


def row_tables(height):
    line = np.arange(height)[None, :]
    frequency = np.arange(PATCH)[:, None]
    angles = 2.0 * np.pi / PATCH * (frequency * line % PATCH)
    cosine, sine = np.cos(angles), np.sin(angles)
    first = np.concatenate([cosine, sine], 1)
    second = np.concatenate([-sine, cosine], 1)
    there = np.stack([first, second]).astype(np.float32)
    count = height // PATCH + 1
    tiled = np.concatenate([np.tile(first, (count, 1)), np.tile(second, (count, 1))], 0)
    turned = np.concatenate([np.tile(second, (count, 1)), np.tile(-first, (count, 1))], 0)
    back = np.stack([tiled.T, turned.T]).astype(np.float32) / (PATCH * PATCH)
    offset = np.arange(PATCH)[None, :]
    angles = 2.0 * np.pi / PATCH * (frequency * offset % PATCH)
    turn = np.stack([np.cos(angles), np.sin(angles)]).astype(np.float32)
    turn_lanes = np.tile(turn.transpose(0, 2, 1), (1, 1, 2 * count))
    return there, back, turn, turn_lanes


def split(value):
    high = value.astype(BF16)
    return high, (value - high.astype(F32)).astype(BF16)


def times_table(value, high, low):
    value_high, value_low = split(value)
    return jnp.dot(
        jnp.concatenate([value_high, value_low, value_high], 1),
        jnp.concatenate([high, high, low], 0),
        preferred_element_type=F32,
    )


def table_times(high, low, value):
    value_high, value_low = split(value)
    return jnp.dot(
        jnp.concatenate([high, high, low], 1),
        jnp.concatenate([value_high, value_low, value_high], 0),
        preferred_element_type=F32,
    )


def chosen(index, table, axis):
    place = lax.broadcasted_iota(jnp.int32, table.shape, axis)
    return jnp.sum(jnp.where(place == index, table, 0.0), axis=axis, keepdims=True)


def pair_kernel(
    pairing,
    offsets,
    images_far,
    range_band_far,
    columns_far,
    azimuth_band,
    rows_there,
    rows_back,
    turn,
    turn_lanes,
    coherence_far,
    filtered_far,
    images,
    range_band,
    columns,
    mains,
    lefts,
    rights,
    own_left,
    own_right,
    heads,
    tails,
    coherence,
    filtered,
    send_sem,
    recv_sem,
    load_sem,
    store_sem,
):
    stack, group, strip = lax.axis_index("stack"), lax.axis_index("acq"), lax.axis_index("rng")
    strips = lax.axis_size("rng")
    height = images.shape[2] // 2
    breadth = images.shape[3]
    wide = breadth + LANES
    near, far = jnp.bitwise_xor(group, 1), jnp.bitwise_xor(group, 2)
    has_left, has_right = strip > 0, strip < strips - 1

    loads = [
        pltpu.make_async_copy(source, target, load_sem.at[index])
        for index, (source, target) in enumerate(
            ((images_far, images), (range_band_far, range_band), (columns_far, columns))
        )
    ]
    loads[0].start()
    barrier = pltpu.get_barrier_semaphore()

    def greet(g, r):
        pl.semaphore_signal(barrier, inc=1, device_id=(stack, g, r), device_id_type=MESH)

    greet(near, strip)
    greet(far, strip)

    @pl.when(has_left)
    def _():
        for g in (group, near, far):
            greet(g, strip - 1)

    @pl.when(has_right)
    def _():
        for g in (group, near, far):
            greet(g, strip + 1)

    loads[1].start()
    loads[2].start()
    loads[0].wait()
    lane = lax.broadcasted_iota(jnp.int32, (2 * height, LANES), 1) // REACH
    head = jnp.zeros((2 * height, LANES), F32)
    tail = jnp.zeros((2 * height, LANES), F32)
    for part in range(2):
        for member in range(2):
            place = 2 * part + member
            first = images[part, member, :, :LANES].astype(F32)
            last = images[part, member, :, breadth - LANES :].astype(F32)
            if place:
                first = pltpu.roll(first, REACH * place, 1)
            if place != 3:
                last = pltpu.roll(last, REACH * (place + 1), 1)
            head = jnp.where(lane == place, first, head)
            tail = jnp.where(lane == place, last, tail)
    heads[...] = head.astype(BF16)
    tails[...] = tail.astype(BF16)

    pl.semaphore_wait(
        barrier, 2 + 3 * has_left.astype(jnp.int32) + 3 * has_right.astype(jnp.int32)
    )

    def copy(source, target, index, g, r):
        return pltpu.make_async_remote_copy(
            src_ref=source,
            dst_ref=target,
            send_sem=send_sem.at[index],
            recv_sem=recv_sem.at[index],
            device_id=(stack, g, r),
            device_id_type=MESH,
        )

    def rows(g):
        return pl.ds(pl.multiple_of((g > group).astype(jnp.int32) * height, height), height)

    main_far = copy(images.at[:, :, rows(far), :], mains.at[1], 0, far, strip)
    main_near = copy(images.at[:, :, rows(near), :], mains.at[0], 1, near, strip)
    right_far = copy(heads.at[rows(far), :], rights.at[1], 2, far, strip - 1)
    right_near = copy(heads.at[rows(near), :], rights.at[0], 3, near, strip - 1)
    right_own = copy(heads, own_right, 4, group, strip - 1)
    left_far = copy(tails.at[rows(far), :], lefts.at[1], 5, far, strip + 1)
    left_near = copy(tails.at[rows(near), :], lefts.at[0], 6, near, strip + 1)
    left_own = copy(tails, own_left, 7, group, strip + 1)
    main_on = copy(mains.at[1], mains.at[2], 8, near, strip)
    right_on = copy(rights.at[1], rights.at[2], 9, near, strip)
    left_on = copy(lefts.at[1], lefts.at[2], 10, near, strip)

    main_near.start()
    main_far.start()

    @pl.when(has_left)
    def _():
        right_near.start()
        right_own.start()
        right_far.start()

    @pl.when(has_right)
    def _():
        left_near.start()
        left_own.start()
        left_far.start()

    def arrive(main, left, right):
        @pl.when(has_left)
        def _():
            left.wait_recv()

        @pl.when(has_right)
        def _():
            right.wait_recv()

        main.wait_recv()

    def stores(matching):
        return [
            pltpu.make_async_copy(
                coherence.at[matching], coherence_far.at[matching], store_sem.at[0, matching]
            ),
            pltpu.make_async_copy(
                filtered.at[:, matching], filtered_far.at[:, matching], store_sem.at[1, matching]
            ),
        ]

    work = functools.partial(
        pair_work,
        pairing,
        offsets,
        images,
        own_left,
        own_right,
        mains,
        lefts,
        rights,
        range_band,
        azimuth_band,
        columns,
        rows_there,
        rows_back,
        turn,
        turn_lanes,
        coherence,
        filtered,
    )

    def step(matching, carry):
        @pl.when(matching == 0)
        def _():
            @pl.when(has_left)
            def _():
                left_own.wait_recv()

            @pl.when(has_right)
            def _():
                right_own.wait_recv()

            arrive(main_near, left_near, right_near)
            loads[1].wait()
            loads[2].wait()

        @pl.when(matching == 1)
        def _():
            arrive(main_far, left_far, right_far)
            main_on.start()

            @pl.when(has_left)
            def _():
                left_on.start()

            @pl.when(has_right)
            def _():
                right_on.start()

        @pl.when(matching == 2)
        def _():
            arrive(main_on, left_on, right_on)

        work(matching)
        for store in stores(matching):
            store.start()
        return carry

    lax.fori_loop(0, MATCH, step, 0)

    main_near.wait_send()
    main_far.wait_send()
    main_on.wait_send()

    @pl.when(has_left)
    def _():
        right_near.wait_send()
        right_own.wait_send()
        right_far.wait_send()
        left_on.wait_send()

    @pl.when(has_right)
    def _():
        left_near.wait_send()
        left_own.wait_send()
        left_far.wait_send()
        right_on.wait_send()

    for matching in range(MATCH):
        for store in stores(matching):
            store.wait()


def pair_work(
    pairing,
    offsets,
    images,
    own_left,
    own_right,
    mains,
    lefts,
    rights,
    range_band,
    azimuth_band,
    columns,
    rows_there,
    rows_back,
    turn,
    turn_lanes,
    coherence,
    filtered,
    matching,
):
    group, strip = lax.axis_index("acq"), lax.axis_index("rng")
    has_left, has_right = strip > 0, strip < lax.axis_size("rng") - 1
    height, breadth = mains.shape[3], mains.shape[4]
    wide = breadth + LANES
    upper = (group > jnp.bitwise_xor(group, matching + 1)).astype(jnp.int32)
    lines = pl.ds(pl.multiple_of(upper * height, height), height)
    lane = lax.broadcasted_iota(jnp.int32, (height, LANES), 1)
    at_right = jnp.logical_and(lane < REACH, has_right)
    at_left = jnp.logical_and(lane >= LANES - REACH, has_left)

    def widened(main, left, right, place):
        if place:
            right = pltpu.roll(right, LANES - REACH * place, 1)
        if place != 3:
            left = pltpu.roll(left, LANES - REACH - REACH * place, 1)
        rim = jnp.where(at_right, right, jnp.where(at_left, left, 0.0))
        return jnp.concatenate([main.astype(F32), rim], 1)

    my_left, my_right = own_left[lines, :].astype(F32), own_right[lines, :].astype(F32)
    their_left, their_right = lefts[matching].astype(F32), rights[matching].astype(F32)
    crossed = lax.rem(pairing[matching, 2 * group], 2)
    crossed = jnp.broadcast_to(crossed, (height, wide)) == 1
    ours, others = [
        [
            [widened(main(part, member), left, right, 2 * part + member) for part in range(2)]
            for member in range(2)
        ]
        for main, left, right in (
            (lambda part, member: images[part, member, lines, :], my_left, my_right),
            (lambda part, member: mains[matching, part, member], their_left, their_right),
        )
    ]
    fields = []
    for member in range(2):
        mine = ours[member]
        theirs = [
            jnp.where(crossed, others[1 - member][part], others[member][part])
            for part in range(2)
        ]
        fields.append(
            [
                mine[0] * theirs[0] + mine[1] * theirs[1],
                mine[1] * theirs[0] - mine[0] * theirs[1],
                mine[0] * mine[0] + mine[1] * mine[1],
                theirs[0] * theirs[0] + theirs[1] * theirs[1],
            ]
        )

    smoothed = times_table(
        jnp.concatenate(fields[0] + fields[1], 0), range_band[0], range_band[1]
    )
    for member in range(2):
        real, imag, mine, theirs = [
            table_times(
                azimuth_band[0],
                azimuth_band[1],
                smoothed[(4 * member + f) * height : (4 * member + f + 1) * height],
            )
            for f in range(4)
        ]
        coherence[matching, member] = (real * real + imag * imag) / (mine * theirs + EPSILON)

    groups = breadth // LANES
    blocks = 2 * groups + 1
    count = height // PATCH + 1
    shift = REACH - offsets[1, matching]
    windows = [
        [pltpu.roll(fields[member][part], shift, 1) for part in range(2)] for member in range(2)
    ]
    cells = []
    for member in range(2):
        for block in range(groups):
            cells.append(
                jnp.concatenate(
                    [w[:, block * LANES : (block + 1) * LANES] for w in windows[member]], 1
                )
            )
    cells.append(
        jnp.concatenate(
            [
                jnp.where(
                    lane < PATCH,
                    windows[0][part][:, breadth:],
                    pltpu.roll(windows[1][part][:, breadth:], PATCH, 1),
                )
                for part in range(2)
            ],
            1,
        )
    )
    rowwise = times_table(jnp.concatenate(cells, 0), columns[0], columns[1])

    def upright(value):
        return jnp.concatenate(
            [
                jnp.concatenate(
                    [
                        value[b * height : (b + 1) * height, :LANES],
                        value[b * height : (b + 1) * height, LANES:],
                    ],
                    0,
                )
                for b in range(blocks)
            ],
            1,
        )

    def flat(value):
        return jnp.concatenate(
            [
                jnp.concatenate(
                    [
                        value[:height, b * LANES : (b + 1) * LANES],
                        value[height:, b * LANES : (b + 1) * LANES],
                    ],
                    1,
                )
                for b in range(blocks)
            ],
            0,
        )

    high = count * PATCH
    line_offset = offsets[0, matching]
    cosine, sine = [chosen(line_offset, turn[k], 1) for k in range(2)]
    upper_rows = rows_there[0] * cosine - rows_there[1] * sine
    lower_rows = rows_there[1] * cosine + rows_there[0] * sine
    line = lax.rem(lax.broadcasted_iota(jnp.int32, upper_rows.shape, 1), height)
    patch = (line - line_offset + PATCH) // PATCH
    there = jnp.concatenate(
        [
            jnp.where(patch == j, table, 0.0)
            for table in (upper_rows, lower_rows)
            for j in range(count)
        ],
        0,
    )
    frequency = table_times(*split(there), upright(rowwise))
    real, imag = frequency[:high], frequency[high:]
    magnitude = lax.rsqrt(lax.rsqrt(real * real + imag * imag + EPSILON))
    sums = [
        jnp.sum(magnitude[j * PATCH : (j + 1) * PATCH], axis=0, keepdims=True)
        for j in range(count)
    ]
    sums = jnp.concatenate(
        [s[:, b * LANES : (b + 1) * LANES] for b in range(blocks) for s in sums]
        + [jnp.zeros((-blocks * count % 8, LANES), F32)] * (blocks * count % 8 != 0),
        0,
    )
    first = lax.broadcasted_iota(jnp.int32, (LANES, LANES), 0) // PATCH
    second = lax.broadcasted_iota(jnp.int32, (LANES, LANES), 1) // PATCH
    ones = (first == second).astype(F32).astype(BF16)
    sums_high, sums_low = split(sums)
    total = jnp.dot(
        jnp.concatenate([sums_high, sums_low], 1),
        jnp.concatenate([ones, ones], 0),
        preferred_element_type=F32,
    )
    inverse = 1.0 / (total * (1.0 / (PATCH * PATCH)) + EPSILON)
    scaling = jnp.concatenate(
        [
            jnp.concatenate(
                [
                    magnitude[j * PATCH : (j + 1) * PATCH, b * LANES : (b + 1) * LANES]
                    * inverse[b * count + j : b * count + j + 1]
                    for j in range(count)
                ],
                0,
            )
            for b in range(blocks)
        ],
        1,
    )
    weighted = jnp.concatenate([real * scaling, imag * scaling], 0)
    cosine, sine = [chosen(line_offset, turn_lanes[k], 0) for k in range(2)]
    back_rows = rows_back[0] * cosine - rows_back[1] * sine
    line = lax.rem(lax.broadcasted_iota(jnp.int32, back_rows.shape, 0), height)
    patch = (line - line_offset + PATCH) // PATCH
    place = lax.rem(lax.broadcasted_iota(jnp.int32, back_rows.shape, 1), high) // PATCH
    back_rows = jnp.where(patch == place, back_rows, 0.0)
    back = table_times(*split(back_rows), weighted)
    final = times_table(flat(back), columns[2], columns[3])
    rim = final[2 * groups * height :]
    for member in range(2):
        for part in range(2):
            pieces = [
                final[b * height : (b + 1) * height, part * LANES : (part + 1) * LANES]
                for b in range(member * groups, (member + 1) * groups)
            ]
            last = rim[:, part * LANES : (part + 1) * LANES]
            if member:
                last = pltpu.roll(last, LANES - PATCH, 1)
            whole = pltpu.roll(jnp.concatenate(pieces + [last], 1), wide - shift, 1)
            filtered[part, matching, member] = whole[:, :breadth].astype(BF16)


def per_device(images, pairing, tile_offsets):
    height, breadth = images.shape[2] // 2, images.shape[3]
    tables = [range_table(breadth), column_tables(), azimuth_table(height)]
    tables += row_tables(height)
    vmem, smem = pl.BlockSpec(memory_space=pltpu.VMEM), pl.BlockSpec(memory_space=pltpu.SMEM)
    anywhere = pl.BlockSpec(memory_space=pl.ANY)
    results = [
        jax.ShapeDtypeStruct((MATCH, 2, height, breadth), F32),
        jax.ShapeDtypeStruct((2, MATCH, 2, height, breadth), BF16),
    ]
    return pl.pallas_call(
        pair_kernel,
        in_specs=[smem] * 2 + [anywhere] * 3 + [vmem] * 5,
        out_specs=[anywhere] * 2,
        out_shape=results,
        scratch_shapes=[
            pltpu.VMEM(images.shape, BF16),
            pltpu.VMEM(tables[0].shape, BF16),
            pltpu.VMEM(tables[1].shape, BF16),
            pltpu.VMEM((MATCH, 2, 2, height, breadth), BF16),
            pltpu.VMEM((MATCH, height, LANES), BF16),
            pltpu.VMEM((MATCH, height, LANES), BF16),
            pltpu.VMEM((2 * height, LANES), BF16),
            pltpu.VMEM((2 * height, LANES), BF16),
            pltpu.VMEM((2 * height, LANES), BF16),
            pltpu.VMEM((2 * height, LANES), BF16),
            pltpu.VMEM(results[0].shape, F32),
            pltpu.VMEM(results[1].shape, BF16),
            pltpu.SemaphoreType.DMA((11,)),
            pltpu.SemaphoreType.DMA((11,)),
            pltpu.SemaphoreType.DMA((3,)),
            pltpu.SemaphoreType.DMA((2, MATCH)),
        ],
        compiler_params=pltpu.CompilerParams(
            collective_id=0, has_side_effects=True, vmem_limit_bytes=63 * 2**20
        ),
        name="pairs",
    )(pairing, tile_offsets.T, images, *[jnp.asarray(table) for table in tables])


def solution(mesh):
    in_specs = (P(None, ("stack", "acq"), None, "rng"), P(), P())
    out_specs = (
        P(None, ("stack", "acq"), None, "rng"),
        P(None, None, ("stack", "acq"), None, "rng"),
    )
    return jax.shard_map(
        per_device, mesh=mesh, in_specs=in_specs, out_specs=out_specs, check_vma=False
    )
```

```python
import functools

import jax
import jax.numpy as jnp
import ml_dtypes
import numpy as np
from jax import lax
from jax.experimental import pallas as pl
from jax.experimental.pallas import tpu as pltpu
from jax.sharding import PartitionSpec as P

MATCH = 3
REACH = 32
PATCH = 32
EPSILON = 1e-06
LANES = 128
MESH = pl.DeviceIdType.MESH
BF16 = jnp.bfloat16
F32 = jnp.float32


def halves(table):
    high = table.astype(ml_dtypes.bfloat16)
    low = (table - high.astype(np.float64)).astype(ml_dtypes.bfloat16)
    return high, low


def gauss(distance):
    weights = np.exp(-(distance.astype(np.float64) ** 2) / (2.0 * (REACH / 8.0) ** 2))
    return np.where(np.abs(distance) <= REACH, weights, 0.0)


def range_table(breadth):
    lane = np.arange(breadth + LANES)
    cell = np.where(lane >= breadth + LANES - REACH, lane - breadth - LANES, lane)
    used = cell < breadth + REACH
    weights = gauss(cell[:, None] - np.arange(breadth)[None, :])
    return np.stack(halves(weights * used[:, None]))


def azimuth_table(height):
    line = np.arange(height)
    return np.stack(halves(gauss(line[:, None] - line[None, :])))


def column_tables():
    counter = np.arange(PATCH)
    angles = 2.0 * np.pi / PATCH * (counter[:, None] * counter[None, :] % PATCH)
    eye = np.eye(LANES // PATCH)
    cosine, sine = np.kron(eye, np.cos(angles)), np.kron(eye, np.sin(angles))
    there = np.block([[cosine, -sine], [sine, cosine]])
    back = np.block([[cosine, sine], [-sine, cosine]])
    return np.stack(halves(there) + halves(back))


def row_tables(height):
    line = np.arange(height)[None, :]
    frequency = np.arange(PATCH)[:, None]
    angles = 2.0 * np.pi / PATCH * (frequency * line % PATCH)
    cosine, sine = np.cos(angles), np.sin(angles)
    first = np.concatenate([cosine, sine], 1)
    second = np.concatenate([-sine, cosine], 1)
    there = np.stack([first, second]).astype(np.float32)
    count = height // PATCH + 1
    tiled = np.concatenate([np.tile(first, (count, 1)), np.tile(second, (count, 1))], 0)
    turned = np.concatenate([np.tile(second, (count, 1)), np.tile(-first, (count, 1))], 0)
    back = np.stack([tiled.T, turned.T]).astype(np.float32) / (PATCH * PATCH)
    offset = np.arange(PATCH)[None, :]
    angles = 2.0 * np.pi / PATCH * (frequency * offset % PATCH)
    turn = np.stack([np.cos(angles), np.sin(angles)]).astype(np.float32)
    turn_lanes = np.tile(turn.transpose(0, 2, 1), (1, 1, 2 * count))
    return there, back, turn, turn_lanes


def split(value):
    high = value.astype(BF16)
    return high, (value - high.astype(F32)).astype(BF16)


def times_table(value, high, low):
    value_high, value_low = split(value)
    return jnp.dot(
        jnp.concatenate([value_high, value_low, value_high], 1),
        jnp.concatenate([high, high, low], 0),
        preferred_element_type=F32,
    )


def table_times(high, low, value):
    value_high, value_low = split(value)
    return jnp.dot(
        jnp.concatenate([high, high, low], 1),
        jnp.concatenate([value_high, value_low, value_high], 0),
        preferred_element_type=F32,
    )


def chosen(index, table, axis):
    place = lax.broadcasted_iota(jnp.int32, table.shape, axis)
    return jnp.sum(jnp.where(place == index, table, 0.0), axis=axis, keepdims=True)


def pair_kernel(
    pairing,
    offsets,
    images_far,
    range_band_far,
    columns_far,
    azimuth_band,
    rows_there,
    rows_back,
    turn,
    turn_lanes,
    coherence,
    filtered,
    images,
    range_band,
    columns,
    mains,
    lefts,
    rights,
    own_left,
    own_right,
    heads,
    tails,
    send_sem,
    recv_sem,
    load_sem,
):
    stack, group, strip = lax.axis_index("stack"), lax.axis_index("acq"), lax.axis_index("rng")
    strips = lax.axis_size("rng")
    height = images.shape[2] // 2
    breadth = images.shape[3]
    wide = breadth + LANES
    near, far = jnp.bitwise_xor(group, 1), jnp.bitwise_xor(group, 2)
    has_left, has_right = strip > 0, strip < strips - 1

    loads = [
        pltpu.make_async_copy(source, target, load_sem.at[index])
        for index, (source, target) in enumerate(
            ((images_far, images), (range_band_far, range_band), (columns_far, columns))
        )
    ]
    loads[0].start()
    barrier = pltpu.get_barrier_semaphore()

    def greet(g, r):
        pl.semaphore_signal(barrier, inc=1, device_id=(stack, g, r), device_id_type=MESH)

    greet(near, strip)
    greet(far, strip)

    @pl.when(has_left)
    def _():
        for g in (group, near, far):
            greet(g, strip - 1)

    @pl.when(has_right)
    def _():
        for g in (group, near, far):
            greet(g, strip + 1)

    loads[1].start()
    loads[2].start()
    loads[0].wait()
    lane = lax.broadcasted_iota(jnp.int32, (2 * height, LANES), 1) // REACH
    head = jnp.zeros((2 * height, LANES), F32)
    tail = jnp.zeros((2 * height, LANES), F32)
    for part in range(2):
        for member in range(2):
            place = 2 * part + member
            first = images[part, member, :, :LANES].astype(F32)
            last = images[part, member, :, breadth - LANES :].astype(F32)
            if place:
                first = pltpu.roll(first, REACH * place, 1)
            if place != 3:
                last = pltpu.roll(last, REACH * (place + 1), 1)
            head = jnp.where(lane == place, first, head)
            tail = jnp.where(lane == place, last, tail)
    heads[...] = head.astype(BF16)
    tails[...] = tail.astype(BF16)

    pl.semaphore_wait(
        barrier, 2 + 3 * has_left.astype(jnp.int32) + 3 * has_right.astype(jnp.int32)
    )

    def copy(source, target, index, g, r):
        return pltpu.make_async_remote_copy(
            src_ref=source,
            dst_ref=target,
            send_sem=send_sem.at[index],
            recv_sem=recv_sem.at[index],
            device_id=(stack, g, r),
            device_id_type=MESH,
        )

    def rows(g):
        return pl.ds(pl.multiple_of((g > group).astype(jnp.int32) * height, height), height)

    main_far = copy(images.at[:, :, rows(far), :], mains.at[1], 0, far, strip)
    main_near = copy(images.at[:, :, rows(near), :], mains.at[0], 1, near, strip)
    right_far = copy(heads.at[rows(far), :], rights.at[1], 2, far, strip - 1)
    right_near = copy(heads.at[rows(near), :], rights.at[0], 3, near, strip - 1)
    right_own = copy(heads, own_right, 4, group, strip - 1)
    left_far = copy(tails.at[rows(far), :], lefts.at[1], 5, far, strip + 1)
    left_near = copy(tails.at[rows(near), :], lefts.at[0], 6, near, strip + 1)
    left_own = copy(tails, own_left, 7, group, strip + 1)
    main_on = copy(mains.at[1], mains.at[2], 8, near, strip)
    right_on = copy(rights.at[1], rights.at[2], 9, near, strip)
    left_on = copy(lefts.at[1], lefts.at[2], 10, near, strip)

    main_near.start()
    main_far.start()

    @pl.when(has_left)
    def _():
        right_near.start()
        right_own.start()
        right_far.start()

    @pl.when(has_right)
    def _():
        left_near.start()
        left_own.start()
        left_far.start()

    def arrive(main, left, right):
        @pl.when(has_left)
        def _():
            left.wait_recv()

        @pl.when(has_right)
        def _():
            right.wait_recv()

        main.wait_recv()

    work = functools.partial(
        pair_work,
        pairing,
        offsets,
        images,
        own_left,
        own_right,
        mains,
        lefts,
        rights,
        range_band,
        azimuth_band,
        columns,
        rows_there,
        rows_back,
        turn,
        turn_lanes,
        coherence,
        filtered,
    )

    def step(matching, carry):
        @pl.when(matching == 0)
        def _():
            @pl.when(has_left)
            def _():
                left_own.wait_recv()

            @pl.when(has_right)
            def _():
                right_own.wait_recv()

            arrive(main_near, left_near, right_near)
            loads[1].wait()
            loads[2].wait()

        @pl.when(matching == 1)
        def _():
            arrive(main_far, left_far, right_far)
            main_on.start()

            @pl.when(has_left)
            def _():
                left_on.start()

            @pl.when(has_right)
            def _():
                right_on.start()

        @pl.when(matching == 2)
        def _():
            arrive(main_on, left_on, right_on)

        work(matching)
        return carry

    lax.fori_loop(0, MATCH, step, 0)

    main_near.wait_send()
    main_far.wait_send()
    main_on.wait_send()

    @pl.when(has_left)
    def _():
        right_near.wait_send()
        right_own.wait_send()
        right_far.wait_send()
        left_on.wait_send()

    @pl.when(has_right)
    def _():
        left_near.wait_send()
        left_own.wait_send()
        left_far.wait_send()
        right_on.wait_send()


def pair_work(
    pairing,
    offsets,
    images,
    own_left,
    own_right,
    mains,
    lefts,
    rights,
    range_band,
    azimuth_band,
    columns,
    rows_there,
    rows_back,
    turn,
    turn_lanes,
    coherence,
    filtered,
    matching,
):
    group, strip = lax.axis_index("acq"), lax.axis_index("rng")
    has_left, has_right = strip > 0, strip < lax.axis_size("rng") - 1
    height, breadth = mains.shape[3], mains.shape[4]
    wide = breadth + LANES
    upper = (group > jnp.bitwise_xor(group, matching + 1)).astype(jnp.int32)
    lines = pl.ds(pl.multiple_of(upper * height, height), height)
    lane = lax.broadcasted_iota(jnp.int32, (height, LANES), 1)
    at_right = jnp.logical_and(lane < REACH, has_right)
    at_left = jnp.logical_and(lane >= LANES - REACH, has_left)

    def widened(main, left, right, place):
        if place:
            right = pltpu.roll(right, LANES - REACH * place, 1)
        if place != 3:
            left = pltpu.roll(left, LANES - REACH - REACH * place, 1)
        rim = jnp.where(at_right, right, jnp.where(at_left, left, 0.0))
        return jnp.concatenate([main.astype(F32), rim], 1)

    my_left, my_right = own_left[lines, :].astype(F32), own_right[lines, :].astype(F32)
    their_left, their_right = lefts[matching].astype(F32), rights[matching].astype(F32)
    crossed = lax.rem(pairing[matching, 2 * group], 2)
    crossed = jnp.broadcast_to(crossed, (height, wide)) == 1
    ours, others = [
        [
            [widened(main(part, member), left, right, 2 * part + member) for part in range(2)]
            for member in range(2)
        ]
        for main, left, right in (
            (lambda part, member: images[part, member, lines, :], my_left, my_right),
            (lambda part, member: mains[matching, part, member], their_left, their_right),
        )
    ]
    fields = []
    for member in range(2):
        mine = ours[member]
        theirs = [
            jnp.where(crossed, others[1 - member][part], others[member][part])
            for part in range(2)
        ]
        fields.append(
            [
                mine[0] * theirs[0] + mine[1] * theirs[1],
                mine[1] * theirs[0] - mine[0] * theirs[1],
                mine[0] * mine[0] + mine[1] * mine[1],
                theirs[0] * theirs[0] + theirs[1] * theirs[1],
            ]
        )

    smoothed = times_table(
        jnp.concatenate(fields[0] + fields[1], 0), range_band[0], range_band[1]
    )
    for member in range(2):
        real, imag, mine, theirs = [
            table_times(
                azimuth_band[0],
                azimuth_band[1],
                smoothed[(4 * member + f) * height : (4 * member + f + 1) * height],
            )
            for f in range(4)
        ]
        coherence[matching, member] = (real * real + imag * imag) / (mine * theirs + EPSILON)

    groups = breadth // LANES
    blocks = 2 * groups + 1
    count = height // PATCH + 1
    shift = REACH - offsets[1, matching]
    windows = [
        [pltpu.roll(fields[member][part], shift, 1) for part in range(2)] for member in range(2)
    ]
    cells = []
    for member in range(2):
        for block in range(groups):
            cells.append(
                jnp.concatenate(
                    [w[:, block * LANES : (block + 1) * LANES] for w in windows[member]], 1
                )
            )
    cells.append(
        jnp.concatenate(
            [
                jnp.where(
                    lane < PATCH,
                    windows[0][part][:, breadth:],
                    pltpu.roll(windows[1][part][:, breadth:], PATCH, 1),
                )
                for part in range(2)
            ],
            1,
        )
    )
    rowwise = times_table(jnp.concatenate(cells, 0), columns[0], columns[1])

    def upright(value):
        return jnp.concatenate(
            [
                jnp.concatenate(
                    [
                        value[b * height : (b + 1) * height, :LANES],
                        value[b * height : (b + 1) * height, LANES:],
                    ],
                    0,
                )
                for b in range(blocks)
            ],
            1,
        )

    def flat(value):
        return jnp.concatenate(
            [
                jnp.concatenate(
                    [
                        value[:height, b * LANES : (b + 1) * LANES],
                        value[height:, b * LANES : (b + 1) * LANES],
                    ],
                    1,
                )
                for b in range(blocks)
            ],
            0,
        )

    high = count * PATCH
    line_offset = offsets[0, matching]
    cosine, sine = [chosen(line_offset, turn[k], 1) for k in range(2)]
    upper_rows = rows_there[0] * cosine - rows_there[1] * sine
    lower_rows = rows_there[1] * cosine + rows_there[0] * sine
    line = lax.rem(lax.broadcasted_iota(jnp.int32, upper_rows.shape, 1), height)
    patch = (line - line_offset + PATCH) // PATCH
    there = jnp.concatenate(
        [
            jnp.where(patch == j, table, 0.0)
            for table in (upper_rows, lower_rows)
            for j in range(count)
        ],
        0,
    )
    frequency = table_times(*split(there), upright(rowwise))
    real, imag = frequency[:high], frequency[high:]
    magnitude = lax.rsqrt(lax.rsqrt(real * real + imag * imag + EPSILON))
    sums = [
        jnp.sum(magnitude[j * PATCH : (j + 1) * PATCH], axis=0, keepdims=True)
        for j in range(count)
    ]
    sums = jnp.concatenate(
        [s[:, b * LANES : (b + 1) * LANES] for b in range(blocks) for s in sums]
        + [jnp.zeros((-blocks * count % 8, LANES), F32)] * (blocks * count % 8 != 0),
        0,
    )
    first = lax.broadcasted_iota(jnp.int32, (LANES, LANES), 0) // PATCH
    second = lax.broadcasted_iota(jnp.int32, (LANES, LANES), 1) // PATCH
    ones = (first == second).astype(F32).astype(BF16)
    sums_high, sums_low = split(sums)
    total = jnp.dot(
        jnp.concatenate([sums_high, sums_low], 1),
        jnp.concatenate([ones, ones], 0),
        preferred_element_type=F32,
    )
    inverse = 1.0 / (total * (1.0 / (PATCH * PATCH)) + EPSILON)
    scaling = jnp.concatenate(
        [
            jnp.concatenate(
                [
                    magnitude[j * PATCH : (j + 1) * PATCH, b * LANES : (b + 1) * LANES]
                    * inverse[b * count + j : b * count + j + 1]
                    for j in range(count)
                ],
                0,
            )
            for b in range(blocks)
        ],
        1,
    )
    weighted = jnp.concatenate([real * scaling, imag * scaling], 0)
    cosine, sine = [chosen(line_offset, turn_lanes[k], 0) for k in range(2)]
    back_rows = rows_back[0] * cosine - rows_back[1] * sine
    line = lax.rem(lax.broadcasted_iota(jnp.int32, back_rows.shape, 0), height)
    patch = (line - line_offset + PATCH) // PATCH
    place = lax.rem(lax.broadcasted_iota(jnp.int32, back_rows.shape, 1), high) // PATCH
    back_rows = jnp.where(patch == place, back_rows, 0.0)
    back = table_times(*split(back_rows), weighted)
    final = times_table(flat(back), columns[2], columns[3])
    rim = final[2 * groups * height :]
    for member in range(2):
        for part in range(2):
            pieces = [
                final[b * height : (b + 1) * height, part * LANES : (part + 1) * LANES]
                for b in range(member * groups, (member + 1) * groups)
            ]
            last = rim[:, part * LANES : (part + 1) * LANES]
            if member:
                last = pltpu.roll(last, LANES - PATCH, 1)
            whole = pltpu.roll(jnp.concatenate(pieces + [last], 1), wide - shift, 1)
            filtered[part, matching, member] = whole[:, :breadth].astype(BF16)


def per_device(images, pairing, tile_offsets):
    height, breadth = images.shape[2] // 2, images.shape[3]
    tables = [range_table(breadth), column_tables(), azimuth_table(height)]
    tables += row_tables(height)
    vmem, smem = pl.BlockSpec(memory_space=pltpu.VMEM), pl.BlockSpec(memory_space=pltpu.SMEM)
    anywhere = pl.BlockSpec(memory_space=pl.ANY)
    results = [
        pltpu.VMEM((MATCH, 2, height, breadth), F32),
        pltpu.VMEM((2, MATCH, 2, height, breadth), BF16),
    ]
    operands = [pairing, tile_offsets.T, images] + [jnp.asarray(table) for table in tables]
    operands = [pltpu.with_memory_space_constraint(array, pltpu.HBM) for array in operands]
    return pl.pallas_call(
        pair_kernel,
        in_specs=[smem] * 2 + [anywhere] * 3 + [vmem] * 5,
        out_specs=[vmem] * 2,
        out_shape=results,
        scratch_shapes=[
            pltpu.VMEM(images.shape, BF16),
            pltpu.VMEM(tables[0].shape, BF16),
            pltpu.VMEM(tables[1].shape, BF16),
            pltpu.VMEM((MATCH, 2, 2, height, breadth), BF16),
            pltpu.VMEM((MATCH, height, LANES), BF16),
            pltpu.VMEM((MATCH, height, LANES), BF16),
            pltpu.VMEM((2 * height, LANES), BF16),
            pltpu.VMEM((2 * height, LANES), BF16),
            pltpu.VMEM((2 * height, LANES), BF16),
            pltpu.VMEM((2 * height, LANES), BF16),
            pltpu.SemaphoreType.DMA((11,)),
            pltpu.SemaphoreType.DMA((11,)),
            pltpu.SemaphoreType.DMA((3,)),
        ],
        compiler_params=pltpu.CompilerParams(
            collective_id=0, has_side_effects=True, vmem_limit_bytes=40 * 2**20
        ),
        name="pairs",
    )(*operands)


def solution(mesh):
    in_specs = (P(None, ("stack", "acq"), None, "rng"), P(), P())
    out_specs = (
        P(None, ("stack", "acq"), None, "rng"),
        P(None, None, ("stack", "acq"), None, "rng"),
    )
    return jax.shard_map(
        per_device, mesh=mesh, in_specs=in_specs, out_specs=out_specs, check_vma=False
    )
```

```python
import functools

import jax
import jax.numpy as jnp
import ml_dtypes
import numpy as np
from jax import lax
from jax.experimental import pallas as pl
from jax.experimental.pallas import tpu as pltpu
from jax.sharding import PartitionSpec as P

MATCH = 3
REACH = 32
PATCH = 32
EPSILON = 1e-06
LANES = 128
MESH = pl.DeviceIdType.MESH
BF16 = jnp.bfloat16
F32 = jnp.float32


def halves(table):
    high = table.astype(ml_dtypes.bfloat16)
    low = (table - high.astype(np.float64)).astype(ml_dtypes.bfloat16)
    return high, low


def gauss(distance):
    weights = np.exp(-(distance.astype(np.float64) ** 2) / (2.0 * (REACH / 8.0) ** 2))
    return np.where(np.abs(distance) <= REACH, weights, 0.0)


def range_table(breadth):
    lane = np.arange(breadth + LANES)
    cell = np.where(lane >= breadth + LANES - REACH, lane - breadth - LANES, lane)
    used = cell < breadth + REACH
    weights = gauss(cell[:, None] - np.arange(breadth)[None, :])
    return np.stack(halves(weights * used[:, None]))


def azimuth_table(height):
    line = np.arange(height)
    return np.stack(halves(gauss(line[:, None] - line[None, :])))


def column_tables():
    counter = np.arange(PATCH)
    angles = 2.0 * np.pi / PATCH * (counter[:, None] * counter[None, :] % PATCH)
    eye = np.eye(LANES // PATCH)
    cosine, sine = np.kron(eye, np.cos(angles)), np.kron(eye, np.sin(angles))
    there = np.block([[cosine, -sine], [sine, cosine]])
    back = np.block([[cosine, sine], [-sine, cosine]])
    return np.stack(halves(there) + halves(back))


def row_tables(height):
    line = np.arange(height)[None, :]
    frequency = np.arange(PATCH)[:, None]
    angles = 2.0 * np.pi / PATCH * (frequency * line % PATCH)
    cosine, sine = np.cos(angles), np.sin(angles)
    first = np.concatenate([cosine, sine], 1)
    second = np.concatenate([-sine, cosine], 1)
    there = np.stack([first, second]).astype(np.float32)
    count = height // PATCH + 1
    tiled = np.concatenate([np.tile(first, (count, 1)), np.tile(second, (count, 1))], 0)
    turned = np.concatenate([np.tile(second, (count, 1)), np.tile(-first, (count, 1))], 0)
    back = np.stack([tiled.T, turned.T]).astype(np.float32) / (PATCH * PATCH)
    offset = np.arange(PATCH)[None, :]
    angles = 2.0 * np.pi / PATCH * (frequency * offset % PATCH)
    turn = np.stack([np.cos(angles), np.sin(angles)]).astype(np.float32)
    turn_lanes = np.tile(turn.transpose(0, 2, 1), (1, 1, 2 * count))
    return there, back, turn, turn_lanes


def split(value):
    high = value.astype(BF16)
    return high, (value - high.astype(F32)).astype(BF16)


def times_table(value, high, low):
    value_high, value_low = split(value)
    return jnp.dot(
        jnp.concatenate([value_high, value_low, value_high], 1),
        jnp.concatenate([high, high, low], 0),
        preferred_element_type=F32,
    )


def table_times(high, low, value):
    count, depth = high.shape
    value_high, value_low = split(value)
    if depth <= LANES:
        lower = jnp.concatenate([low, jnp.zeros_like(low)], 1)
        both = jnp.dot(
            jnp.concatenate([jnp.concatenate([high, high], 1), lower], 0),
            jnp.concatenate([value_high, value_low], 0),
            preferred_element_type=F32,
        )
        return both[:count] + both[count:]
    both = jnp.dot(
        jnp.concatenate([high, low], 0), value_high, preferred_element_type=F32
    )
    rest = jnp.dot(high, value_low, preferred_element_type=F32)
    return both[:count] + both[count:] + rest


def chosen(index, table, axis):
    place = lax.broadcasted_iota(jnp.int32, table.shape, axis)
    return jnp.sum(jnp.where(place == index, table, 0.0), axis=axis, keepdims=True)


def pair_kernel(
    pairing,
    offsets,
    images_far,
    range_band_far,
    columns_far,
    azimuth_band,
    rows_there,
    rows_back,
    turn,
    turn_lanes,
    coherence,
    filtered,
    images,
    range_band,
    columns,
    mains,
    lefts,
    rights,
    own_left,
    own_right,
    heads,
    tails,
    send_sem,
    recv_sem,
    load_sem,
):
    stack, group, strip = lax.axis_index("stack"), lax.axis_index("acq"), lax.axis_index("rng")
    strips = lax.axis_size("rng")
    height = images.shape[2] // 2
    breadth = images.shape[3]
    wide = breadth + LANES
    near, far = jnp.bitwise_xor(group, 1), jnp.bitwise_xor(group, 2)
    has_left, has_right = strip > 0, strip < strips - 1

    loads = [
        pltpu.make_async_copy(source, target, load_sem.at[index])
        for index, (source, target) in enumerate(
            ((images_far, images), (range_band_far, range_band), (columns_far, columns))
        )
    ]
    loads[0].start()
    barrier = pltpu.get_barrier_semaphore()

    def greet(g, r):
        pl.semaphore_signal(barrier, inc=1, device_id=(stack, g, r), device_id_type=MESH)

    greet(near, strip)
    greet(far, strip)

    @pl.when(has_left)
    def _():
        for g in (group, near, far):
            greet(g, strip - 1)

    @pl.when(has_right)
    def _():
        for g in (group, near, far):
            greet(g, strip + 1)

    loads[1].start()
    loads[2].start()
    loads[0].wait()
    lane = lax.broadcasted_iota(jnp.int32, (2 * height, LANES), 1) // REACH
    head = jnp.zeros((2 * height, LANES), F32)
    tail = jnp.zeros((2 * height, LANES), F32)
    for part in range(2):
        for member in range(2):
            place = 2 * part + member
            first = images[part, member, :, :LANES].astype(F32)
            last = images[part, member, :, breadth - LANES :].astype(F32)
            if place:
                first = pltpu.roll(first, REACH * place, 1)
            if place != 3:
                last = pltpu.roll(last, REACH * (place + 1), 1)
            head = jnp.where(lane == place, first, head)
            tail = jnp.where(lane == place, last, tail)
    heads[...] = head.astype(BF16)
    tails[...] = tail.astype(BF16)

    pl.semaphore_wait(
        barrier, 2 + 3 * has_left.astype(jnp.int32) + 3 * has_right.astype(jnp.int32)
    )

    def copy(source, target, index, g, r):
        return pltpu.make_async_remote_copy(
            src_ref=source,
            dst_ref=target,
            send_sem=send_sem.at[index],
            recv_sem=recv_sem.at[index],
            device_id=(stack, g, r),
            device_id_type=MESH,
        )

    def rows(g):
        return pl.ds(pl.multiple_of((g > group).astype(jnp.int32) * height, height), height)

    main_far = copy(images.at[:, :, rows(far), :], mains.at[1], 0, far, strip)
    main_near = copy(images.at[:, :, rows(near), :], mains.at[0], 1, near, strip)
    right_far = copy(heads.at[rows(far), :], rights.at[1], 2, far, strip - 1)
    right_near = copy(heads.at[rows(near), :], rights.at[0], 3, near, strip - 1)
    right_own = copy(heads, own_right, 4, group, strip - 1)
    left_far = copy(tails.at[rows(far), :], lefts.at[1], 5, far, strip + 1)
    left_near = copy(tails.at[rows(near), :], lefts.at[0], 6, near, strip + 1)
    left_own = copy(tails, own_left, 7, group, strip + 1)
    main_on = copy(mains.at[1], mains.at[2], 8, near, strip)
    right_on = copy(rights.at[1], rights.at[2], 9, near, strip)
    left_on = copy(lefts.at[1], lefts.at[2], 10, near, strip)

    main_near.start()
    main_far.start()

    @pl.when(has_left)
    def _():
        right_near.start()
        right_own.start()
        right_far.start()

    @pl.when(has_right)
    def _():
        left_near.start()
        left_own.start()
        left_far.start()

    def arrive(main, left, right):
        @pl.when(has_left)
        def _():
            left.wait_recv()

        @pl.when(has_right)
        def _():
            right.wait_recv()

        main.wait_recv()

    work = functools.partial(
        pair_work,
        pairing,
        offsets,
        images,
        own_left,
        own_right,
        mains,
        lefts,
        rights,
        range_band,
        azimuth_band,
        columns,
        rows_there,
        rows_back,
        turn,
        turn_lanes,
        coherence,
        filtered,
    )

    def step(matching, carry):
        @pl.when(matching == 0)
        def _():
            @pl.when(has_left)
            def _():
                left_own.wait_recv()

            @pl.when(has_right)
            def _():
                right_own.wait_recv()

            arrive(main_near, left_near, right_near)
            loads[1].wait()
            loads[2].wait()

        @pl.when(matching == 1)
        def _():
            arrive(main_far, left_far, right_far)
            main_on.start()

            @pl.when(has_left)
            def _():
                left_on.start()

            @pl.when(has_right)
            def _():
                right_on.start()

        @pl.when(matching == 2)
        def _():
            arrive(main_on, left_on, right_on)

        work(matching)
        return carry

    lax.fori_loop(0, MATCH, step, 0)

    main_near.wait_send()
    main_far.wait_send()
    main_on.wait_send()

    @pl.when(has_left)
    def _():
        right_near.wait_send()
        right_own.wait_send()
        right_far.wait_send()
        left_on.wait_send()

    @pl.when(has_right)
    def _():
        left_near.wait_send()
        left_own.wait_send()
        left_far.wait_send()
        right_on.wait_send()


def pair_work(
    pairing,
    offsets,
    images,
    own_left,
    own_right,
    mains,
    lefts,
    rights,
    range_band,
    azimuth_band,
    columns,
    rows_there,
    rows_back,
    turn,
    turn_lanes,
    coherence,
    filtered,
    matching,
):
    group, strip = lax.axis_index("acq"), lax.axis_index("rng")
    has_left, has_right = strip > 0, strip < lax.axis_size("rng") - 1
    height, breadth = mains.shape[3], mains.shape[4]
    wide = breadth + LANES
    upper = (group > jnp.bitwise_xor(group, matching + 1)).astype(jnp.int32)
    lines = pl.ds(pl.multiple_of(upper * height, height), height)
    lane = lax.broadcasted_iota(jnp.int32, (height, LANES), 1)
    at_right = jnp.logical_and(lane < REACH, has_right)
    at_left = jnp.logical_and(lane >= LANES - REACH, has_left)

    def widened(main, left, right, place):
        if place:
            right = pltpu.roll(right, LANES - REACH * place, 1)
        if place != 3:
            left = pltpu.roll(left, LANES - REACH - REACH * place, 1)
        rim = jnp.where(at_right, right, jnp.where(at_left, left, 0.0))
        return jnp.concatenate([main.astype(F32), rim], 1)

    my_left, my_right = own_left[lines, :].astype(F32), own_right[lines, :].astype(F32)
    their_left, their_right = lefts[matching].astype(F32), rights[matching].astype(F32)
    crossed = lax.rem(pairing[matching, 2 * group], 2)
    crossed = jnp.broadcast_to(crossed, (height, wide)) == 1
    ours, others = [
        [
            [widened(main(part, member), left, right, 2 * part + member) for part in range(2)]
            for member in range(2)
        ]
        for main, left, right in (
            (lambda part, member: images[part, member, lines, :], my_left, my_right),
            (lambda part, member: mains[matching, part, member], their_left, their_right),
        )
    ]
    fields = []
    for member in range(2):
        mine = ours[member]
        theirs = [
            jnp.where(crossed, others[1 - member][part], others[member][part])
            for part in range(2)
        ]
        fields.append(
            [
                mine[0] * theirs[0] + mine[1] * theirs[1],
                mine[1] * theirs[0] - mine[0] * theirs[1],
                mine[0] * mine[0] + mine[1] * mine[1],
                theirs[0] * theirs[0] + theirs[1] * theirs[1],
            ]
        )

    smoothed = times_table(
        jnp.concatenate(fields[0] + fields[1], 0), range_band[0], range_band[1]
    )
    groups = breadth // LANES
    blocks = 2 * groups + 1
    count = height // PATCH + 1
    shift = REACH - offsets[1, matching]
    windows = [
        [pltpu.roll(fields[member][part], shift, 1) for part in range(2)] for member in range(2)
    ]
    cells = []
    for member in range(2):
        for block in range(groups):
            cells.append(
                jnp.concatenate(
                    [w[:, block * LANES : (block + 1) * LANES] for w in windows[member]], 1
                )
            )
    cells.append(
        jnp.concatenate(
            [
                jnp.where(
                    lane < PATCH,
                    windows[0][part][:, breadth:],
                    pltpu.roll(windows[1][part][:, breadth:], PATCH, 1),
                )
                for part in range(2)
            ],
            1,
        )
    )
    rowwise = times_table(jnp.concatenate(cells, 0), columns[0], columns[1])
    spread = [
        table_times(
            azimuth_band[0], azimuth_band[1], smoothed[f * height : (f + 1) * height]
        )
        for f in range(8)
    ]

    def upright(value):
        return jnp.concatenate(
            [
                jnp.concatenate(
                    [
                        value[b * height : (b + 1) * height, :LANES],
                        value[b * height : (b + 1) * height, LANES:],
                    ],
                    0,
                )
                for b in range(blocks)
            ],
            1,
        )

    def flat(value):
        return jnp.concatenate(
            [
                jnp.concatenate(
                    [
                        value[:height, b * LANES : (b + 1) * LANES],
                        value[height:, b * LANES : (b + 1) * LANES],
                    ],
                    1,
                )
                for b in range(blocks)
            ],
            0,
        )

    high = count * PATCH
    line_offset = offsets[0, matching]
    cosine, sine = [chosen(line_offset, turn[k], 1) for k in range(2)]
    upper_rows = rows_there[0] * cosine - rows_there[1] * sine
    lower_rows = rows_there[1] * cosine + rows_there[0] * sine
    line = lax.rem(lax.broadcasted_iota(jnp.int32, upper_rows.shape, 1), height)
    patch = (line - line_offset + PATCH) // PATCH
    there = jnp.concatenate(
        [
            jnp.where(patch == j, table, 0.0)
            for table in (upper_rows, lower_rows)
            for j in range(count)
        ],
        0,
    )
    frequency = table_times(*split(there), upright(rowwise))
    for member in range(2):
        real, imag, mine, theirs = spread[4 * member : 4 * member + 4]
        coherence[matching, member] = (real * real + imag * imag) / (mine * theirs + EPSILON)

    real, imag = frequency[:high], frequency[high:]
    magnitude = lax.rsqrt(lax.rsqrt(real * real + imag * imag + EPSILON))
    sums = [
        jnp.sum(magnitude[j * PATCH : (j + 1) * PATCH], axis=0, keepdims=True)
        for j in range(count)
    ]
    sums = jnp.concatenate(
        [s[:, b * LANES : (b + 1) * LANES] for b in range(blocks) for s in sums]
        + [jnp.zeros((-blocks * count % 8, LANES), F32)] * (blocks * count % 8 != 0),
        0,
    )
    first = lax.broadcasted_iota(jnp.int32, (LANES, LANES), 0) // PATCH
    second = lax.broadcasted_iota(jnp.int32, (LANES, LANES), 1) // PATCH
    ones = (first == second).astype(F32).astype(BF16)
    sums_high, sums_low = split(sums)
    total = jnp.dot(
        jnp.concatenate([sums_high, sums_low], 1),
        jnp.concatenate([ones, ones], 0),
        preferred_element_type=F32,
    )
    inverse = 1.0 / (total * (1.0 / (PATCH * PATCH)) + EPSILON)
    scaling = jnp.concatenate(
        [
            jnp.concatenate(
                [
                    magnitude[j * PATCH : (j + 1) * PATCH, b * LANES : (b + 1) * LANES]
                    * inverse[b * count + j : b * count + j + 1]
                    for j in range(count)
                ],
                0,
            )
            for b in range(blocks)
        ],
        1,
    )
    weighted = jnp.concatenate([real * scaling, imag * scaling], 0)
    cosine, sine = [chosen(line_offset, turn_lanes[k], 0) for k in range(2)]
    back_rows = rows_back[0] * cosine - rows_back[1] * sine
    line = lax.rem(lax.broadcasted_iota(jnp.int32, back_rows.shape, 0), height)
    patch = (line - line_offset + PATCH) // PATCH
    place = lax.rem(lax.broadcasted_iota(jnp.int32, back_rows.shape, 1), high) // PATCH
    back_rows = jnp.where(patch == place, back_rows, 0.0)
    back = table_times(*split(back_rows), weighted)
    final = times_table(flat(back), columns[2], columns[3])
    rim = final[2 * groups * height :]
    for member in range(2):
        for part in range(2):
            pieces = [
                final[b * height : (b + 1) * height, part * LANES : (part + 1) * LANES]
                for b in range(member * groups, (member + 1) * groups)
            ]
            last = rim[:, part * LANES : (part + 1) * LANES]
            if member:
                last = pltpu.roll(last, LANES - PATCH, 1)
            whole = pltpu.roll(jnp.concatenate(pieces + [last], 1), wide - shift, 1)
            filtered[part, matching, member] = whole[:, :breadth].astype(BF16)


def per_device(images, pairing, tile_offsets):
    height, breadth = images.shape[2] // 2, images.shape[3]
    tables = [range_table(breadth), column_tables(), azimuth_table(height)]
    tables += row_tables(height)
    vmem, smem = pl.BlockSpec(memory_space=pltpu.VMEM), pl.BlockSpec(memory_space=pltpu.SMEM)
    anywhere = pl.BlockSpec(memory_space=pl.ANY)
    results = [
        pltpu.VMEM((MATCH, 2, height, breadth), F32),
        pltpu.VMEM((2, MATCH, 2, height, breadth), BF16),
    ]
    operands = [pairing, tile_offsets.T, images] + [jnp.asarray(table) for table in tables]
    operands = [pltpu.with_memory_space_constraint(array, pltpu.HBM) for array in operands]
    return pl.pallas_call(
        pair_kernel,
        in_specs=[smem] * 2 + [anywhere] * 3 + [vmem] * 5,
        out_specs=[vmem] * 2,
        out_shape=results,
        scratch_shapes=[
            pltpu.VMEM(images.shape, BF16),
            pltpu.VMEM(tables[0].shape, BF16),
            pltpu.VMEM(tables[1].shape, BF16),
            pltpu.VMEM((MATCH, 2, 2, height, breadth), BF16),
            pltpu.VMEM((MATCH, height, LANES), BF16),
            pltpu.VMEM((MATCH, height, LANES), BF16),
            pltpu.VMEM((2 * height, LANES), BF16),
            pltpu.VMEM((2 * height, LANES), BF16),
            pltpu.VMEM((2 * height, LANES), BF16),
            pltpu.VMEM((2 * height, LANES), BF16),
            pltpu.SemaphoreType.DMA((11,)),
            pltpu.SemaphoreType.DMA((11,)),
            pltpu.SemaphoreType.DMA((3,)),
        ],
        compiler_params=pltpu.CompilerParams(
            collective_id=0, has_side_effects=True, vmem_limit_bytes=40 * 2**20
        ),
        name="pairs",
    )(*operands)


def solution(mesh):
    in_specs = (P(None, ("stack", "acq"), None, "rng"), P(), P())
    out_specs = (
        P(None, ("stack", "acq"), None, "rng"),
        P(None, None, ("stack", "acq"), None, "rng"),
    )
    return jax.shard_map(
        per_device, mesh=mesh, in_specs=in_specs, out_specs=out_specs, check_vma=False
    )
```

```python
import jax
import jax.numpy as jnp
import ml_dtypes
import numpy as np
from jax import lax
from jax.experimental import pallas as pl
from jax.experimental.pallas import tpu as pltpu
from jax.sharding import PartitionSpec as P

MATCH = 3
REACH = 32
PATCH = 32
EPSILON = 1e-06
LANES = 128
MESH = pl.DeviceIdType.MESH
BF16 = jnp.bfloat16
F32 = jnp.float32


def halves(table):
    high = table.astype(ml_dtypes.bfloat16)
    low = (table - high.astype(np.float64)).astype(ml_dtypes.bfloat16)
    return high, low


def gauss(distance):
    weights = np.exp(-(distance.astype(np.float64) ** 2) / (2.0 * (REACH / 8.0) ** 2))
    return np.where(np.abs(distance) <= REACH, weights, 0.0)


def range_table(breadth):
    lane = np.arange(breadth + LANES)
    cell = np.where(lane >= breadth + LANES - REACH, lane - breadth - LANES, lane)
    used = cell < breadth + REACH
    weights = gauss(cell[:, None] - np.arange(breadth)[None, :])
    return np.stack(halves(weights * used[:, None]))


def azimuth_table(height):
    line = np.arange(height)
    return np.stack(halves(gauss(line[:, None] - line[None, :])))


def column_tables():
    counter = np.arange(PATCH)
    angles = 2.0 * np.pi / PATCH * (counter[:, None] * counter[None, :] % PATCH)
    eye = np.eye(LANES // PATCH)
    cosine, sine = np.kron(eye, np.cos(angles)), np.kron(eye, np.sin(angles))
    there = np.block([[cosine, -sine], [sine, cosine]])
    back = np.block([[cosine, sine], [-sine, cosine]])
    return np.stack(halves(there) + halves(back))


def row_tables(height):
    line = np.arange(height)[None, :]
    frequency = np.arange(PATCH)[:, None]
    angles = 2.0 * np.pi / PATCH * (frequency * line % PATCH)
    cosine, sine = np.cos(angles), np.sin(angles)
    first = np.concatenate([cosine, sine], 1)
    second = np.concatenate([-sine, cosine], 1)
    there = np.stack([first, second]).astype(np.float32)
    count = height // PATCH + 1
    tiled = np.concatenate([np.tile(first, (count, 1)), np.tile(second, (count, 1))], 0)
    turned = np.concatenate([np.tile(second, (count, 1)), np.tile(-first, (count, 1))], 0)
    back = np.stack([tiled.T, turned.T]).astype(np.float32) / (PATCH * PATCH)
    offset = np.arange(PATCH)[None, :]
    angles = 2.0 * np.pi / PATCH * (frequency * offset % PATCH)
    turn = np.stack([np.cos(angles), np.sin(angles)]).astype(np.float32)
    turn_lanes = np.tile(turn.transpose(0, 2, 1), (1, 1, 2 * count))
    return there, back, turn, turn_lanes


def split(value):
    high = value.astype(BF16)
    return high, (value - high.astype(F32)).astype(BF16)


def times_table(value, high, low):
    value_high, value_low = split(value)
    return jnp.dot(
        jnp.concatenate([value_high, value_low, value_high], 1),
        jnp.concatenate([high, high, low], 0),
        preferred_element_type=F32,
    )


def table_times(high, low, value):
    count, depth = high.shape
    value_high, value_low = split(value)
    if depth <= LANES:
        lower = jnp.concatenate([low, jnp.zeros_like(low)], 1)
        both = jnp.dot(
            jnp.concatenate([jnp.concatenate([high, high], 1), lower], 0),
            jnp.concatenate([value_high, value_low], 0),
            preferred_element_type=F32,
        )
        return both[:count] + both[count:]
    both = jnp.dot(
        jnp.concatenate([high, low], 0), value_high, preferred_element_type=F32
    )
    rest = jnp.dot(high, value_low, preferred_element_type=F32)
    return both[:count] + both[count:] + rest


def chosen(index, table, axis):
    place = lax.broadcasted_iota(jnp.int32, table.shape, axis)
    return jnp.sum(jnp.where(place == index, table, 0.0), axis=axis, keepdims=True)


TABLES = ("range_band", "columns", "azimuth_band", "rows_there", "rows_back", "turn", "turn_lanes")


def first_kernel(
    pairing_far,
    offsets_far,
    images_far,
    *refs,
):
    tables_far, refs = refs[: len(TABLES)], refs[len(TABLES) :]
    (coherence, filtered, power, images, own_left, own_right, main_last, left_last, right_last), refs = (
        refs[:9],
        refs[9:],
    )
    tables, refs = refs[: len(TABLES)], refs[len(TABLES) :]
    pairing, offsets, mains, lefts, rights, heads, tails, send_sem, recv_sem, load_sem = refs
    stack, group, strip = lax.axis_index("stack"), lax.axis_index("acq"), lax.axis_index("rng")
    strips = lax.axis_size("rng")
    height = images.shape[2] // 2
    breadth = images.shape[3]
    near, far = jnp.bitwise_xor(group, 1), jnp.bitwise_xor(group, 2)
    has_left, has_right = strip > 0, strip < strips - 1

    pairs = [(images_far, images), (pairing_far, pairing), (offsets_far, offsets)]
    pairs += list(zip(tables_far, tables))
    loads = [
        pltpu.make_async_copy(source, target, load_sem.at[index])
        for index, (source, target) in enumerate(pairs)
    ]
    loads[0].start()
    barrier = pltpu.get_barrier_semaphore()

    def greet(g, r):
        pl.semaphore_signal(barrier, inc=1, device_id=(stack, g, r), device_id_type=MESH)

    greet(near, strip)
    greet(far, strip)

    @pl.when(has_left)
    def _():
        for g in (group, near, far):
            greet(g, strip - 1)

    @pl.when(has_right)
    def _():
        for g in (group, near, far):
            greet(g, strip + 1)

    for load in loads[1:]:
        load.start()
    loads[0].wait()
    lane = lax.broadcasted_iota(jnp.int32, (2 * height, LANES), 1) // REACH
    head = jnp.zeros((2 * height, LANES), F32)
    tail = jnp.zeros((2 * height, LANES), F32)
    for part in range(2):
        for member in range(2):
            place = 2 * part + member
            first = images[part, member, :, :LANES].astype(F32)
            last = images[part, member, :, breadth - LANES :].astype(F32)
            if place:
                first = pltpu.roll(first, REACH * place, 1)
            if place != 3:
                last = pltpu.roll(last, REACH * (place + 1), 1)
            head = jnp.where(lane == place, first, head)
            tail = jnp.where(lane == place, last, tail)
    heads[...] = head.astype(BF16)
    tails[...] = tail.astype(BF16)

    pl.semaphore_wait(
        barrier, 2 + 3 * has_left.astype(jnp.int32) + 3 * has_right.astype(jnp.int32)
    )

    def copy(source, target, index, g, r):
        return pltpu.make_async_remote_copy(
            src_ref=source,
            dst_ref=target,
            send_sem=send_sem.at[index],
            recv_sem=recv_sem.at[index],
            device_id=(stack, g, r),
            device_id_type=MESH,
        )

    def rows(g):
        return pl.ds(pl.multiple_of((g > group).astype(jnp.int32) * height, height), height)

    main_far = copy(images.at[:, :, rows(far), :], mains.at[1], 0, far, strip)
    main_near = copy(images.at[:, :, rows(near), :], mains.at[0], 1, near, strip)
    right_far = copy(heads.at[rows(far), :], rights.at[1], 2, far, strip - 1)
    right_near = copy(heads.at[rows(near), :], rights.at[0], 3, near, strip - 1)
    right_own = copy(heads, own_right, 4, group, strip - 1)
    left_far = copy(tails.at[rows(far), :], lefts.at[1], 5, far, strip + 1)
    left_near = copy(tails.at[rows(near), :], lefts.at[0], 6, near, strip + 1)
    left_own = copy(tails, own_left, 7, group, strip + 1)
    main_on = copy(mains.at[1], main_last, 8, near, strip)
    right_on = copy(rights.at[1], right_last, 9, near, strip)
    left_on = copy(lefts.at[1], left_last, 10, near, strip)

    main_near.start()
    main_far.start()

    @pl.when(has_left)
    def _():
        right_near.start()
        right_own.start()
        right_far.start()

    @pl.when(has_right)
    def _():
        left_near.start()
        left_own.start()
        left_far.start()

    def arrive(main, left, right):
        @pl.when(has_left)
        def _():
            left.wait_recv()

        @pl.when(has_right)
        def _():
            right.wait_recv()

        main.wait_recv()

    def step(matching, carry):
        @pl.when(matching == 0)
        def _():
            @pl.when(has_left)
            def _():
                left_own.wait_recv()

            @pl.when(has_right)
            def _():
                right_own.wait_recv()

            arrive(main_near, left_near, right_near)
            for load in loads[1:]:
                load.wait()

        @pl.when(matching == 1)
        def _():
            arrive(main_far, left_far, right_far)
            main_on.start()

            @pl.when(has_left)
            def _():
                left_on.start()

            @pl.when(has_right)
            def _():
                right_on.start()

        pair_work(
            pairing,
            offsets,
            images,
            own_left,
            own_right,
            mains.at[matching],
            lefts.at[matching],
            rights.at[matching],
            tables,
            coherence.at[matching],
            filtered.at[:, matching],
            power,
            matching,
            False,
        )
        return carry

    lax.fori_loop(0, MATCH - 1, step, 0)

    arrive(main_on, left_on, right_on)
    main_near.wait_send()
    main_far.wait_send()
    main_on.wait_send()

    @pl.when(has_left)
    def _():
        right_near.wait_send()
        right_own.wait_send()
        right_far.wait_send()
        left_on.wait_send()

    @pl.when(has_right)
    def _():
        left_near.wait_send()
        left_own.wait_send()
        left_far.wait_send()
        right_on.wait_send()


def last_kernel(
    pairing,
    offsets,
    coherence_first,
    filtered_first,
    power,
    images,
    own_left,
    own_right,
    main_last,
    left_last,
    right_last,
    *refs,
):
    tables, refs = refs[: len(TABLES)], refs[len(TABLES) :]
    coherence_far, filtered_far, coherence, filtered, early_sem, late_sem = refs
    last = MATCH - 1
    early = [
        pltpu.make_async_copy(
            coherence_first.at[m], coherence_far.at[m], early_sem.at[0, m]
        )
        for m in range(last)
    ] + [
        pltpu.make_async_copy(
            filtered_first.at[:, m], filtered_far.at[:, m], early_sem.at[1, m]
        )
        for m in range(last)
    ]
    late = [
        pltpu.make_async_copy(coherence, coherence_far.at[last], late_sem.at[0]),
        pltpu.make_async_copy(filtered, filtered_far.at[:, last], late_sem.at[1]),
    ]
    for store in early:
        store.start()
    pair_work(
        pairing,
        offsets,
        images,
        own_left,
        own_right,
        main_last,
        left_last,
        right_last,
        tables,
        coherence,
        filtered,
        power,
        last,
        True,
        late[0].start,
    )
    late[1].start()
    for store in early + late:
        store.wait()


def pair_work(
    pairing,
    offsets,
    images,
    own_left,
    own_right,
    main,
    left,
    right,
    tables,
    coherence,
    filtered,
    power,
    matching,
    known,
    stored=lambda: None,
):
    range_band, columns, azimuth_band, rows_there, rows_back, turn, turn_lanes = tables
    group, strip = lax.axis_index("acq"), lax.axis_index("rng")
    has_left, has_right = strip > 0, strip < lax.axis_size("rng") - 1
    height, breadth = main.shape[2], main.shape[3]
    wide = breadth + LANES
    upper = (group > jnp.bitwise_xor(group, matching + 1)).astype(jnp.int32)
    lines = pl.ds(pl.multiple_of(upper * height, height), height)
    lane = lax.broadcasted_iota(jnp.int32, (height, LANES), 1)
    at_right = jnp.logical_and(lane < REACH, has_right)
    at_left = jnp.logical_and(lane >= LANES - REACH, has_left)

    def widened(main, left, right, place):
        if place:
            right = pltpu.roll(right, LANES - REACH * place, 1)
        if place != 3:
            left = pltpu.roll(left, LANES - REACH - REACH * place, 1)
        rim = jnp.where(at_right, right, jnp.where(at_left, left, 0.0))
        return jnp.concatenate([main.astype(F32), rim], 1)

    my_left, my_right = own_left[lines, :].astype(F32), own_right[lines, :].astype(F32)
    their_left, their_right = left[...].astype(F32), right[...].astype(F32)
    crossed = lax.rem(pairing[matching, 2 * group], 2)
    crossed = jnp.broadcast_to(crossed, (height, wide)) == 1
    ours, others = [
        [
            [widened(source(part, member), left, right, 2 * part + member) for part in range(2)]
            for member in range(2)
        ]
        for source, left, right in (
            (lambda part, member: images[part, member, lines, :], my_left, my_right),
            (lambda part, member: main[part, member], their_left, their_right),
        )
    ]
    fields = []
    for member in range(2):
        mine = ours[member]
        theirs = [
            jnp.where(crossed, others[1 - member][part], others[member][part])
            for part in range(2)
        ]
        fields.append(
            [
                mine[0] * theirs[0] + mine[1] * theirs[1],
                mine[1] * theirs[0] - mine[0] * theirs[1],
                theirs[0] * theirs[0] + theirs[1] * theirs[1],
            ]
            + ([] if known else [mine[0] * mine[0] + mine[1] * mine[1]])
        )

    smoothed = times_table(
        jnp.concatenate(fields[0] + fields[1], 0), range_band[0], range_band[1]
    )
    groups = breadth // LANES
    blocks = 2 * groups + 1
    count = height // PATCH + 1
    shift = REACH - offsets[1, matching]
    windows = [
        [pltpu.roll(fields[member][part], shift, 1) for part in range(2)] for member in range(2)
    ]
    cells = []
    for member in range(2):
        for block in range(groups):
            cells.append(
                jnp.concatenate(
                    [w[:, block * LANES : (block + 1) * LANES] for w in windows[member]], 1
                )
            )
    cells.append(
        jnp.concatenate(
            [
                jnp.where(
                    lane < PATCH,
                    windows[0][part][:, breadth:],
                    pltpu.roll(windows[1][part][:, breadth:], PATCH, 1),
                )
                for part in range(2)
            ],
            1,
        )
    )
    rowwise = times_table(jnp.concatenate(cells, 0), columns[0], columns[1])
    spread = [
        table_times(
            azimuth_band[0], azimuth_band[1], smoothed[f * height : (f + 1) * height]
        )
        for f in range(2 * len(fields[0]))
    ]

    def upright(value):
        return jnp.concatenate(
            [
                jnp.concatenate(
                    [
                        value[b * height : (b + 1) * height, :LANES],
                        value[b * height : (b + 1) * height, LANES:],
                    ],
                    0,
                )
                for b in range(blocks)
            ],
            1,
        )

    def flat(value):
        return jnp.concatenate(
            [
                jnp.concatenate(
                    [
                        value[:height, b * LANES : (b + 1) * LANES],
                        value[height:, b * LANES : (b + 1) * LANES],
                    ],
                    1,
                )
                for b in range(blocks)
            ],
            0,
        )

    high = count * PATCH
    line_offset = offsets[0, matching]
    cosine, sine = [chosen(line_offset, turn[k], 1) for k in range(2)]
    upper_rows = rows_there[0] * cosine - rows_there[1] * sine
    lower_rows = rows_there[1] * cosine + rows_there[0] * sine
    line = lax.rem(lax.broadcasted_iota(jnp.int32, upper_rows.shape, 1), height)
    patch = (line - line_offset + PATCH) // PATCH
    there = jnp.concatenate(
        [
            jnp.where(patch == j, table, 0.0)
            for table in (upper_rows, lower_rows)
            for j in range(count)
        ],
        0,
    )
    frequency = table_times(*split(there), upright(rowwise))
    for member in range(2):
        count_fields = len(fields[0])
        real, imag, theirs = spread[count_fields * member : count_fields * member + 3]
        mine = power[member] if known else spread[count_fields * member + 3]
        if not known:
            power[member] = mine
        coherence[member] = (real * real + imag * imag) / (mine * theirs + EPSILON)
    stored()

    real, imag = frequency[:high], frequency[high:]
    magnitude = lax.rsqrt(lax.rsqrt(real * real + imag * imag + EPSILON))
    sums = [
        jnp.sum(magnitude[j * PATCH : (j + 1) * PATCH], axis=0, keepdims=True)
        for j in range(count)
    ]
    sums = jnp.concatenate(
        [s[:, b * LANES : (b + 1) * LANES] for b in range(blocks) for s in sums]
        + [jnp.zeros((-blocks * count % 8, LANES), F32)] * (blocks * count % 8 != 0),
        0,
    )
    first = lax.broadcasted_iota(jnp.int32, (LANES, LANES), 0) // PATCH
    second = lax.broadcasted_iota(jnp.int32, (LANES, LANES), 1) // PATCH
    ones = (first == second).astype(F32).astype(BF16)
    sums_high, sums_low = split(sums)
    total = jnp.dot(
        jnp.concatenate([sums_high, sums_low], 1),
        jnp.concatenate([ones, ones], 0),
        preferred_element_type=F32,
    )
    inverse = 1.0 / (total * (1.0 / (PATCH * PATCH)) + EPSILON)
    scaling = jnp.concatenate(
        [
            jnp.concatenate(
                [
                    magnitude[j * PATCH : (j + 1) * PATCH, b * LANES : (b + 1) * LANES]
                    * inverse[b * count + j : b * count + j + 1]
                    for j in range(count)
                ],
                0,
            )
            for b in range(blocks)
        ],
        1,
    )
    weighted = jnp.concatenate([real * scaling, imag * scaling], 0)
    cosine, sine = [chosen(line_offset, turn_lanes[k], 0) for k in range(2)]
    back_rows = rows_back[0] * cosine - rows_back[1] * sine
    line = lax.rem(lax.broadcasted_iota(jnp.int32, back_rows.shape, 0), height)
    patch = (line - line_offset + PATCH) // PATCH
    place = lax.rem(lax.broadcasted_iota(jnp.int32, back_rows.shape, 1), high) // PATCH
    back_rows = jnp.where(patch == place, back_rows, 0.0)
    back = table_times(*split(back_rows), weighted)
    final = times_table(flat(back), columns[2], columns[3])
    rim = final[2 * groups * height :]
    for member in range(2):
        for part in range(2):
            pieces = [
                final[b * height : (b + 1) * height, part * LANES : (part + 1) * LANES]
                for b in range(member * groups, (member + 1) * groups)
            ]
            last = rim[:, part * LANES : (part + 1) * LANES]
            if member:
                last = pltpu.roll(last, LANES - PATCH, 1)
            whole = pltpu.roll(jnp.concatenate(pieces + [last], 1), wide - shift, 1)
            filtered[part, member] = whole[:, :breadth].astype(BF16)


def per_device(images, pairing, tile_offsets):
    height, breadth = images.shape[2] // 2, images.shape[3]
    tables = [range_table(breadth), column_tables(), azimuth_table(height)]
    tables += row_tables(height)
    offsets = tile_offsets.T
    vmem, smem = pl.BlockSpec(memory_space=pltpu.VMEM), pl.BlockSpec(memory_space=pltpu.SMEM)
    anywhere = pl.BlockSpec(memory_space=pl.ANY)
    operands = [pairing, offsets, images] + [jnp.asarray(table) for table in tables]
    operands = [pltpu.with_memory_space_constraint(array, pltpu.HBM) for array in operands]
    slab, halo = (2, 2, height, breadth), (height, LANES)
    between = [
        pltpu.VMEM((MATCH - 1, 2, height, breadth), F32),
        pltpu.VMEM((2, MATCH - 1, 2, height, breadth), BF16),
        pltpu.VMEM((2, height, breadth), F32),
        pltpu.VMEM(images.shape, BF16),
        pltpu.VMEM((2 * height, LANES), BF16),
        pltpu.VMEM((2 * height, LANES), BF16),
        pltpu.VMEM(slab, BF16),
        pltpu.VMEM(halo, BF16),
        pltpu.VMEM(halo, BF16),
    ] + [pltpu.VMEM(table.shape, jnp.dtype(table.dtype)) for table in tables]
    held = pl.pallas_call(
        first_kernel,
        in_specs=[anywhere] * len(operands),
        out_specs=[vmem] * len(between),
        out_shape=between,
        scratch_shapes=[
            pltpu.SMEM(pairing.shape, jnp.int32),
            pltpu.SMEM(offsets.shape, jnp.int32),
            pltpu.VMEM((MATCH - 1,) + slab, BF16),
            pltpu.VMEM((MATCH - 1,) + halo, BF16),
            pltpu.VMEM((MATCH - 1,) + halo, BF16),
            pltpu.VMEM((2 * height, LANES), BF16),
            pltpu.VMEM((2 * height, LANES), BF16),
            pltpu.SemaphoreType.DMA((11,)),
            pltpu.SemaphoreType.DMA((11,)),
            pltpu.SemaphoreType.DMA((len(operands),)),
        ],
        compiler_params=pltpu.CompilerParams(
            collective_id=0, has_side_effects=True, vmem_limit_bytes=40 * 2**20
        ),
        name="first",
    )(*operands)
    held = [pltpu.with_memory_space_constraint(array, pltpu.VMEM) for array in held]
    return pl.pallas_call(
        last_kernel,
        in_specs=[smem] * 2 + [vmem] * len(held),
        out_specs=[anywhere] * 2,
        out_shape=[
            jax.ShapeDtypeStruct((MATCH, 2, height, breadth), F32),
            jax.ShapeDtypeStruct((2, MATCH, 2, height, breadth), BF16),
        ],
        scratch_shapes=[
            pltpu.VMEM((2, height, breadth), F32),
            pltpu.VMEM(slab, BF16),
            pltpu.SemaphoreType.DMA((2, MATCH - 1)),
            pltpu.SemaphoreType.DMA((2,)),
        ],
        compiler_params=pltpu.CompilerParams(vmem_limit_bytes=40 * 2**20),
        name="last",
    )(*operands[:2], *held)


def solution(mesh):
    in_specs = (P(None, ("stack", "acq"), None, "rng"), P(), P())
    out_specs = (
        P(None, ("stack", "acq"), None, "rng"),
        P(None, None, ("stack", "acq"), None, "rng"),
    )
    return jax.shard_map(
        per_device, mesh=mesh, in_specs=in_specs, out_specs=out_specs, check_vma=False
    )
```

```python
import jax
import jax.numpy as jnp
import ml_dtypes
import numpy as np
from jax import lax
from jax.experimental import pallas as pl
from jax.experimental.pallas import tpu as pltpu
from jax.sharding import PartitionSpec as P

MATCH = 3
REACH = 32
PATCH = 32
EPSILON = 1e-06
LANES = 128
MESH = pl.DeviceIdType.MESH
BF16 = jnp.bfloat16
F32 = jnp.float32


def halves(table):
    high = table.astype(ml_dtypes.bfloat16)
    low = (table - high.astype(np.float64)).astype(ml_dtypes.bfloat16)
    return high, low


def gauss(distance):
    weights = np.exp(-(distance.astype(np.float64) ** 2) / (2.0 * (REACH / 8.0) ** 2))
    return np.where(np.abs(distance) <= REACH, weights, 0.0)


def range_table(breadth):
    lane = np.arange(breadth + LANES)
    cell = np.where(lane >= breadth + LANES - REACH, lane - breadth - LANES, lane)
    used = cell < breadth + REACH
    weights = gauss(cell[:, None] - np.arange(breadth)[None, :])
    return np.stack(halves(weights * used[:, None]))


def azimuth_table(height):
    line = np.arange(height)
    return np.stack(halves(gauss(line[:, None] - line[None, :])))


def column_tables():
    counter = np.arange(PATCH)
    angles = 2.0 * np.pi / PATCH * (counter[:, None] * counter[None, :] % PATCH)
    eye = np.eye(LANES // PATCH)
    cosine, sine = np.kron(eye, np.cos(angles)), np.kron(eye, np.sin(angles))
    there = np.block([[cosine, -sine], [sine, cosine]])
    back = np.block([[cosine, sine], [-sine, cosine]])
    return np.stack(halves(there) + halves(back))


def row_tables(height):
    line = np.arange(height)[None, :]
    frequency = np.arange(PATCH)[:, None]
    angles = 2.0 * np.pi / PATCH * (frequency * line % PATCH)
    cosine, sine = np.cos(angles), np.sin(angles)
    first = np.concatenate([cosine, sine], 1)
    second = np.concatenate([-sine, cosine], 1)
    there = np.stack([first, second]).astype(np.float32)
    count = height // PATCH + 1
    tiled = np.concatenate([np.tile(first, (count, 1)), np.tile(second, (count, 1))], 0)
    turned = np.concatenate([np.tile(second, (count, 1)), np.tile(-first, (count, 1))], 0)
    back = np.stack([tiled.T, turned.T]).astype(np.float32) / (PATCH * PATCH)
    offset = np.arange(PATCH)[None, :]
    angles = 2.0 * np.pi / PATCH * (frequency * offset % PATCH)
    turn = np.stack([np.cos(angles), np.sin(angles)]).astype(np.float32)
    turn_lanes = np.tile(turn.transpose(0, 2, 1), (1, 1, 2 * count))
    return there, back, turn, turn_lanes


def split(value):
    high = value.astype(BF16)
    return high, (value - high.astype(F32)).astype(BF16)


def times_table(value, high, low):
    value_high, value_low = split(value)
    return jnp.dot(
        jnp.concatenate([value_high, value_low, value_high], 1),
        jnp.concatenate([high, high, low], 0),
        preferred_element_type=F32,
    )


def table_times(high, low, value):
    count, depth = high.shape
    value_high, value_low = split(value)
    if depth <= LANES:
        lower = jnp.concatenate([low, jnp.zeros_like(low)], 1)
        both = jnp.dot(
            jnp.concatenate([jnp.concatenate([high, high], 1), lower], 0),
            jnp.concatenate([value_high, value_low], 0),
            preferred_element_type=F32,
        )
        return both[:count] + both[count:]
    both = jnp.dot(
        jnp.concatenate([high, low], 0), value_high, preferred_element_type=F32
    )
    rest = jnp.dot(high, value_low, preferred_element_type=F32)
    return both[:count] + both[count:] + rest


def chosen(index, table, axis):
    place = lax.broadcasted_iota(jnp.int32, table.shape, axis)
    return jnp.sum(jnp.where(place == index, table, 0.0), axis=axis, keepdims=True)


TABLES = ("range_band", "columns", "azimuth_band", "rows_there", "rows_back", "turn", "turn_lanes")


def first_kernel(
    pairing_far,
    offsets_far,
    images_far,
    *refs,
):
    tables_far, refs = refs[: len(TABLES)], refs[len(TABLES) :]
    (coherence, filtered, power, images, own_left, own_right, main_last, left_last, right_last), refs = (
        refs[:9],
        refs[9:],
    )
    tables, refs = refs[: len(TABLES)], refs[len(TABLES) :]
    pairing, offsets, mains, lefts, rights, heads, tails, send_sem, recv_sem, load_sem = refs
    stack, group, strip = lax.axis_index("stack"), lax.axis_index("acq"), lax.axis_index("rng")
    strips = lax.axis_size("rng")
    height = images.shape[2] // 2
    breadth = images.shape[3]
    near, far = jnp.bitwise_xor(group, 1), jnp.bitwise_xor(group, 2)
    has_left, has_right = strip > 0, strip < strips - 1

    pairs = [(images_far, images), (pairing_far, pairing), (offsets_far, offsets)]
    pairs += list(zip(tables_far, tables))
    loads = [
        pltpu.make_async_copy(source, target, load_sem.at[index])
        for index, (source, target) in enumerate(pairs)
    ]
    loads[0].start()
    barrier = pltpu.get_barrier_semaphore()

    def greet(g, r):
        pl.semaphore_signal(barrier, inc=1, device_id=(stack, g, r), device_id_type=MESH)

    greet(near, strip)
    greet(far, strip)

    @pl.when(has_left)
    def _():
        for g in (group, near, far):
            greet(g, strip - 1)

    @pl.when(has_right)
    def _():
        for g in (group, near, far):
            greet(g, strip + 1)

    for load in loads[1:]:
        load.start()
    loads[0].wait()
    lane = lax.broadcasted_iota(jnp.int32, (2 * height, LANES), 1) // REACH
    head = jnp.zeros((2 * height, LANES), F32)
    tail = jnp.zeros((2 * height, LANES), F32)
    for part in range(2):
        for member in range(2):
            place = 2 * part + member
            first = images[part, member, :, :LANES].astype(F32)
            last = images[part, member, :, breadth - LANES :].astype(F32)
            if place:
                first = pltpu.roll(first, REACH * place, 1)
                last = pltpu.roll(last, REACH * place, 1)
            head = jnp.where(lane == place, first, head)
            tail = jnp.where(lane == (place + 3) % 4, last, tail)
    heads[...] = head.astype(BF16)
    tails[...] = tail.astype(BF16)

    pl.semaphore_wait(
        barrier, 2 + 3 * has_left.astype(jnp.int32) + 3 * has_right.astype(jnp.int32)
    )

    def copy(source, target, index, g, r):
        return pltpu.make_async_remote_copy(
            src_ref=source,
            dst_ref=target,
            send_sem=send_sem.at[index],
            recv_sem=recv_sem.at[index],
            device_id=(stack, g, r),
            device_id_type=MESH,
        )

    def rows(g):
        return pl.ds(pl.multiple_of((g > group).astype(jnp.int32) * height, height), height)

    main_far = copy(images.at[:, :, rows(far), :], mains.at[1], 0, far, strip)
    main_near = copy(images.at[:, :, rows(near), :], mains.at[0], 1, near, strip)
    right_far = copy(heads.at[rows(far), :], rights.at[1], 2, far, strip - 1)
    right_near = copy(heads.at[rows(near), :], rights.at[0], 3, near, strip - 1)
    right_own = copy(heads, own_right, 4, group, strip - 1)
    left_far = copy(tails.at[rows(far), :], lefts.at[1], 5, far, strip + 1)
    left_near = copy(tails.at[rows(near), :], lefts.at[0], 6, near, strip + 1)
    left_own = copy(tails, own_left, 7, group, strip + 1)
    main_on = copy(mains.at[1], main_last, 8, near, strip)
    right_on = copy(rights.at[1], right_last, 9, near, strip)
    left_on = copy(lefts.at[1], left_last, 10, near, strip)

    main_near.start()
    main_far.start()

    @pl.when(has_left)
    def _():
        right_near.start()
        right_own.start()
        right_far.start()

    @pl.when(has_right)
    def _():
        left_near.start()
        left_own.start()
        left_far.start()

    def arrive(main, left, right):
        @pl.when(has_left)
        def _():
            left.wait_recv()

        @pl.when(has_right)
        def _():
            right.wait_recv()

        main.wait_recv()

    def step(matching, carry):
        @pl.when(matching == 0)
        def _():
            @pl.when(has_left)
            def _():
                left_own.wait_recv()

            @pl.when(has_right)
            def _():
                right_own.wait_recv()

            arrive(main_near, left_near, right_near)
            for load in loads[1:]:
                load.wait()

        @pl.when(matching == 1)
        def _():
            arrive(main_far, left_far, right_far)
            main_on.start()

            @pl.when(has_left)
            def _():
                left_on.start()

            @pl.when(has_right)
            def _():
                right_on.start()

        pair_work(
            pairing,
            offsets,
            images,
            own_left,
            own_right,
            mains.at[matching],
            lefts.at[matching],
            rights.at[matching],
            tables,
            coherence.at[matching],
            filtered.at[:, matching],
            power,
            matching,
            False,
        )
        return carry

    lax.fori_loop(0, MATCH - 1, step, 0)

    arrive(main_on, left_on, right_on)
    main_near.wait_send()
    main_far.wait_send()
    main_on.wait_send()

    @pl.when(has_left)
    def _():
        right_near.wait_send()
        right_own.wait_send()
        right_far.wait_send()
        left_on.wait_send()

    @pl.when(has_right)
    def _():
        left_near.wait_send()
        left_own.wait_send()
        left_far.wait_send()
        right_on.wait_send()


def last_kernel(
    pairing,
    offsets,
    coherence_first,
    filtered_first,
    power,
    images,
    own_left,
    own_right,
    main_last,
    left_last,
    right_last,
    *refs,
):
    tables, refs = refs[: len(TABLES)], refs[len(TABLES) :]
    coherence_far, filtered_far, coherence, filtered, early_sem, late_sem = refs
    last = MATCH - 1
    early = [
        pltpu.make_async_copy(
            coherence_first.at[m], coherence_far.at[m], early_sem.at[0, m]
        )
        for m in range(last)
    ] + [
        pltpu.make_async_copy(
            filtered_first.at[:, m], filtered_far.at[:, m], early_sem.at[1, m]
        )
        for m in range(last)
    ]
    late = [
        pltpu.make_async_copy(coherence, coherence_far.at[last], late_sem.at[0]),
        pltpu.make_async_copy(filtered, filtered_far.at[:, last], late_sem.at[1]),
    ]
    for store in early:
        store.start()
    pair_work(
        pairing,
        offsets,
        images,
        own_left,
        own_right,
        main_last,
        left_last,
        right_last,
        tables,
        coherence,
        filtered,
        power,
        last,
        True,
        late[0].start,
    )
    late[1].start()
    for store in early + late:
        store.wait()


def pair_work(
    pairing,
    offsets,
    images,
    own_left,
    own_right,
    main,
    left,
    right,
    tables,
    coherence,
    filtered,
    power,
    matching,
    known,
    stored=lambda: None,
):
    range_band, columns, azimuth_band, rows_there, rows_back, turn, turn_lanes = tables
    group, strip = lax.axis_index("acq"), lax.axis_index("rng")
    has_left, has_right = strip > 0, strip < lax.axis_size("rng") - 1
    height, breadth = main.shape[2], main.shape[3]
    wide = breadth + LANES
    upper = (group > jnp.bitwise_xor(group, matching + 1)).astype(jnp.int32)
    lines = pl.ds(pl.multiple_of(upper * height, height), height)
    lane = lax.broadcasted_iota(jnp.int32, (height, LANES), 1)
    slot = lane // REACH

    def widened(main, left, right, place):
        at_right = jnp.logical_and(slot == place, has_right)
        at_left = jnp.logical_and(slot == (place + 3) % 4, has_left)
        rim = jnp.where(at_right, right, jnp.where(at_left, left, 0.0))
        if place:
            rim = pltpu.roll(rim, LANES - REACH * place, 1)
        return jnp.concatenate([main.astype(F32), rim], 1)

    my_left, my_right = own_left[lines, :].astype(F32), own_right[lines, :].astype(F32)
    their_left, their_right = left[...].astype(F32), right[...].astype(F32)
    crossed = lax.rem(pairing[matching, 2 * group], 2)
    crossed = jnp.broadcast_to(crossed, (height, wide)) == 1
    ours, others = [
        [
            [widened(source(part, member), left, right, 2 * part + member) for part in range(2)]
            for member in range(2)
        ]
        for source, left, right in (
            (lambda part, member: images[part, member, lines, :], my_left, my_right),
            (lambda part, member: main[part, member], their_left, their_right),
        )
    ]
    fields = []
    for member in range(2):
        mine = ours[member]
        theirs = [
            jnp.where(crossed, others[1 - member][part], others[member][part])
            for part in range(2)
        ]
        fields.append(
            [
                mine[0] * theirs[0] + mine[1] * theirs[1],
                mine[1] * theirs[0] - mine[0] * theirs[1],
                theirs[0] * theirs[0] + theirs[1] * theirs[1],
            ]
            + ([] if known else [mine[0] * mine[0] + mine[1] * mine[1]])
        )

    smoothed = times_table(
        jnp.concatenate(fields[0] + fields[1], 0), range_band[0], range_band[1]
    )

    def spread(member):
        count_fields = len(fields[0])
        results = [
            table_times(
                azimuth_band[0],
                azimuth_band[1],
                smoothed[(count_fields * member + f) * height :][:height],
            )
            for f in range(count_fields)
        ]
        if known:
            results.append(power[member])
        else:
            power[member] = results[3]
        return results

    def finish(member, results):
        real, imag, theirs, mine = results
        coherence[member] = (real * real + imag * imag) / (mine * theirs + EPSILON)

    groups = breadth // LANES
    count = height // PATCH + 1
    high = count * PATCH
    line_offset = offsets[0, matching]
    shift = REACH - offsets[1, matching]

    def window(field):
        turned = [
            pltpu.roll(field[:, g * LANES : (g + 1) * LANES], shift, 1)
            for g in range(groups + 1)
        ]
        return [jnp.where(lane < shift, turned[g - 1], turned[g]) for g in range(groups + 1)]

    def unwindow(pieces):
        turned = [pltpu.roll(piece, LANES - shift, 1) for piece in pieces]
        return jnp.concatenate(
            [jnp.where(lane < LANES - shift, turned[g], turned[g + 1]) for g in range(groups)], 1
        )

    windows = [[window(fields[member][part]) for part in range(2)] for member in range(2)]
    cells = [
        jnp.concatenate([windows[member][part][block] for part in range(2)], 1)
        for member in range(2)
        for block in range(groups)
    ]
    cells.append(
        jnp.concatenate(
            [
                jnp.where(
                    lane < PATCH,
                    windows[0][part][groups],
                    pltpu.roll(windows[1][part][groups], PATCH, 1),
                )
                for part in range(2)
            ],
            1,
        )
    )
    rowwise = times_table(jnp.concatenate(cells, 0), columns[0], columns[1])

    cosine, sine = [chosen(line_offset, turn[k], 1) for k in range(2)]
    upper_rows = rows_there[0] * cosine - rows_there[1] * sine
    lower_rows = rows_there[1] * cosine + rows_there[0] * sine
    line = lax.rem(lax.broadcasted_iota(jnp.int32, upper_rows.shape, 1), height)
    patch = (line - line_offset + PATCH) // PATCH
    there = split(
        jnp.concatenate(
            [
                jnp.where(patch == j, table, 0.0)
                for table in (upper_rows, lower_rows)
                for j in range(count)
            ],
            0,
        )
    )
    cosine, sine = [chosen(line_offset, turn_lanes[k], 0) for k in range(2)]
    back_rows = rows_back[0] * cosine - rows_back[1] * sine
    line = lax.rem(lax.broadcasted_iota(jnp.int32, back_rows.shape, 0), height)
    patch = (line - line_offset + PATCH) // PATCH
    place = lax.rem(lax.broadcasted_iota(jnp.int32, back_rows.shape, 1), high) // PATCH
    back_again = split(jnp.where(patch == place, back_rows, 0.0))

    first = lax.broadcasted_iota(jnp.int32, (2 * LANES, LANES), 0) % LANES // PATCH
    second = lax.broadcasted_iota(jnp.int32, (2 * LANES, LANES), 1) // PATCH
    ones = (first == second).astype(F32).astype(BF16)

    def transformed(blocks):
        upright = jnp.concatenate(
            [
                jnp.concatenate(
                    [
                        rowwise[b * height : (b + 1) * height, :LANES],
                        rowwise[b * height : (b + 1) * height, LANES:],
                    ],
                    0,
                )
                for b in blocks
            ],
            1,
        )
        return table_times(*there, upright)

    def reweighted(frequency):
        blocks = frequency.shape[1] // LANES
        real, imag = frequency[:high], frequency[high:]
        magnitude = lax.rsqrt(lax.rsqrt(real * real + imag * imag + EPSILON))
        sums = [
            jnp.sum(magnitude[j * PATCH : (j + 1) * PATCH], axis=0, keepdims=True)
            for j in range(count)
        ]
        sums = [s[:, b * LANES : (b + 1) * LANES] for b in range(blocks) for s in sums]
        if len(sums) % 8:
            sums.append(jnp.zeros((-len(sums) % 8, LANES), F32))
        total = jnp.dot(
            jnp.concatenate(split(jnp.concatenate(sums, 0)), 1),
            ones,
            preferred_element_type=F32,
        )
        inverse = 1.0 / (total * (1.0 / (PATCH * PATCH)) + EPSILON)
        scaling = jnp.concatenate(
            [
                jnp.concatenate(
                    [
                        magnitude[j * PATCH : (j + 1) * PATCH, b * LANES : (b + 1) * LANES]
                        * inverse[b * count + j : b * count + j + 1]
                        for j in range(count)
                    ],
                    0,
                )
                for b in range(blocks)
            ],
            1,
        )
        return jnp.concatenate([real * scaling, imag * scaling], 0)

    def returned(weighted):
        back = table_times(*back_again, weighted)
        return [
            jnp.concatenate(
                [
                    back[:height, b * LANES : (b + 1) * LANES],
                    back[height:, b * LANES : (b + 1) * LANES],
                ],
                1,
            )
            for b in range(weighted.shape[1] // LANES)
        ]

    chains = [range(groups), range(groups, 2 * groups), range(2 * groups, 2 * groups + 1)]
    frequency = [transformed(chains[0]), transformed(chains[1])]
    results = spread(0)
    flat = returned(reweighted(frequency[0]))
    frequency.append(transformed(chains[2]))
    finish(0, results)
    flat += returned(reweighted(frequency[1]))
    results = spread(1)
    flat += returned(reweighted(frequency[2]))
    finish(1, results)
    stored()
    final = times_table(jnp.concatenate(flat, 0), columns[2], columns[3])
    for member in range(2):
        for part in range(2):
            pieces = [
                final[b * height : (b + 1) * height, part * LANES : (part + 1) * LANES]
                for b in [*chains[member], 2 * groups]
            ]
            if member:
                pieces[-1] = pltpu.roll(pieces[-1], LANES - PATCH, 1)
            filtered[part, member] = unwindow(pieces).astype(BF16)


def per_device(images, pairing, tile_offsets):
    height, breadth = images.shape[2] // 2, images.shape[3]
    tables = [range_table(breadth), column_tables(), azimuth_table(height)]
    tables += row_tables(height)
    offsets = tile_offsets.T
    vmem, smem = pl.BlockSpec(memory_space=pltpu.VMEM), pl.BlockSpec(memory_space=pltpu.SMEM)
    anywhere = pl.BlockSpec(memory_space=pl.ANY)
    operands = [pairing, offsets, images] + [jnp.asarray(table) for table in tables]
    operands = [pltpu.with_memory_space_constraint(array, pltpu.HBM) for array in operands]
    slab, halo = (2, 2, height, breadth), (height, LANES)
    between = [
        pltpu.VMEM((MATCH - 1, 2, height, breadth), F32),
        pltpu.VMEM((2, MATCH - 1, 2, height, breadth), BF16),
        pltpu.VMEM((2, height, breadth), F32),
        pltpu.VMEM(images.shape, BF16),
        pltpu.VMEM((2 * height, LANES), BF16),
        pltpu.VMEM((2 * height, LANES), BF16),
        pltpu.VMEM(slab, BF16),
        pltpu.VMEM(halo, BF16),
        pltpu.VMEM(halo, BF16),
    ] + [pltpu.VMEM(table.shape, jnp.dtype(table.dtype)) for table in tables]
    held = pl.pallas_call(
        first_kernel,
        in_specs=[anywhere] * len(operands),
        out_specs=[vmem] * len(between),
        out_shape=between,
        scratch_shapes=[
            pltpu.SMEM(pairing.shape, jnp.int32),
            pltpu.SMEM(offsets.shape, jnp.int32),
            pltpu.VMEM((MATCH - 1,) + slab, BF16),
            pltpu.VMEM((MATCH - 1,) + halo, BF16),
            pltpu.VMEM((MATCH - 1,) + halo, BF16),
            pltpu.VMEM((2 * height, LANES), BF16),
            pltpu.VMEM((2 * height, LANES), BF16),
            pltpu.SemaphoreType.DMA((11,)),
            pltpu.SemaphoreType.DMA((11,)),
            pltpu.SemaphoreType.DMA((len(operands),)),
        ],
        compiler_params=pltpu.CompilerParams(
            collective_id=0, has_side_effects=True, vmem_limit_bytes=40 * 2**20
        ),
        name="first",
    )(*operands)
    held = [pltpu.with_memory_space_constraint(array, pltpu.VMEM) for array in held]
    return pl.pallas_call(
        last_kernel,
        in_specs=[smem] * 2 + [vmem] * len(held),
        out_specs=[anywhere] * 2,
        out_shape=[
            jax.ShapeDtypeStruct((MATCH, 2, height, breadth), F32),
            jax.ShapeDtypeStruct((2, MATCH, 2, height, breadth), BF16),
        ],
        scratch_shapes=[
            pltpu.VMEM((2, height, breadth), F32),
            pltpu.VMEM(slab, BF16),
            pltpu.SemaphoreType.DMA((2, MATCH - 1)),
            pltpu.SemaphoreType.DMA((2,)),
        ],
        compiler_params=pltpu.CompilerParams(vmem_limit_bytes=40 * 2**20),
        name="last",
    )(*operands[:2], *held)


def solution(mesh):
    in_specs = (P(None, ("stack", "acq"), None, "rng"), P(), P())
    out_specs = (
        P(None, ("stack", "acq"), None, "rng"),
        P(None, None, ("stack", "acq"), None, "rng"),
    )
    return jax.shard_map(
        per_device, mesh=mesh, in_specs=in_specs, out_specs=out_specs, check_vma=False
    )
```

```python
import jax
import jax.numpy as jnp
import ml_dtypes
import numpy as np
from jax import lax
from jax.experimental import pallas as pl
from jax.experimental.pallas import tpu as pltpu
from jax.sharding import PartitionSpec as P

MATCH = 3
REACH = 32
PATCH = 32
EPSILON = 1e-06
LANES = 128
MESH = pl.DeviceIdType.MESH
BF16 = jnp.bfloat16
F32 = jnp.float32


def halves(table):
    high = table.astype(ml_dtypes.bfloat16)
    low = (table - high.astype(np.float64)).astype(ml_dtypes.bfloat16)
    return high, low


def gauss(distance):
    weights = np.exp(-(distance.astype(np.float64) ** 2) / (2.0 * (REACH / 8.0) ** 2))
    return np.where(np.abs(distance) <= REACH, weights, 0.0)


def range_table(breadth):
    lane = np.arange(breadth + LANES)
    cell = np.where(lane >= breadth + LANES - REACH, lane - breadth - LANES, lane)
    used = cell < breadth + REACH
    weights = gauss(cell[:, None] - np.arange(breadth)[None, :])
    high, low = halves(weights * used[:, None])
    rim = high[breadth:].astype(np.float64)
    packed = (rim + np.roll(rim, LANES // 2, 0)).astype(ml_dtypes.bfloat16)
    return np.concatenate([high[:breadth], packed, low[breadth:], low[:breadth]], 0)


def azimuth_table(height):
    line = np.arange(height)
    return np.stack(halves(gauss(line[:, None] - line[None, :])))


def column_tables():
    counter = np.arange(PATCH)
    angles = 2.0 * np.pi / PATCH * (counter[:, None] * counter[None, :] % PATCH)
    eye = np.eye(LANES // PATCH)
    cosine, sine = np.kron(eye, np.cos(angles)), np.kron(eye, np.sin(angles))
    there = np.block([[cosine, -sine], [sine, cosine]])
    back = np.block([[cosine, sine], [-sine, cosine]])
    return np.stack(halves(there) + halves(back))


def row_tables(height):
    line = np.arange(height)[None, :]
    frequency = np.arange(PATCH)[:, None]
    angles = 2.0 * np.pi / PATCH * (frequency * line % PATCH)
    cosine, sine = np.cos(angles), np.sin(angles)
    first = np.concatenate([cosine, sine], 1)
    second = np.concatenate([-sine, cosine], 1)
    there = np.stack([first, second]).astype(np.float32)
    count = height // PATCH + 1
    tiled = np.concatenate([np.tile(first, (count, 1)), np.tile(second, (count, 1))], 0)
    turned = np.concatenate([np.tile(second, (count, 1)), np.tile(-first, (count, 1))], 0)
    back = np.stack([tiled.T, turned.T]).astype(np.float32) / (PATCH * PATCH)
    offset = np.arange(PATCH)[None, :]
    angles = 2.0 * np.pi / PATCH * (frequency * offset % PATCH)
    turn = np.stack([np.cos(angles), np.sin(angles)]).astype(np.float32)
    turn_lanes = np.tile(turn.transpose(0, 2, 1), (1, 1, 2 * count))
    return there, back, turn, turn_lanes


def split(value):
    high = value.astype(BF16)
    return high, (value - high.astype(F32)).astype(BF16)


def times_table(value, high, low):
    value_high, value_low = split(value)
    return jnp.dot(
        jnp.concatenate([value_high, value_low, value_high], 1),
        jnp.concatenate([high, high, low], 0),
        preferred_element_type=F32,
    )


def table_times(high, low, value):
    count, depth = high.shape
    value_high, value_low = split(value)
    if depth <= LANES:
        lower = jnp.concatenate([low, jnp.zeros_like(low)], 1)
        both = jnp.dot(
            jnp.concatenate([jnp.concatenate([high, high], 1), lower], 0),
            jnp.concatenate([value_high, value_low], 0),
            preferred_element_type=F32,
        )
        return both[:count] + both[count:]
    both = jnp.dot(
        jnp.concatenate([high, low], 0), value_high, preferred_element_type=F32
    )
    rest = jnp.dot(high, value_low, preferred_element_type=F32)
    return both[:count] + both[count:] + rest


def chosen(index, table, axis):
    place = lax.broadcasted_iota(jnp.int32, table.shape, axis)
    return jnp.sum(jnp.where(place == index, table, 0.0), axis=axis, keepdims=True)


TABLES = ("range_band", "columns", "azimuth_band", "rows_there", "rows_back", "turn", "turn_lanes")


def first_kernel(
    pairing_far,
    offsets_far,
    images_far,
    *refs,
):
    tables_far, refs = refs[: len(TABLES)], refs[len(TABLES) :]
    (coherence, filtered, power, images, own_left, own_right, main_last, left_last, right_last), refs = (
        refs[:9],
        refs[9:],
    )
    tables, refs = refs[: len(TABLES)], refs[len(TABLES) :]
    pairing, offsets, mains, lefts, rights, heads, tails, send_sem, recv_sem, load_sem = refs
    stack, group, strip = lax.axis_index("stack"), lax.axis_index("acq"), lax.axis_index("rng")
    strips = lax.axis_size("rng")
    height = images.shape[2] // 2
    breadth = images.shape[3]
    near, far = jnp.bitwise_xor(group, 1), jnp.bitwise_xor(group, 2)
    has_left, has_right = strip > 0, strip < strips - 1

    pairs = [(images_far, images), (pairing_far, pairing), (offsets_far, offsets)]
    pairs += list(zip(tables_far, tables))
    loads = [
        pltpu.make_async_copy(source, target, load_sem.at[index])
        for index, (source, target) in enumerate(pairs)
    ]
    loads[0].start()
    barrier = pltpu.get_barrier_semaphore()

    def greet(g, r):
        pl.semaphore_signal(barrier, inc=1, device_id=(stack, g, r), device_id_type=MESH)

    greet(near, strip)
    greet(far, strip)

    @pl.when(has_left)
    def _():
        for g in (group, near, far):
            greet(g, strip - 1)

    @pl.when(has_right)
    def _():
        for g in (group, near, far):
            greet(g, strip + 1)

    for load in loads[1:]:
        load.start()
    loads[0].wait()
    lane = lax.broadcasted_iota(jnp.int32, (2 * height, LANES), 1) // REACH
    head = jnp.zeros((2 * height, LANES), F32)
    tail = jnp.zeros((2 * height, LANES), F32)
    for part in range(2):
        for member in range(2):
            place = 2 * part + member
            first = images[part, member, :, :LANES].astype(F32)
            last = images[part, member, :, breadth - LANES :].astype(F32)
            if place:
                first = pltpu.roll(first, REACH * place, 1)
                last = pltpu.roll(last, REACH * place, 1)
            head = jnp.where(lane == place, first, head)
            tail = jnp.where(lane == (place + 3) % 4, last, tail)
    heads[...] = head.astype(BF16)
    tails[...] = tail.astype(BF16)

    pl.semaphore_wait(
        barrier, 2 + 3 * has_left.astype(jnp.int32) + 3 * has_right.astype(jnp.int32)
    )

    def copy(source, target, index, g, r):
        return pltpu.make_async_remote_copy(
            src_ref=source,
            dst_ref=target,
            send_sem=send_sem.at[index],
            recv_sem=recv_sem.at[index],
            device_id=(stack, g, r),
            device_id_type=MESH,
        )

    def rows(g):
        return pl.ds(pl.multiple_of((g > group).astype(jnp.int32) * height, height), height)

    main_far = copy(images.at[:, :, rows(far), :], mains.at[1], 0, far, strip)
    main_near = copy(images.at[:, :, rows(near), :], mains.at[0], 1, near, strip)
    right_far = copy(heads.at[rows(far), :], rights.at[1], 2, far, strip - 1)
    right_near = copy(heads.at[rows(near), :], rights.at[0], 3, near, strip - 1)
    right_own = copy(heads, own_right, 4, group, strip - 1)
    left_far = copy(tails.at[rows(far), :], lefts.at[1], 5, far, strip + 1)
    left_near = copy(tails.at[rows(near), :], lefts.at[0], 6, near, strip + 1)
    left_own = copy(tails, own_left, 7, group, strip + 1)
    main_on = copy(mains.at[1], main_last, 8, near, strip)
    right_on = copy(rights.at[1], right_last, 9, near, strip)
    left_on = copy(lefts.at[1], left_last, 10, near, strip)

    main_near.start()
    main_far.start()

    @pl.when(has_left)
    def _():
        right_near.start()
        right_own.start()
        right_far.start()

    @pl.when(has_right)
    def _():
        left_near.start()
        left_own.start()
        left_far.start()

    def arrive(main, left, right):
        @pl.when(has_left)
        def _():
            left.wait_recv()

        @pl.when(has_right)
        def _():
            right.wait_recv()

        main.wait_recv()

    def step(matching, carry):
        @pl.when(matching == 0)
        def _():
            @pl.when(has_left)
            def _():
                left_own.wait_recv()

            @pl.when(has_right)
            def _():
                right_own.wait_recv()

            arrive(main_near, left_near, right_near)
            for load in loads[1:]:
                load.wait()

        @pl.when(matching == 1)
        def _():
            arrive(main_far, left_far, right_far)
            main_on.start()

            @pl.when(has_left)
            def _():
                left_on.start()

            @pl.when(has_right)
            def _():
                right_on.start()

        pair_work(
            pairing,
            offsets,
            images,
            own_left,
            own_right,
            mains.at[matching],
            lefts.at[matching],
            rights.at[matching],
            tables,
            coherence.at[matching],
            filtered.at[:, matching],
            power,
            matching,
            False,
        )
        return carry

    lax.fori_loop(0, MATCH - 1, step, 0)

    arrive(main_on, left_on, right_on)
    main_near.wait_send()
    main_far.wait_send()
    main_on.wait_send()

    @pl.when(has_left)
    def _():
        right_near.wait_send()
        right_own.wait_send()
        right_far.wait_send()
        left_on.wait_send()

    @pl.when(has_right)
    def _():
        left_near.wait_send()
        left_own.wait_send()
        left_far.wait_send()
        right_on.wait_send()


def last_kernel(
    pairing,
    offsets,
    coherence_first,
    filtered_first,
    power,
    images,
    own_left,
    own_right,
    main_last,
    left_last,
    right_last,
    *refs,
):
    tables, refs = refs[: len(TABLES)], refs[len(TABLES) :]
    coherence_far, filtered_far, coherence, filtered, early_sem, late_sem = refs
    last = MATCH - 1
    early = [
        pltpu.make_async_copy(
            coherence_first.at[m], coherence_far.at[m], early_sem.at[0, m]
        )
        for m in range(last)
    ] + [
        pltpu.make_async_copy(
            filtered_first.at[:, m], filtered_far.at[:, m], early_sem.at[1, m]
        )
        for m in range(last)
    ]
    late = [
        pltpu.make_async_copy(coherence, coherence_far.at[last], late_sem.at[0]),
        pltpu.make_async_copy(filtered, filtered_far.at[:, last], late_sem.at[1]),
    ]
    for store in early:
        store.start()
    pair_work(
        pairing,
        offsets,
        images,
        own_left,
        own_right,
        main_last,
        left_last,
        right_last,
        tables,
        coherence,
        filtered,
        power,
        last,
        True,
        late[0].start,
    )
    late[1].start()
    for store in early + late:
        store.wait()


def pair_work(
    pairing,
    offsets,
    images,
    own_left,
    own_right,
    main,
    left,
    right,
    tables,
    coherence,
    filtered,
    power,
    matching,
    known,
    stored=lambda: None,
):
    range_band, columns, azimuth_band, rows_there, rows_back, turn, turn_lanes = tables
    group, strip = lax.axis_index("acq"), lax.axis_index("rng")
    has_left, has_right = strip > 0, strip < lax.axis_size("rng") - 1
    height, breadth = main.shape[2], main.shape[3]
    wide = breadth + LANES
    upper = (group > jnp.bitwise_xor(group, matching + 1)).astype(jnp.int32)
    lines = pl.ds(pl.multiple_of(upper * height, height), height)
    lane = lax.broadcasted_iota(jnp.int32, (height, LANES), 1)
    slot = lane // REACH

    def widened(main, left, right, place):
        at_right = jnp.logical_and(slot == place, has_right)
        at_left = jnp.logical_and(slot == (place + 3) % 4, has_left)
        rim = jnp.where(at_right, right, jnp.where(at_left, left, 0.0))
        if place:
            rim = pltpu.roll(rim, LANES - REACH * place, 1)
        return jnp.concatenate([main.astype(F32), rim], 1)

    my_left, my_right = own_left[lines, :].astype(F32), own_right[lines, :].astype(F32)
    their_left, their_right = left[...].astype(F32), right[...].astype(F32)
    crossed = lax.rem(pairing[matching, 2 * group], 2)
    crossed = jnp.broadcast_to(crossed, (height, wide)) == 1
    ours, others = [
        [
            [widened(source(part, member), left, right, 2 * part + member) for part in range(2)]
            for member in range(2)
        ]
        for source, left, right in (
            (lambda part, member: images[part, member, lines, :], my_left, my_right),
            (lambda part, member: main[part, member], their_left, their_right),
        )
    ]
    fields = []
    for member in range(2):
        mine = ours[member]
        theirs = [
            jnp.where(crossed, others[1 - member][part], others[member][part])
            for part in range(2)
        ]
        fields.append(
            [
                mine[0] * theirs[0] + mine[1] * theirs[1],
                mine[1] * theirs[0] - mine[0] * theirs[1],
                theirs[0] * theirs[0] + theirs[1] * theirs[1],
            ]
            + ([] if known else [mine[0] * mine[0] + mine[1] * mine[1]])
        )

    stacked = jnp.concatenate(fields[0] + fields[1], 0)
    main_high, main_low = split(stacked[:, :breadth])
    rim = stacked[:, breadth:]
    rim_high = rim.astype(BF16)
    rest = rim - rim_high.astype(F32)
    packed = rim_high.astype(F32) + pltpu.roll(rest, LANES // 2, 1)
    band = range_band[...]
    smoothed = jnp.dot(
        jnp.concatenate([main_high, main_low, packed.astype(BF16), rim_high, main_high], 1),
        jnp.concatenate([band[:breadth], band], 0),
        preferred_element_type=F32,
    )

    def spread(member):
        count_fields = len(fields[0])
        results = [
            table_times(
                azimuth_band[0],
                azimuth_band[1],
                smoothed[(count_fields * member + f) * height :][:height],
            )
            for f in range(count_fields)
        ]
        if known:
            results.append(power[member])
        else:
            power[member] = results[3]
        return results

    def finish(member, results):
        real, imag, theirs, mine = results
        coherence[member] = (real * real + imag * imag) / (mine * theirs + EPSILON)

    groups = breadth // LANES
    count = height // PATCH + 1
    high = count * PATCH
    line_offset = offsets[0, matching]
    shift = REACH - offsets[1, matching]

    def window(field):
        turned = [
            pltpu.roll(field[:, g * LANES : (g + 1) * LANES], shift, 1)
            for g in range(groups + 1)
        ]
        return [jnp.where(lane < shift, turned[g - 1], turned[g]) for g in range(groups + 1)]

    def unwindow(pieces):
        turned = [pltpu.roll(piece, LANES - shift, 1) for piece in pieces]
        return jnp.concatenate(
            [jnp.where(lane < LANES - shift, turned[g], turned[g + 1]) for g in range(groups)], 1
        )

    windows = [[window(fields[member][part]) for part in range(2)] for member in range(2)]
    cells = [
        jnp.concatenate([windows[member][part][block] for part in range(2)], 1)
        for member in range(2)
        for block in range(groups)
    ]
    cells.append(
        jnp.concatenate(
            [
                jnp.where(
                    lane < PATCH,
                    windows[0][part][groups],
                    pltpu.roll(windows[1][part][groups], PATCH, 1),
                )
                for part in range(2)
            ],
            1,
        )
    )
    rowwise = times_table(jnp.concatenate(cells, 0), columns[0], columns[1])

    cosine, sine = [chosen(line_offset, turn[k], 1) for k in range(2)]
    upper_rows = rows_there[0] * cosine - rows_there[1] * sine
    lower_rows = rows_there[1] * cosine + rows_there[0] * sine
    line = lax.rem(lax.broadcasted_iota(jnp.int32, upper_rows.shape, 1), height)
    patch = (line - line_offset + PATCH) // PATCH
    there = split(
        jnp.concatenate(
            [
                jnp.where(patch == j, table, 0.0)
                for table in (upper_rows, lower_rows)
                for j in range(count)
            ],
            0,
        )
    )
    cosine, sine = [chosen(line_offset, turn_lanes[k], 0) for k in range(2)]
    back_rows = rows_back[0] * cosine - rows_back[1] * sine
    line = lax.rem(lax.broadcasted_iota(jnp.int32, back_rows.shape, 0), height)
    patch = (line - line_offset + PATCH) // PATCH
    place = lax.rem(lax.broadcasted_iota(jnp.int32, back_rows.shape, 1), high) // PATCH
    back_again = split(jnp.where(patch == place, back_rows, 0.0))

    first = lax.broadcasted_iota(jnp.int32, (2 * LANES, LANES), 0) % LANES // PATCH
    second = lax.broadcasted_iota(jnp.int32, (2 * LANES, LANES), 1) // PATCH
    ones = (first == second).astype(F32).astype(BF16)

    def transformed(blocks):
        upright = jnp.concatenate(
            [
                jnp.concatenate(
                    [
                        rowwise[b * height : (b + 1) * height, :LANES],
                        rowwise[b * height : (b + 1) * height, LANES:],
                    ],
                    0,
                )
                for b in blocks
            ],
            1,
        )
        return table_times(*there, upright)

    def reweighted(frequency):
        blocks = frequency.shape[1] // LANES
        real, imag = frequency[:high], frequency[high:]
        magnitude = lax.rsqrt(lax.rsqrt(real * real + imag * imag + EPSILON))
        sums = [
            jnp.sum(magnitude[j * PATCH : (j + 1) * PATCH], axis=0, keepdims=True)
            for j in range(count)
        ]
        sums = [s[:, b * LANES : (b + 1) * LANES] for b in range(blocks) for s in sums]
        if len(sums) % 8:
            sums.append(jnp.zeros((-len(sums) % 8, LANES), F32))
        total = jnp.dot(
            jnp.concatenate(split(jnp.concatenate(sums, 0)), 1),
            ones,
            preferred_element_type=F32,
        )
        inverse = 1.0 / (total * (1.0 / (PATCH * PATCH)) + EPSILON)
        scaling = jnp.concatenate(
            [
                jnp.concatenate(
                    [
                        magnitude[j * PATCH : (j + 1) * PATCH, b * LANES : (b + 1) * LANES]
                        * inverse[b * count + j : b * count + j + 1]
                        for j in range(count)
                    ],
                    0,
                )
                for b in range(blocks)
            ],
            1,
        )
        return jnp.concatenate([real * scaling, imag * scaling], 0)

    def returned(weighted):
        back = table_times(*back_again, weighted)
        return [
            jnp.concatenate(
                [
                    back[:height, b * LANES : (b + 1) * LANES],
                    back[height:, b * LANES : (b + 1) * LANES],
                ],
                1,
            )
            for b in range(weighted.shape[1] // LANES)
        ]

    chains = [range(groups), range(groups, 2 * groups), range(2 * groups, 2 * groups + 1)]
    frequency = [transformed(chains[0]), transformed(chains[1])]
    results = spread(0)
    flat = returned(reweighted(frequency[0]))
    frequency.append(transformed(chains[2]))
    finish(0, results)
    flat += returned(reweighted(frequency[1]))
    results = spread(1)
    flat += returned(reweighted(frequency[2]))
    finish(1, results)
    stored()
    final = times_table(jnp.concatenate(flat, 0), columns[2], columns[3])
    for member in range(2):
        for part in range(2):
            pieces = [
                final[b * height : (b + 1) * height, part * LANES : (part + 1) * LANES]
                for b in [*chains[member], 2 * groups]
            ]
            if member:
                pieces[-1] = pltpu.roll(pieces[-1], LANES - PATCH, 1)
            filtered[part, member] = unwindow(pieces).astype(BF16)


def per_device(images, pairing, tile_offsets):
    height, breadth = images.shape[2] // 2, images.shape[3]
    tables = [range_table(breadth), column_tables(), azimuth_table(height)]
    tables += row_tables(height)
    offsets = tile_offsets.T
    vmem, smem = pl.BlockSpec(memory_space=pltpu.VMEM), pl.BlockSpec(memory_space=pltpu.SMEM)
    anywhere = pl.BlockSpec(memory_space=pl.ANY)
    operands = [pairing, offsets, images] + [jnp.asarray(table) for table in tables]
    operands = [pltpu.with_memory_space_constraint(array, pltpu.HBM) for array in operands]
    slab, halo = (2, 2, height, breadth), (height, LANES)
    between = [
        pltpu.VMEM((MATCH - 1, 2, height, breadth), F32),
        pltpu.VMEM((2, MATCH - 1, 2, height, breadth), BF16),
        pltpu.VMEM((2, height, breadth), F32),
        pltpu.VMEM(images.shape, BF16),
        pltpu.VMEM((2 * height, LANES), BF16),
        pltpu.VMEM((2 * height, LANES), BF16),
        pltpu.VMEM(slab, BF16),
        pltpu.VMEM(halo, BF16),
        pltpu.VMEM(halo, BF16),
    ] + [pltpu.VMEM(table.shape, jnp.dtype(table.dtype)) for table in tables]
    held = pl.pallas_call(
        first_kernel,
        in_specs=[anywhere] * len(operands),
        out_specs=[vmem] * len(between),
        out_shape=between,
        scratch_shapes=[
            pltpu.SMEM(pairing.shape, jnp.int32),
            pltpu.SMEM(offsets.shape, jnp.int32),
            pltpu.VMEM((MATCH - 1,) + slab, BF16),
            pltpu.VMEM((MATCH - 1,) + halo, BF16),
            pltpu.VMEM((MATCH - 1,) + halo, BF16),
            pltpu.VMEM((2 * height, LANES), BF16),
            pltpu.VMEM((2 * height, LANES), BF16),
            pltpu.SemaphoreType.DMA((11,)),
            pltpu.SemaphoreType.DMA((11,)),
            pltpu.SemaphoreType.DMA((len(operands),)),
        ],
        compiler_params=pltpu.CompilerParams(
            collective_id=0, has_side_effects=True, vmem_limit_bytes=40 * 2**20
        ),
        name="first",
    )(*operands)
    held = [pltpu.with_memory_space_constraint(array, pltpu.VMEM) for array in held]
    return pl.pallas_call(
        last_kernel,
        in_specs=[smem] * 2 + [vmem] * len(held),
        out_specs=[anywhere] * 2,
        out_shape=[
            jax.ShapeDtypeStruct((MATCH, 2, height, breadth), F32),
            jax.ShapeDtypeStruct((2, MATCH, 2, height, breadth), BF16),
        ],
        scratch_shapes=[
            pltpu.VMEM((2, height, breadth), F32),
            pltpu.VMEM(slab, BF16),
            pltpu.SemaphoreType.DMA((2, MATCH - 1)),
            pltpu.SemaphoreType.DMA((2,)),
        ],
        compiler_params=pltpu.CompilerParams(vmem_limit_bytes=40 * 2**20),
        name="last",
    )(*operands[:2], *held)


def solution(mesh):
    in_specs = (P(None, ("stack", "acq"), None, "rng"), P(), P())
    out_specs = (
        P(None, ("stack", "acq"), None, "rng"),
        P(None, None, ("stack", "acq"), None, "rng"),
    )
    return jax.shard_map(
        per_device, mesh=mesh, in_specs=in_specs, out_specs=out_specs, check_vma=False
    )
```

```python
import jax
import jax.numpy as jnp
import ml_dtypes
import numpy as np
from jax import lax
from jax.experimental import pallas as pl
from jax.experimental.pallas import tpu as pltpu
from jax.sharding import PartitionSpec as P

MATCH = 3
REACH = 32
PATCH = 32
EPSILON = 1e-06
LANES = 128
MESH = pl.DeviceIdType.MESH
BF16 = jnp.bfloat16
F32 = jnp.float32


def halves(table):
    high = table.astype(ml_dtypes.bfloat16)
    low = (table - high.astype(np.float64)).astype(ml_dtypes.bfloat16)
    return high, low


def gauss(distance):
    weights = np.exp(-(distance.astype(np.float64) ** 2) / (2.0 * (REACH / 8.0) ** 2))
    return np.where(np.abs(distance) <= REACH, weights, 0.0)


def range_table(breadth):
    lane = np.arange(breadth + LANES)
    cell = np.where(lane >= breadth + LANES - REACH, lane - breadth - LANES, lane)
    used = cell < breadth + REACH
    weights = gauss(cell[:, None] - np.arange(breadth)[None, :])
    return np.stack(halves(weights * used[:, None]))


def azimuth_table(height):
    line = np.arange(height)
    return np.stack(halves(gauss(line[:, None] - line[None, :])))


def column_tables():
    counter = np.arange(PATCH)
    angles = 2.0 * np.pi / PATCH * (counter[:, None] * counter[None, :] % PATCH)
    eye = np.eye(LANES // PATCH)
    cosine, sine = np.kron(eye, np.cos(angles)), np.kron(eye, np.sin(angles))
    there = np.block([[cosine, -sine], [sine, cosine]])
    back = np.block([[cosine, sine], [-sine, cosine]])
    return np.stack(halves(there) + halves(back))


def row_tables(height):
    line = np.arange(height)[None, :]
    frequency = np.arange(PATCH)[:, None]
    angles = 2.0 * np.pi / PATCH * (frequency * line % PATCH)
    cosine, sine = np.cos(angles), np.sin(angles)
    first = np.concatenate([cosine, sine], 1)
    second = np.concatenate([-sine, cosine], 1)
    there = np.stack([first, second]).astype(np.float32)
    count = height // PATCH + 1
    tiled = np.concatenate([np.tile(first, (count, 1)), np.tile(second, (count, 1))], 0)
    turned = np.concatenate([np.tile(second, (count, 1)), np.tile(-first, (count, 1))], 0)
    back = np.stack([tiled.T, turned.T]).astype(np.float32) / (PATCH * PATCH)
    offset = np.arange(PATCH)[None, :]
    angles = 2.0 * np.pi / PATCH * (frequency * offset % PATCH)
    turn = np.stack([np.cos(angles), np.sin(angles)]).astype(np.float32)
    turn_lanes = np.tile(turn.transpose(0, 2, 1), (1, 1, 2 * count))
    patch = np.arange(2 * count * PATCH)[:, None] // PATCH % count
    place = np.arange(2 * height)[None, :] % height + PATCH - PATCH * patch
    place = place.astype(np.float32)
    return there, back, turn, turn_lanes, place, np.ascontiguousarray(place.T)


def sum_table():
    first = np.arange(2 * LANES)[:, None] % LANES // PATCH
    second = np.arange(LANES)[None, :] // PATCH
    return (first == second).astype(ml_dtypes.bfloat16)


def split(value):
    high = value.astype(BF16)
    return high, (value - high.astype(F32)).astype(BF16)


def times_table(value, high, low):
    value_high, value_low = split(value)
    return jnp.dot(
        jnp.concatenate([value_high, value_low, value_high], 1),
        jnp.concatenate([high, high, low], 0),
        preferred_element_type=F32,
    )


def table_times(high, low, value):
    count, depth = high.shape
    value_high, value_low = split(value)
    if depth <= LANES:
        lower = jnp.concatenate([low, jnp.zeros_like(low)], 1)
        both = jnp.dot(
            jnp.concatenate([jnp.concatenate([high, high], 1), lower], 0),
            jnp.concatenate([value_high, value_low], 0),
            preferred_element_type=F32,
        )
        return both[:count] + both[count:]
    both = jnp.dot(
        jnp.concatenate([high, low], 0), value_high, preferred_element_type=F32
    )
    rest = jnp.dot(high, value_low, preferred_element_type=F32)
    return both[:count] + both[count:] + rest


def chosen(index, table, axis):
    place = lax.broadcasted_iota(jnp.int32, table.shape, axis)
    return jnp.sum(jnp.where(place == index, table, 0.0), axis=axis, keepdims=True)


TABLES = 10


def first_kernel(
    pairing_far,
    offsets_far,
    images_far,
    *refs,
):
    tables_far, refs = refs[: TABLES], refs[TABLES :]
    (coherence, filtered, power, images, own_left, own_right, main_last, left_last, right_last), refs = (
        refs[:9],
        refs[9:],
    )
    tables, refs = refs[: TABLES], refs[TABLES :]
    pairing, offsets, mains, lefts, rights, heads, tails, send_sem, recv_sem, load_sem = refs
    stack, group, strip = lax.axis_index("stack"), lax.axis_index("acq"), lax.axis_index("rng")
    strips = lax.axis_size("rng")
    height = images.shape[2] // 2
    breadth = images.shape[3]
    near, far = jnp.bitwise_xor(group, 1), jnp.bitwise_xor(group, 2)
    has_left, has_right = strip > 0, strip < strips - 1

    pairs = [(images_far, images), (pairing_far, pairing), (offsets_far, offsets)]
    pairs += list(zip(tables_far, tables))
    loads = [
        pltpu.make_async_copy(source, target, load_sem.at[index])
        for index, (source, target) in enumerate(pairs)
    ]
    loads[0].start()
    barrier = pltpu.get_barrier_semaphore()

    def greet(g, r):
        pl.semaphore_signal(barrier, inc=1, device_id=(stack, g, r), device_id_type=MESH)

    greet(near, strip)
    greet(far, strip)

    @pl.when(has_left)
    def _():
        for g in (group, near, far):
            greet(g, strip - 1)

    @pl.when(has_right)
    def _():
        for g in (group, near, far):
            greet(g, strip + 1)

    for load in loads[1:]:
        load.start()
    loads[0].wait()
    lane = lax.broadcasted_iota(jnp.int32, (2 * height, LANES), 1)
    lane = lax.shift_right_logical(lane, REACH.bit_length() - 1)
    head = jnp.zeros((2 * height, LANES), F32)
    tail = jnp.zeros((2 * height, LANES), F32)
    for part in range(2):
        for member in range(2):
            place = 2 * part + member
            first = images[part, member, :, :LANES].astype(F32)
            last = images[part, member, :, breadth - LANES :].astype(F32)
            if place:
                first = pltpu.roll(first, REACH * place, 1)
                last = pltpu.roll(last, REACH * place, 1)
            head = jnp.where(lane == place, first, head)
            tail = jnp.where(lane == (place + 3) % 4, last, tail)
    heads[...] = head.astype(BF16)
    tails[...] = tail.astype(BF16)

    pl.semaphore_wait(
        barrier, 2 + 3 * has_left.astype(jnp.int32) + 3 * has_right.astype(jnp.int32)
    )

    def copy(source, target, index, g, r):
        return pltpu.make_async_remote_copy(
            src_ref=source,
            dst_ref=target,
            send_sem=send_sem.at[index],
            recv_sem=recv_sem.at[index],
            device_id=(stack, g, r),
            device_id_type=MESH,
        )

    def rows(g):
        return pl.ds(pl.multiple_of((g > group).astype(jnp.int32) * height, height), height)

    main_far = copy(images.at[:, :, rows(far), :], mains.at[1], 0, far, strip)
    main_near = copy(images.at[:, :, rows(near), :], mains.at[0], 1, near, strip)
    right_far = copy(heads.at[rows(far), :], rights.at[1], 2, far, strip - 1)
    right_near = copy(heads.at[rows(near), :], rights.at[0], 3, near, strip - 1)
    right_own = copy(heads, own_right, 4, group, strip - 1)
    left_far = copy(tails.at[rows(far), :], lefts.at[1], 5, far, strip + 1)
    left_near = copy(tails.at[rows(near), :], lefts.at[0], 6, near, strip + 1)
    left_own = copy(tails, own_left, 7, group, strip + 1)
    main_on = copy(mains.at[1], main_last, 8, near, strip)
    right_on = copy(rights.at[1], right_last, 9, near, strip)
    left_on = copy(lefts.at[1], left_last, 10, near, strip)

    main_near.start()
    main_far.start()

    @pl.when(has_left)
    def _():
        right_near.start()
        right_own.start()
        right_far.start()

    @pl.when(has_right)
    def _():
        left_near.start()
        left_own.start()
        left_far.start()

    def arrive(main, left, right):
        @pl.when(has_left)
        def _():
            left.wait_recv()

        @pl.when(has_right)
        def _():
            right.wait_recv()

        main.wait_recv()

    def step(matching, carry):
        @pl.when(matching == 0)
        def _():
            @pl.when(has_left)
            def _():
                left_own.wait_recv()

            @pl.when(has_right)
            def _():
                right_own.wait_recv()

            arrive(main_near, left_near, right_near)
            for load in loads[1:]:
                load.wait()

        @pl.when(matching == 1)
        def _():
            arrive(main_far, left_far, right_far)
            main_on.start()

            @pl.when(has_left)
            def _():
                left_on.start()

            @pl.when(has_right)
            def _():
                right_on.start()

        pair_work(
            pairing,
            offsets,
            images,
            own_left,
            own_right,
            mains.at[matching],
            lefts.at[matching],
            rights.at[matching],
            tables,
            coherence.at[matching],
            filtered.at[:, matching],
            power,
            matching,
            False,
        )
        return carry

    lax.fori_loop(0, MATCH - 1, step, 0)

    arrive(main_on, left_on, right_on)
    main_near.wait_send()
    main_far.wait_send()
    main_on.wait_send()

    @pl.when(has_left)
    def _():
        right_near.wait_send()
        right_own.wait_send()
        right_far.wait_send()
        left_on.wait_send()

    @pl.when(has_right)
    def _():
        left_near.wait_send()
        left_own.wait_send()
        left_far.wait_send()
        right_on.wait_send()


def last_kernel(
    pairing,
    offsets,
    coherence_first,
    filtered_first,
    power,
    images,
    own_left,
    own_right,
    main_last,
    left_last,
    right_last,
    *refs,
):
    tables, refs = refs[: TABLES], refs[TABLES :]
    coherence_far, filtered_far, coherence, filtered, early_sem, late_sem = refs
    last = MATCH - 1
    early = [
        pltpu.make_async_copy(
            coherence_first.at[m], coherence_far.at[m], early_sem.at[0, m]
        )
        for m in range(last)
    ] + [
        pltpu.make_async_copy(
            filtered_first.at[:, m], filtered_far.at[:, m], early_sem.at[1, m]
        )
        for m in range(last)
    ]
    late = [
        pltpu.make_async_copy(coherence, coherence_far.at[last], late_sem.at[0]),
        pltpu.make_async_copy(filtered, filtered_far.at[:, last], late_sem.at[1]),
    ]
    for store in early:
        store.start()
    pair_work(
        pairing,
        offsets,
        images,
        own_left,
        own_right,
        main_last,
        left_last,
        right_last,
        tables,
        coherence,
        filtered,
        power,
        last,
        True,
        late[0].start,
    )
    late[1].start()
    for store in early + late:
        store.wait()


def pair_work(
    pairing,
    offsets,
    images,
    own_left,
    own_right,
    main,
    left,
    right,
    tables,
    coherence,
    filtered,
    power,
    matching,
    known,
    stored=lambda: None,
):
    range_band, columns, azimuth_band, ones, rows_there, rows_back, turn, turn_lanes = tables[:8]
    place_there, place_back = tables[8:]
    group, strip = lax.axis_index("acq"), lax.axis_index("rng")
    has_left, has_right = strip > 0, strip < lax.axis_size("rng") - 1
    height, breadth = main.shape[2], main.shape[3]
    wide = breadth + LANES
    upper = (group > jnp.bitwise_xor(group, matching + 1)).astype(jnp.int32)
    lines = pl.ds(pl.multiple_of(upper * height, height), height)
    lane = lax.broadcasted_iota(jnp.int32, (height, LANES), 1)
    slot = lax.shift_right_logical(lane, REACH.bit_length() - 1)

    def widened(main, left, right, place):
        at_right = jnp.logical_and(slot == place, has_right)
        at_left = jnp.logical_and(slot == (place + 3) % 4, has_left)
        rim = jnp.where(at_right, right, jnp.where(at_left, left, 0.0))
        if place:
            rim = pltpu.roll(rim, LANES - REACH * place, 1)
        return jnp.concatenate([main.astype(F32), rim], 1)

    my_left, my_right = own_left[lines, :].astype(F32), own_right[lines, :].astype(F32)
    their_left, their_right = left[...].astype(F32), right[...].astype(F32)
    crossed = lax.rem(pairing[matching, 2 * group], 2)
    crossed = jnp.broadcast_to(crossed, (height, wide)) == 1
    ours, others = [
        [
            [widened(source(part, member), left, right, 2 * part + member) for part in range(2)]
            for member in range(2)
        ]
        for source, left, right in (
            (lambda part, member: images[part, member, lines, :], my_left, my_right),
            (lambda part, member: main[part, member], their_left, their_right),
        )
    ]
    fields = []
    for member in range(2):
        mine = ours[member]
        theirs = [
            jnp.where(crossed, others[1 - member][part], others[member][part])
            for part in range(2)
        ]
        fields.append(
            [
                mine[0] * theirs[0] + mine[1] * theirs[1],
                mine[1] * theirs[0] - mine[0] * theirs[1],
                theirs[0] * theirs[0] + theirs[1] * theirs[1],
            ]
            + ([] if known else [mine[0] * mine[0] + mine[1] * mine[1]])
        )

    smoothed = times_table(
        jnp.concatenate(fields[0] + fields[1], 0), range_band[0], range_band[1]
    )

    def spread(member):
        count_fields = len(fields[0])
        results = [
            table_times(
                azimuth_band[0],
                azimuth_band[1],
                smoothed[(count_fields * member + f) * height :][:height],
            )
            for f in range(count_fields)
        ]
        if known:
            results.append(power[member])
        else:
            power[member] = results[3]
        return results

    def finish(member, results):
        real, imag, theirs, mine = results
        coherence[member] = (real * real + imag * imag) / (mine * theirs + EPSILON)

    groups = breadth // LANES
    count = height // PATCH + 1
    high = count * PATCH
    line_offset = offsets[0, matching]
    shift = REACH - offsets[1, matching]

    def window(field):
        turned = [
            pltpu.roll(field[:, g * LANES : (g + 1) * LANES], shift, 1)
            for g in range(groups + 1)
        ]
        return [jnp.where(lane < shift, turned[g - 1], turned[g]) for g in range(groups + 1)]

    def unwindow(pieces):
        turned = [pltpu.roll(piece, LANES - shift, 1) for piece in pieces]
        return jnp.concatenate(
            [jnp.where(lane < LANES - shift, turned[g], turned[g + 1]) for g in range(groups)], 1
        )

    windows = [[window(fields[member][part]) for part in range(2)] for member in range(2)]
    cells = [
        jnp.concatenate([windows[member][part][block] for part in range(2)], 1)
        for member in range(2)
        for block in range(groups)
    ]
    cells.append(
        jnp.concatenate(
            [
                jnp.where(
                    lane < PATCH,
                    windows[0][part][groups],
                    pltpu.roll(windows[1][part][groups], PATCH, 1),
                )
                for part in range(2)
            ],
            1,
        )
    )
    rowwise = times_table(jnp.concatenate(cells, 0), columns[0], columns[1])

    cosine, sine = [chosen(line_offset, turn[k], 1) for k in range(2)]
    upper_rows = rows_there[0] * cosine - rows_there[1] * sine
    lower_rows = rows_there[1] * cosine + rows_there[0] * sine
    line_start = line_offset.astype(F32)

    def inside(place, table):
        from_start = place[...] - line_start
        return jnp.where(
            jnp.logical_and(from_start >= 0.0, from_start < PATCH), table, 0.0
        )

    tall = jnp.concatenate([upper_rows] * count + [lower_rows] * count, 0)
    there = split(inside(place_there, tall))
    cosine, sine = [chosen(line_offset, turn_lanes[k], 0) for k in range(2)]
    back_again = split(inside(place_back, rows_back[0] * cosine - rows_back[1] * sine))

    def transformed(blocks):
        upright = jnp.concatenate(
            [
                jnp.concatenate(
                    [
                        rowwise[b * height : (b + 1) * height, :LANES],
                        rowwise[b * height : (b + 1) * height, LANES:],
                    ],
                    0,
                )
                for b in blocks
            ],
            1,
        )
        return table_times(*there, upright)

    def reweighted(frequency):
        blocks = frequency.shape[1] // LANES
        real, imag = frequency[:high], frequency[high:]
        magnitude = lax.rsqrt(lax.rsqrt(real * real + imag * imag + EPSILON))
        sums = [
            jnp.sum(magnitude[j * PATCH : (j + 1) * PATCH], axis=0, keepdims=True)
            for j in range(count)
        ]
        sums = [s[:, b * LANES : (b + 1) * LANES] for b in range(blocks) for s in sums]
        if len(sums) % 8:
            sums.append(jnp.zeros((-len(sums) % 8, LANES), F32))
        total = jnp.dot(
            jnp.concatenate(split(jnp.concatenate(sums, 0)), 1),
            ones[...],
            preferred_element_type=F32,
        )
        inverse = 1.0 / (total * (1.0 / (PATCH * PATCH)) + EPSILON)
        scaling = jnp.concatenate(
            [
                jnp.concatenate(
                    [
                        magnitude[j * PATCH : (j + 1) * PATCH, b * LANES : (b + 1) * LANES]
                        * inverse[b * count + j : b * count + j + 1]
                        for j in range(count)
                    ],
                    0,
                )
                for b in range(blocks)
            ],
            1,
        )
        return jnp.concatenate([real * scaling, imag * scaling], 0)

    def returned(weighted):
        back = table_times(*back_again, weighted)
        return [
            jnp.concatenate(
                [
                    back[:height, b * LANES : (b + 1) * LANES],
                    back[height:, b * LANES : (b + 1) * LANES],
                ],
                1,
            )
            for b in range(weighted.shape[1] // LANES)
        ]

    chains = [range(groups), range(groups, 2 * groups), range(2 * groups, 2 * groups + 1)]
    frequency = [transformed(chains[0]), transformed(chains[1])]
    results = spread(0)
    flat = returned(reweighted(frequency[0]))
    frequency.append(transformed(chains[2]))
    finish(0, results)
    flat += returned(reweighted(frequency[1]))
    results = spread(1)
    flat += returned(reweighted(frequency[2]))
    finish(1, results)
    stored()
    final = times_table(jnp.concatenate(flat, 0), columns[2], columns[3])
    for member in range(2):
        for part in range(2):
            pieces = [
                final[b * height : (b + 1) * height, part * LANES : (part + 1) * LANES]
                for b in [*chains[member], 2 * groups]
            ]
            if member:
                pieces[-1] = pltpu.roll(pieces[-1], LANES - PATCH, 1)
            filtered[part, member] = unwindow(pieces).astype(BF16)


def per_device(images, pairing, tile_offsets):
    height, breadth = images.shape[2] // 2, images.shape[3]
    tables = [range_table(breadth), column_tables(), azimuth_table(height), sum_table()]
    tables += row_tables(height)
    offsets = tile_offsets.T
    vmem, smem = pl.BlockSpec(memory_space=pltpu.VMEM), pl.BlockSpec(memory_space=pltpu.SMEM)
    anywhere = pl.BlockSpec(memory_space=pl.ANY)
    operands = [pairing, offsets, images] + [jnp.asarray(table) for table in tables]
    operands = [pltpu.with_memory_space_constraint(array, pltpu.HBM) for array in operands]
    slab, halo = (2, 2, height, breadth), (height, LANES)
    between = [
        pltpu.VMEM((MATCH - 1, 2, height, breadth), F32),
        pltpu.VMEM((2, MATCH - 1, 2, height, breadth), BF16),
        pltpu.VMEM((2, height, breadth), F32),
        pltpu.VMEM(images.shape, BF16),
        pltpu.VMEM((2 * height, LANES), BF16),
        pltpu.VMEM((2 * height, LANES), BF16),
        pltpu.VMEM(slab, BF16),
        pltpu.VMEM(halo, BF16),
        pltpu.VMEM(halo, BF16),
    ] + [pltpu.VMEM(table.shape, jnp.dtype(table.dtype)) for table in tables]
    held = pl.pallas_call(
        first_kernel,
        in_specs=[anywhere] * len(operands),
        out_specs=[vmem] * len(between),
        out_shape=between,
        scratch_shapes=[
            pltpu.SMEM(pairing.shape, jnp.int32),
            pltpu.SMEM(offsets.shape, jnp.int32),
            pltpu.VMEM((MATCH - 1,) + slab, BF16),
            pltpu.VMEM((MATCH - 1,) + halo, BF16),
            pltpu.VMEM((MATCH - 1,) + halo, BF16),
            pltpu.VMEM((2 * height, LANES), BF16),
            pltpu.VMEM((2 * height, LANES), BF16),
            pltpu.SemaphoreType.DMA((11,)),
            pltpu.SemaphoreType.DMA((11,)),
            pltpu.SemaphoreType.DMA((len(operands),)),
        ],
        compiler_params=pltpu.CompilerParams(
            collective_id=0, has_side_effects=True, vmem_limit_bytes=40 * 2**20
        ),
        name="first",
    )(*operands)
    held = [pltpu.with_memory_space_constraint(array, pltpu.VMEM) for array in held]
    return pl.pallas_call(
        last_kernel,
        in_specs=[smem] * 2 + [vmem] * len(held),
        out_specs=[anywhere] * 2,
        out_shape=[
            jax.ShapeDtypeStruct((MATCH, 2, height, breadth), F32),
            jax.ShapeDtypeStruct((2, MATCH, 2, height, breadth), BF16),
        ],
        scratch_shapes=[
            pltpu.VMEM((2, height, breadth), F32),
            pltpu.VMEM(slab, BF16),
            pltpu.SemaphoreType.DMA((2, MATCH - 1)),
            pltpu.SemaphoreType.DMA((2,)),
        ],
        compiler_params=pltpu.CompilerParams(vmem_limit_bytes=40 * 2**20),
        name="last",
    )(*operands[:2], *held)


def solution(mesh):
    in_specs = (P(None, ("stack", "acq"), None, "rng"), P(), P())
    out_specs = (
        P(None, ("stack", "acq"), None, "rng"),
        P(None, None, ("stack", "acq"), None, "rng"),
    )
    return jax.shard_map(
        per_device, mesh=mesh, in_specs=in_specs, out_specs=out_specs, check_vma=False
    )
```

```python
import jax
import jax.numpy as jnp
import ml_dtypes
import numpy as np
from jax import lax
from jax.experimental import pallas as pl
from jax.experimental.pallas import tpu as pltpu
from jax.sharding import PartitionSpec as P

MATCH = 3
REACH = 32
PATCH = 32
EPSILON = 1e-06
LANES = 128
MESH = pl.DeviceIdType.MESH
BF16 = jnp.bfloat16
F32 = jnp.float32


def halves(table):
    high = table.astype(ml_dtypes.bfloat16)
    low = (table - high.astype(np.float64)).astype(ml_dtypes.bfloat16)
    return high, low


def gauss(distance):
    weights = np.exp(-(distance.astype(np.float64) ** 2) / (2.0 * (REACH / 8.0) ** 2))
    return np.where(np.abs(distance) <= REACH, weights, 0.0)


def range_table(breadth):
    lane = np.arange(breadth + LANES)
    cell = np.where(lane >= breadth + LANES - REACH, lane - breadth - LANES, lane)
    used = cell < breadth + REACH
    weights = gauss(cell[:, None] - np.arange(breadth)[None, :])
    return np.stack(halves(weights * used[:, None]))


def azimuth_table(height):
    line = np.arange(height)
    return np.stack(halves(gauss(line[:, None] - line[None, :])))


def column_tables():
    counter = np.arange(PATCH)
    angles = 2.0 * np.pi / PATCH * (counter[:, None] * counter[None, :] % PATCH)
    eye = np.eye(LANES // PATCH)
    cosine, sine = np.kron(eye, np.cos(angles)), np.kron(eye, np.sin(angles))
    there = np.block([[cosine, -sine], [sine, cosine]])
    back = np.block([[cosine, sine], [-sine, cosine]])
    return np.stack(halves(there) + halves(back))


def row_tables(height):
    line = np.arange(height)[None, :]
    frequency = np.arange(PATCH)[:, None]
    angles = 2.0 * np.pi / PATCH * (frequency * line % PATCH)
    cosine, sine = np.cos(angles), np.sin(angles)
    first = np.concatenate([cosine, sine], 1)
    second = np.concatenate([-sine, cosine], 1)
    there = np.stack([first, second]).astype(np.float32)
    count = height // PATCH + 1
    tiled = np.concatenate([np.tile(first, (count, 1)), np.tile(second, (count, 1))], 0)
    turned = np.concatenate([np.tile(second, (count, 1)), np.tile(-first, (count, 1))], 0)
    back = np.stack([tiled.T, turned.T]).astype(np.float32) / (PATCH * PATCH)
    offset = np.arange(PATCH)[None, :]
    angles = 2.0 * np.pi / PATCH * (frequency * offset % PATCH)
    turn = np.stack([np.cos(angles), np.sin(angles)]).astype(np.float32)
    turn_lanes = np.tile(turn.transpose(0, 2, 1), (1, 1, 2 * count))
    patch = np.arange(2 * count * PATCH)[:, None] // PATCH % count
    place = np.arange(2 * height)[None, :] % height + PATCH - PATCH * patch
    place = place.astype(np.float32)
    return there, back, turn, turn_lanes, place, np.ascontiguousarray(place.T)


def sum_table():
    first = np.arange(2 * LANES)[:, None] % LANES // PATCH
    second = np.arange(LANES)[None, :] // PATCH
    return (first == second).astype(ml_dtypes.bfloat16)


def split(value):
    high = value.astype(BF16)
    return high, (value - high.astype(F32)).astype(BF16)


def times_table(value, high, low):
    value_high, value_low = split(value)
    return jnp.dot(
        jnp.concatenate([value_high, value_low, value_high], 1),
        jnp.concatenate([high, high, low], 0),
        preferred_element_type=F32,
    )


def table_times(high, low, value):
    count, depth = high.shape
    value_high, value_low = split(value)
    if depth <= LANES:
        lower = jnp.concatenate([low, jnp.zeros_like(low)], 1)
        both = jnp.dot(
            jnp.concatenate([jnp.concatenate([high, high], 1), lower], 0),
            jnp.concatenate([value_high, value_low], 0),
            preferred_element_type=F32,
        )
        return both[:count] + both[count:]
    both = jnp.dot(
        jnp.concatenate([high, low], 0), value_high, preferred_element_type=F32
    )
    rest = jnp.dot(high, value_low, preferred_element_type=F32)
    return both[:count] + both[count:] + rest


def chosen(index, table, axis):
    place = lax.broadcasted_iota(jnp.int32, table.shape, axis)
    return jnp.sum(jnp.where(place == index, table, 0.0), axis=axis, keepdims=True)


TABLES = 10


def first_kernel(
    pairing_far,
    offsets_far,
    images_far,
    *refs,
):
    tables_far, refs = refs[: TABLES], refs[TABLES :]
    (coherence, filtered, power, images, own_left, own_right, main_last, left_last, right_last), refs = (
        refs[:9],
        refs[9:],
    )
    tables, refs = refs[:TABLES], refs[TABLES:]
    there_rows, back_rows, *refs = refs
    pairing, offsets, mains, lefts, rights, heads, tails, send_sem, recv_sem, load_sem = refs
    stack, group, strip = lax.axis_index("stack"), lax.axis_index("acq"), lax.axis_index("rng")
    strips = lax.axis_size("rng")
    height = images.shape[2] // 2
    breadth = images.shape[3]
    near, far = jnp.bitwise_xor(group, 1), jnp.bitwise_xor(group, 2)
    has_left, has_right = strip > 0, strip < strips - 1

    pairs = [(images_far, images), (pairing_far, pairing), (offsets_far, offsets)]
    pairs += list(zip(tables_far, tables))
    loads = [
        pltpu.make_async_copy(source, target, load_sem.at[index])
        for index, (source, target) in enumerate(pairs)
    ]
    loads[0].start()
    barrier = pltpu.get_barrier_semaphore()

    def greet(g, r):
        pl.semaphore_signal(barrier, inc=1, device_id=(stack, g, r), device_id_type=MESH)

    greet(near, strip)
    greet(far, strip)

    @pl.when(has_left)
    def _():
        for g in (group, near, far):
            greet(g, strip - 1)

    @pl.when(has_right)
    def _():
        for g in (group, near, far):
            greet(g, strip + 1)

    for load in loads[1:]:
        load.start()
    loads[0].wait()
    lane = lax.broadcasted_iota(jnp.int32, (2 * height, LANES), 1)
    lane = lax.shift_right_logical(lane, REACH.bit_length() - 1)
    head = jnp.zeros((2 * height, LANES), F32)
    tail = jnp.zeros((2 * height, LANES), F32)
    for part in range(2):
        for member in range(2):
            place = 2 * part + member
            first = images[part, member, :, :LANES].astype(F32)
            last = images[part, member, :, breadth - LANES :].astype(F32)
            if place:
                first = pltpu.roll(first, REACH * place, 1)
                last = pltpu.roll(last, REACH * place, 1)
            head = jnp.where(lane == place, first, head)
            tail = jnp.where(lane == (place + 3) % 4, last, tail)
    heads[...] = head.astype(BF16)
    tails[...] = tail.astype(BF16)

    pl.semaphore_wait(
        barrier, 2 + 3 * has_left.astype(jnp.int32) + 3 * has_right.astype(jnp.int32)
    )

    def copy(source, target, index, g, r):
        return pltpu.make_async_remote_copy(
            src_ref=source,
            dst_ref=target,
            send_sem=send_sem.at[index],
            recv_sem=recv_sem.at[index],
            device_id=(stack, g, r),
            device_id_type=MESH,
        )

    def rows(g):
        return pl.ds(pl.multiple_of((g > group).astype(jnp.int32) * height, height), height)

    main_far = copy(images.at[:, :, rows(far), :], mains.at[1], 0, far, strip)
    main_near = copy(images.at[:, :, rows(near), :], mains.at[0], 1, near, strip)
    right_far = copy(heads.at[rows(far), :], rights.at[1], 2, far, strip - 1)
    right_near = copy(heads.at[rows(near), :], rights.at[0], 3, near, strip - 1)
    right_own = copy(heads, own_right, 4, group, strip - 1)
    left_far = copy(tails.at[rows(far), :], lefts.at[1], 5, far, strip + 1)
    left_near = copy(tails.at[rows(near), :], lefts.at[0], 6, near, strip + 1)
    left_own = copy(tails, own_left, 7, group, strip + 1)
    main_on = copy(mains.at[1], main_last, 8, near, strip)
    right_on = copy(rights.at[1], right_last, 9, near, strip)
    left_on = copy(lefts.at[1], left_last, 10, near, strip)

    main_near.start()
    main_far.start()

    @pl.when(has_left)
    def _():
        right_near.start()
        right_own.start()
        right_far.start()

    @pl.when(has_right)
    def _():
        left_near.start()
        left_own.start()
        left_far.start()

    for load in loads[1:]:
        load.wait()
    for matching in range(MATCH):
        build_rows(offsets, tables, there_rows, back_rows, matching)

    def arrive(main, left, right):
        @pl.when(has_left)
        def _():
            left.wait_recv()

        @pl.when(has_right)
        def _():
            right.wait_recv()

        main.wait_recv()

    def step(matching, carry):
        @pl.when(matching == 0)
        def _():
            @pl.when(has_left)
            def _():
                left_own.wait_recv()

            @pl.when(has_right)
            def _():
                right_own.wait_recv()

            arrive(main_near, left_near, right_near)

        @pl.when(matching == 1)
        def _():
            arrive(main_far, left_far, right_far)
            main_on.start()

            @pl.when(has_left)
            def _():
                left_on.start()

            @pl.when(has_right)
            def _():
                right_on.start()

        pair_work(
            pairing,
            offsets,
            images,
            own_left,
            own_right,
            mains.at[matching],
            lefts.at[matching],
            rights.at[matching],
            tables,
            there_rows,
            back_rows,
            coherence.at[matching],
            filtered.at[:, matching],
            power,
            matching,
            False,
        )
        return carry

    lax.fori_loop(0, MATCH - 1, step, 0)

    arrive(main_on, left_on, right_on)
    main_near.wait_send()
    main_far.wait_send()
    main_on.wait_send()

    @pl.when(has_left)
    def _():
        right_near.wait_send()
        right_own.wait_send()
        right_far.wait_send()
        left_on.wait_send()

    @pl.when(has_right)
    def _():
        left_near.wait_send()
        left_own.wait_send()
        left_far.wait_send()
        right_on.wait_send()


def last_kernel(
    pairing,
    offsets,
    coherence_first,
    filtered_first,
    power,
    images,
    own_left,
    own_right,
    main_last,
    left_last,
    right_last,
    *refs,
):
    tables, refs = refs[: TABLES], refs[TABLES :]
    there_rows, back_rows, *refs = refs
    coherence_far, filtered_far, coherence, filtered, early_sem, late_sem = refs
    last = MATCH - 1
    early = [
        pltpu.make_async_copy(
            coherence_first.at[m], coherence_far.at[m], early_sem.at[0, m]
        )
        for m in range(last)
    ] + [
        pltpu.make_async_copy(
            filtered_first.at[:, m], filtered_far.at[:, m], early_sem.at[1, m]
        )
        for m in range(last)
    ]
    late = [
        pltpu.make_async_copy(coherence, coherence_far.at[last], late_sem.at[0]),
        pltpu.make_async_copy(filtered, filtered_far.at[:, last], late_sem.at[1]),
    ]
    for store in early:
        store.start()
    pair_work(
        pairing,
        offsets,
        images,
        own_left,
        own_right,
        main_last,
        left_last,
        right_last,
        tables,
        there_rows,
        back_rows,
        coherence,
        filtered,
        power,
        last,
        True,
        late[0].start,
    )
    late[1].start()
    for store in early + late:
        store.wait()


def build_rows(offsets, tables, there_rows, back_rows, matching):
    rows_there, rows_back, turn, turn_lanes, place_there, place_back = tables[4:]
    line_offset = offsets[0, matching]
    cosine, sine = [chosen(line_offset, turn[k], 1) for k in range(2)]
    upper_rows = rows_there[0] * cosine - rows_there[1] * sine
    lower_rows = rows_there[1] * cosine + rows_there[0] * sine
    line_start = line_offset.astype(F32)

    def inside(place, table):
        from_start = place[...] - line_start
        return jnp.where(
            jnp.logical_and(from_start >= 0.0, from_start < PATCH), table, 0.0
        )

    count = place_there.shape[0] // (2 * PATCH)
    tall = jnp.concatenate([upper_rows] * count + [lower_rows] * count, 0)
    there_rows[matching, 0], there_rows[matching, 1] = split(inside(place_there, tall))
    cosine, sine = [chosen(line_offset, turn_lanes[k], 0) for k in range(2)]
    turned = rows_back[0] * cosine - rows_back[1] * sine
    back_rows[matching, 0], back_rows[matching, 1] = split(inside(place_back, turned))


def pair_work(
    pairing,
    offsets,
    images,
    own_left,
    own_right,
    main,
    left,
    right,
    tables,
    there_rows,
    back_rows,
    coherence,
    filtered,
    power,
    matching,
    known,
    stored=lambda: None,
):
    range_band, columns, azimuth_band, ones = tables[:4]
    group, strip = lax.axis_index("acq"), lax.axis_index("rng")
    has_left, has_right = strip > 0, strip < lax.axis_size("rng") - 1
    height, breadth = main.shape[2], main.shape[3]
    wide = breadth + LANES
    upper = (group > jnp.bitwise_xor(group, matching + 1)).astype(jnp.int32)
    lines = pl.ds(pl.multiple_of(upper * height, height), height)
    lane = lax.broadcasted_iota(jnp.int32, (height, LANES), 1)
    slot = lax.shift_right_logical(lane, REACH.bit_length() - 1)

    def widened(main, left, right, place):
        at_right = jnp.logical_and(slot == place, has_right)
        at_left = jnp.logical_and(slot == (place + 3) % 4, has_left)
        rim = jnp.where(at_right, right, jnp.where(at_left, left, 0.0))
        if place:
            rim = pltpu.roll(rim, LANES - REACH * place, 1)
        return jnp.concatenate([main.astype(F32), rim], 1)

    my_left, my_right = own_left[lines, :].astype(F32), own_right[lines, :].astype(F32)
    their_left, their_right = left[...].astype(F32), right[...].astype(F32)
    crossed = lax.rem(pairing[matching, 2 * group], 2)
    crossed = jnp.broadcast_to(crossed, (height, wide)) == 1
    ours, others = [
        [
            [widened(source(part, member), left, right, 2 * part + member) for part in range(2)]
            for member in range(2)
        ]
        for source, left, right in (
            (lambda part, member: images[part, member, lines, :], my_left, my_right),
            (lambda part, member: main[part, member], their_left, their_right),
        )
    ]
    fields = []
    for member in range(2):
        mine = ours[member]
        theirs = [
            jnp.where(crossed, others[1 - member][part], others[member][part])
            for part in range(2)
        ]
        fields.append(
            [
                mine[0] * theirs[0] + mine[1] * theirs[1],
                mine[1] * theirs[0] - mine[0] * theirs[1],
                theirs[0] * theirs[0] + theirs[1] * theirs[1],
            ]
            + ([] if known else [mine[0] * mine[0] + mine[1] * mine[1]])
        )

    smoothed = times_table(
        jnp.concatenate(fields[0] + fields[1], 0), range_band[0], range_band[1]
    )

    def spread(member):
        count_fields = len(fields[0])
        results = [
            table_times(
                azimuth_band[0],
                azimuth_band[1],
                smoothed[(count_fields * member + f) * height :][:height],
            )
            for f in range(count_fields)
        ]
        if known:
            results.append(power[member])
        else:
            power[member] = results[3]
        return results

    def finish(member, results):
        real, imag, theirs, mine = results
        coherence[member] = (real * real + imag * imag) / (mine * theirs + EPSILON)

    groups = breadth // LANES
    count = height // PATCH + 1
    high = count * PATCH
    shift = REACH - offsets[1, matching]

    def window(field):
        turned = [
            pltpu.roll(field[:, g * LANES : (g + 1) * LANES], shift, 1)
            for g in range(groups + 1)
        ]
        return [jnp.where(lane < shift, turned[g - 1], turned[g]) for g in range(groups + 1)]

    def unwindow(pieces):
        turned = [pltpu.roll(piece, LANES - shift, 1) for piece in pieces]
        return jnp.concatenate(
            [jnp.where(lane < LANES - shift, turned[g], turned[g + 1]) for g in range(groups)], 1
        )

    windows = [[window(fields[member][part]) for part in range(2)] for member in range(2)]
    cells = [
        jnp.concatenate([windows[member][part][block] for part in range(2)], 1)
        for member in range(2)
        for block in range(groups)
    ]
    cells.append(
        jnp.concatenate(
            [
                jnp.where(
                    lane < PATCH,
                    windows[0][part][groups],
                    pltpu.roll(windows[1][part][groups], PATCH, 1),
                )
                for part in range(2)
            ],
            1,
        )
    )
    rowwise = times_table(jnp.concatenate(cells, 0), columns[0], columns[1])

    there = (there_rows[matching, 0], there_rows[matching, 1])
    back_again = (back_rows[matching, 0], back_rows[matching, 1])

    def transformed(blocks):
        upright = jnp.concatenate(
            [
                jnp.concatenate(
                    [
                        rowwise[b * height : (b + 1) * height, :LANES],
                        rowwise[b * height : (b + 1) * height, LANES:],
                    ],
                    0,
                )
                for b in blocks
            ],
            1,
        )
        return table_times(*there, upright)

    def reweighted(frequency):
        blocks = frequency.shape[1] // LANES
        real, imag = frequency[:high], frequency[high:]
        magnitude = lax.rsqrt(lax.rsqrt(real * real + imag * imag + EPSILON))
        sums = [
            jnp.sum(magnitude[j * PATCH : (j + 1) * PATCH], axis=0, keepdims=True)
            for j in range(count)
        ]
        sums = [s[:, b * LANES : (b + 1) * LANES] for b in range(blocks) for s in sums]
        if len(sums) % 8:
            sums.append(jnp.zeros((-len(sums) % 8, LANES), F32))
        total = jnp.dot(
            jnp.concatenate(split(jnp.concatenate(sums, 0)), 1),
            ones[...],
            preferred_element_type=F32,
        )
        inverse = 1.0 / (total * (1.0 / (PATCH * PATCH)) + EPSILON)
        scaling = jnp.concatenate(
            [
                jnp.concatenate(
                    [
                        magnitude[j * PATCH : (j + 1) * PATCH, b * LANES : (b + 1) * LANES]
                        * inverse[b * count + j : b * count + j + 1]
                        for j in range(count)
                    ],
                    0,
                )
                for b in range(blocks)
            ],
            1,
        )
        return jnp.concatenate([real * scaling, imag * scaling], 0)

    def returned(weighted):
        back = table_times(*back_again, weighted)
        return [
            jnp.concatenate(
                [
                    back[:height, b * LANES : (b + 1) * LANES],
                    back[height:, b * LANES : (b + 1) * LANES],
                ],
                1,
            )
            for b in range(weighted.shape[1] // LANES)
        ]

    chains = [range(groups), range(groups, 2 * groups), range(2 * groups, 2 * groups + 1)]
    frequency = [transformed(chains[0]), transformed(chains[1])]
    results = spread(0)
    flat = returned(reweighted(frequency[0]))
    frequency.append(transformed(chains[2]))
    finish(0, results)
    flat += returned(reweighted(frequency[1]))
    results = spread(1)
    flat += returned(reweighted(frequency[2]))
    finish(1, results)
    stored()
    final = times_table(jnp.concatenate(flat, 0), columns[2], columns[3])
    for member in range(2):
        for part in range(2):
            pieces = [
                final[b * height : (b + 1) * height, part * LANES : (part + 1) * LANES]
                for b in [*chains[member], 2 * groups]
            ]
            if member:
                pieces[-1] = pltpu.roll(pieces[-1], LANES - PATCH, 1)
            filtered[part, member] = unwindow(pieces).astype(BF16)


def per_device(images, pairing, tile_offsets):
    height, breadth = images.shape[2] // 2, images.shape[3]
    tables = [range_table(breadth), column_tables(), azimuth_table(height), sum_table()]
    tables += row_tables(height)
    offsets = tile_offsets.T
    vmem, smem = pl.BlockSpec(memory_space=pltpu.VMEM), pl.BlockSpec(memory_space=pltpu.SMEM)
    anywhere = pl.BlockSpec(memory_space=pl.ANY)
    operands = [pairing, offsets, images] + [jnp.asarray(table) for table in tables]
    operands = [pltpu.with_memory_space_constraint(array, pltpu.HBM) for array in operands]
    slab, halo = (2, 2, height, breadth), (height, LANES)
    between = [
        pltpu.VMEM((MATCH - 1, 2, height, breadth), F32),
        pltpu.VMEM((2, MATCH - 1, 2, height, breadth), BF16),
        pltpu.VMEM((2, height, breadth), F32),
        pltpu.VMEM(images.shape, BF16),
        pltpu.VMEM((2 * height, LANES), BF16),
        pltpu.VMEM((2 * height, LANES), BF16),
        pltpu.VMEM(slab, BF16),
        pltpu.VMEM(halo, BF16),
        pltpu.VMEM(halo, BF16),
    ] + [pltpu.VMEM(table.shape, jnp.dtype(table.dtype)) for table in tables]
    deep, high = 2 * height, 2 * (height + PATCH)
    between += [pltpu.VMEM((MATCH, 2, high, deep), BF16), pltpu.VMEM((MATCH, 2, deep, high), BF16)]
    held = pl.pallas_call(
        first_kernel,
        in_specs=[anywhere] * len(operands),
        out_specs=[vmem] * len(between),
        out_shape=between,
        scratch_shapes=[
            pltpu.SMEM(pairing.shape, jnp.int32),
            pltpu.SMEM(offsets.shape, jnp.int32),
            pltpu.VMEM((MATCH - 1,) + slab, BF16),
            pltpu.VMEM((MATCH - 1,) + halo, BF16),
            pltpu.VMEM((MATCH - 1,) + halo, BF16),
            pltpu.VMEM((2 * height, LANES), BF16),
            pltpu.VMEM((2 * height, LANES), BF16),
            pltpu.SemaphoreType.DMA((11,)),
            pltpu.SemaphoreType.DMA((11,)),
            pltpu.SemaphoreType.DMA((len(operands),)),
        ],
        compiler_params=pltpu.CompilerParams(
            collective_id=0, has_side_effects=True, vmem_limit_bytes=40 * 2**20
        ),
        name="first",
    )(*operands)
    held = [pltpu.with_memory_space_constraint(array, pltpu.VMEM) for array in held]
    return pl.pallas_call(
        last_kernel,
        in_specs=[smem] * 2 + [vmem] * len(held),
        out_specs=[anywhere] * 2,
        out_shape=[
            jax.ShapeDtypeStruct((MATCH, 2, height, breadth), F32),
            jax.ShapeDtypeStruct((2, MATCH, 2, height, breadth), BF16),
        ],
        scratch_shapes=[
            pltpu.VMEM((2, height, breadth), F32),
            pltpu.VMEM(slab, BF16),
            pltpu.SemaphoreType.DMA((2, MATCH - 1)),
            pltpu.SemaphoreType.DMA((2,)),
        ],
        compiler_params=pltpu.CompilerParams(vmem_limit_bytes=40 * 2**20),
        name="last",
    )(*operands[:2], *held)


def solution(mesh):
    in_specs = (P(None, ("stack", "acq"), None, "rng"), P(), P())
    out_specs = (
        P(None, ("stack", "acq"), None, "rng"),
        P(None, None, ("stack", "acq"), None, "rng"),
    )
    return jax.shard_map(
        per_device, mesh=mesh, in_specs=in_specs, out_specs=out_specs, check_vma=False
    )
```

```python
import jax
import jax.numpy as jnp
import ml_dtypes
import numpy as np
from jax import lax
from jax.experimental import pallas as pl
from jax.experimental.pallas import tpu as pltpu
from jax.sharding import PartitionSpec as P

MATCH = 3
REACH = 32
PATCH = 32
EPSILON = 1e-06
LANES = 128
MESH = pl.DeviceIdType.MESH
BF16 = jnp.bfloat16
F32 = jnp.float32


def halves(table):
    high = table.astype(ml_dtypes.bfloat16)
    low = (table - high.astype(np.float64)).astype(ml_dtypes.bfloat16)
    return high, low


def gauss(distance):
    weights = np.exp(-(distance.astype(np.float64) ** 2) / (2.0 * (REACH / 8.0) ** 2))
    return np.where(np.abs(distance) <= REACH, weights, 0.0)


def range_table(breadth):
    lane = np.arange(breadth + LANES)
    cell = np.where(lane >= breadth + LANES - REACH, lane - breadth - LANES, lane)
    used = cell < breadth + REACH
    weights = gauss(cell[:, None] - np.arange(breadth)[None, :])
    return np.stack(halves(weights * used[:, None]))


def azimuth_table(height):
    line = np.arange(height)
    return np.stack(halves(gauss(line[:, None] - line[None, :])))


def column_tables():
    counter = np.arange(PATCH)
    angles = 2.0 * np.pi / PATCH * (counter[:, None] * counter[None, :] % PATCH)
    eye = np.eye(LANES // PATCH)
    cosine, sine = np.kron(eye, np.cos(angles)), np.kron(eye, np.sin(angles))
    there = np.block([[cosine, -sine], [sine, cosine]])
    back = np.block([[cosine, sine], [-sine, cosine]])
    return np.stack(halves(there) + halves(back))


def row_tables(height):
    line = np.arange(height)[None, :]
    frequency = np.arange(PATCH)[:, None]
    angles = 2.0 * np.pi / PATCH * (frequency * line % PATCH)
    cosine, sine = np.cos(angles), np.sin(angles)
    first = np.concatenate([cosine, sine], 1)
    second = np.concatenate([-sine, cosine], 1)
    there = np.stack([first, second]).astype(np.float32)
    count = height // PATCH + 1
    tiled = np.concatenate([np.tile(first, (count, 1)), np.tile(second, (count, 1))], 0)
    turned = np.concatenate([np.tile(second, (count, 1)), np.tile(-first, (count, 1))], 0)
    back = np.stack([tiled.T, turned.T]).astype(np.float32) / (PATCH * PATCH)
    offset = np.arange(PATCH)[None, :]
    angles = 2.0 * np.pi / PATCH * (frequency * offset % PATCH)
    turn = np.stack([np.cos(angles), np.sin(angles)]).astype(np.float32)
    turn_lanes = np.tile(turn.transpose(0, 2, 1), (1, 1, 2 * count))
    patch = np.arange(2 * count * PATCH)[:, None] // PATCH % count
    place = np.arange(2 * height)[None, :] % height + PATCH - PATCH * patch
    place = place.astype(np.float32)
    return there, back, turn, turn_lanes, place, np.ascontiguousarray(place.T)


def sum_table():
    first = np.arange(2 * LANES)[:, None] % LANES // PATCH
    second = np.arange(LANES)[None, :] // PATCH
    return (first == second).astype(ml_dtypes.bfloat16)


def split(value):
    high = value.astype(BF16)
    return high, (value - high.astype(F32)).astype(BF16)


def times_table(value, high, low):
    value_high, value_low = split(value)
    return jnp.dot(
        jnp.concatenate([value_high, value_low, value_high], 1),
        jnp.concatenate([high, high, low], 0),
        preferred_element_type=F32,
    )


def table_times(high, low, value):
    count, depth = high.shape
    value_high, value_low = split(value)
    if depth <= LANES:
        lower = jnp.concatenate([low, jnp.zeros_like(low)], 1)
        both = jnp.dot(
            jnp.concatenate([jnp.concatenate([high, high], 1), lower], 0),
            jnp.concatenate([value_high, value_low], 0),
            preferred_element_type=F32,
        )
        return both[:count] + both[count:]
    both = jnp.dot(
        jnp.concatenate([high, low], 0), value_high, preferred_element_type=F32
    )
    rest = jnp.dot(high, value_low, preferred_element_type=F32)
    return both[:count] + both[count:] + rest


def chosen(index, table, axis):
    place = lax.broadcasted_iota(jnp.int32, table.shape, axis)
    return jnp.sum(jnp.where(place == index, table, 0.0), axis=axis, keepdims=True)


TABLES = 10


def first_kernel(
    pairing_far,
    offsets_far,
    images_far,
    *refs,
):
    tables_far, refs = refs[: TABLES], refs[TABLES :]
    (coherence, filtered, power, images, own_left, own_right, main_last, left_last, right_last), refs = (
        refs[:9],
        refs[9:],
    )
    tables, refs = refs[:TABLES], refs[TABLES:]
    there_rows, back_rows, *refs = refs
    pairing, offsets, mains, lefts, rights, heads, tails, send_sem, recv_sem, load_sem = refs
    stack, group, strip = lax.axis_index("stack"), lax.axis_index("acq"), lax.axis_index("rng")
    strips = lax.axis_size("rng")
    height = images.shape[2] // 2
    breadth = images.shape[3]
    near, far = jnp.bitwise_xor(group, 1), jnp.bitwise_xor(group, 2)
    has_left, has_right = strip > 0, strip < strips - 1

    pairs = [(images_far, images), (pairing_far, pairing), (offsets_far, offsets)]
    pairs += list(zip(tables_far, tables))
    loads = [
        pltpu.make_async_copy(source, target, load_sem.at[index])
        for index, (source, target) in enumerate(pairs)
    ]
    loads[0].start()
    barrier = pltpu.get_barrier_semaphore()

    def greet(g, r):
        pl.semaphore_signal(barrier, inc=1, device_id=(stack, g, r), device_id_type=MESH)

    greet(near, strip)
    greet(far, strip)

    @pl.when(has_left)
    def _():
        for g in (group, near, far):
            greet(g, strip - 1)

    @pl.when(has_right)
    def _():
        for g in (group, near, far):
            greet(g, strip + 1)

    for load in loads[1:]:
        load.start()
    loads[0].wait()
    lane = lax.broadcasted_iota(jnp.int32, (2 * height, LANES), 1)
    lane = lax.shift_right_logical(lane, REACH.bit_length() - 1)
    head = jnp.zeros((2 * height, LANES), F32)
    tail = jnp.zeros((2 * height, LANES), F32)
    for part in range(2):
        for member in range(2):
            place = 2 * part + member
            first = images[part, member, :, :LANES].astype(F32)
            last = images[part, member, :, breadth - LANES :].astype(F32)
            if place:
                first = pltpu.roll(first, REACH * place, 1)
                last = pltpu.roll(last, REACH * place, 1)
            head = jnp.where(lane == place, first, head)
            tail = jnp.where(lane == (place + 3) % 4, last, tail)
    heads[...] = head.astype(BF16)
    tails[...] = tail.astype(BF16)

    pl.semaphore_wait(
        barrier, 2 + 3 * has_left.astype(jnp.int32) + 3 * has_right.astype(jnp.int32)
    )

    def copy(source, target, index, g, r):
        return pltpu.make_async_remote_copy(
            src_ref=source,
            dst_ref=target,
            send_sem=send_sem.at[index],
            recv_sem=recv_sem.at[index],
            device_id=(stack, g, r),
            device_id_type=MESH,
        )

    def rows(g):
        return pl.ds(pl.multiple_of((g > group).astype(jnp.int32) * height, height), height)

    main_far = copy(images.at[:, :, rows(far), :], mains.at[1], 0, far, strip)
    main_near = copy(images.at[:, :, rows(near), :], mains.at[0], 1, near, strip)
    right_far = copy(heads.at[rows(far), :], rights.at[1], 2, far, strip - 1)
    right_near = copy(heads.at[rows(near), :], rights.at[0], 3, near, strip - 1)
    right_own = copy(heads, own_right, 4, group, strip - 1)
    left_far = copy(tails.at[rows(far), :], lefts.at[1], 5, far, strip + 1)
    left_near = copy(tails.at[rows(near), :], lefts.at[0], 6, near, strip + 1)
    left_own = copy(tails, own_left, 7, group, strip + 1)
    main_on = copy(mains.at[1], main_last, 8, near, strip)
    right_on = copy(rights.at[1], right_last, 9, near, strip)
    left_on = copy(lefts.at[1], left_last, 10, near, strip)

    main_near.start()
    main_far.start()

    @pl.when(has_left)
    def _():
        right_near.start()
        right_own.start()
        right_far.start()

    @pl.when(has_right)
    def _():
        left_near.start()
        left_own.start()
        left_far.start()

    for load in loads[1:]:
        load.wait()
    for matching in range(MATCH):
        build_rows(offsets, tables, there_rows, back_rows, matching)

    def arrive(main, left, right):
        @pl.when(has_left)
        def _():
            left.wait_recv()

        @pl.when(has_right)
        def _():
            right.wait_recv()

        main.wait_recv()

    def step(matching, carry):
        @pl.when(matching == 0)
        def _():
            @pl.when(has_left)
            def _():
                left_own.wait_recv()

            @pl.when(has_right)
            def _():
                right_own.wait_recv()

            arrive(main_near, left_near, right_near)

        @pl.when(matching == 1)
        def _():
            arrive(main_far, left_far, right_far)
            main_on.start()

            @pl.when(has_left)
            def _():
                left_on.start()

            @pl.when(has_right)
            def _():
                right_on.start()

        pair_work(
            pairing,
            offsets,
            images,
            own_left,
            own_right,
            mains.at[matching],
            lefts.at[matching],
            rights.at[matching],
            tables,
            there_rows,
            back_rows,
            coherence.at[matching],
            filtered.at[:, matching],
            power,
            matching,
            False,
        )
        return carry

    for matching in range(MATCH - 1):
        step(matching, 0)

    arrive(main_on, left_on, right_on)
    main_near.wait_send()
    main_far.wait_send()
    main_on.wait_send()

    @pl.when(has_left)
    def _():
        right_near.wait_send()
        right_own.wait_send()
        right_far.wait_send()
        left_on.wait_send()

    @pl.when(has_right)
    def _():
        left_near.wait_send()
        left_own.wait_send()
        left_far.wait_send()
        right_on.wait_send()


def last_kernel(
    pairing,
    offsets,
    coherence_first,
    filtered_first,
    power,
    images,
    own_left,
    own_right,
    main_last,
    left_last,
    right_last,
    *refs,
):
    tables, refs = refs[: TABLES], refs[TABLES :]
    there_rows, back_rows, *refs = refs
    coherence_far, filtered_far, coherence, filtered, early_sem, late_sem = refs
    last = MATCH - 1
    early = [
        pltpu.make_async_copy(
            coherence_first.at[m], coherence_far.at[m], early_sem.at[0, m]
        )
        for m in range(last)
    ] + [
        pltpu.make_async_copy(
            filtered_first.at[:, m], filtered_far.at[:, m], early_sem.at[1, m]
        )
        for m in range(last)
    ]
    late = [
        pltpu.make_async_copy(coherence, coherence_far.at[last], late_sem.at[0]),
        pltpu.make_async_copy(filtered, filtered_far.at[:, last], late_sem.at[1]),
    ]
    for store in early:
        store.start()
    pair_work(
        pairing,
        offsets,
        images,
        own_left,
        own_right,
        main_last,
        left_last,
        right_last,
        tables,
        there_rows,
        back_rows,
        coherence,
        filtered,
        power,
        last,
        True,
        late[0].start,
    )
    late[1].start()
    for store in early + late:
        store.wait()


def build_rows(offsets, tables, there_rows, back_rows, matching):
    rows_there, rows_back, turn, turn_lanes, place_there, place_back = tables[4:]
    line_offset = offsets[0, matching]
    cosine, sine = [chosen(line_offset, turn[k], 1) for k in range(2)]
    upper_rows = rows_there[0] * cosine - rows_there[1] * sine
    lower_rows = rows_there[1] * cosine + rows_there[0] * sine
    line_start = line_offset.astype(F32)

    def inside(place, table):
        from_start = place[...] - line_start
        return jnp.where(
            jnp.logical_and(from_start >= 0.0, from_start < PATCH), table, 0.0
        )

    count = place_there.shape[0] // (2 * PATCH)
    tall = jnp.concatenate([upper_rows] * count + [lower_rows] * count, 0)
    there_rows[matching, 0], there_rows[matching, 1] = split(inside(place_there, tall))
    cosine, sine = [chosen(line_offset, turn_lanes[k], 0) for k in range(2)]
    turned = rows_back[0] * cosine - rows_back[1] * sine
    back_rows[matching, 0], back_rows[matching, 1] = split(inside(place_back, turned))


def pair_work(
    pairing,
    offsets,
    images,
    own_left,
    own_right,
    main,
    left,
    right,
    tables,
    there_rows,
    back_rows,
    coherence,
    filtered,
    power,
    matching,
    known,
    stored=lambda: None,
):
    range_band, columns, azimuth_band, ones = tables[:4]
    group, strip = lax.axis_index("acq"), lax.axis_index("rng")
    has_left, has_right = strip > 0, strip < lax.axis_size("rng") - 1
    height, breadth = main.shape[2], main.shape[3]
    wide = breadth + LANES
    upper = (group > jnp.bitwise_xor(group, matching + 1)).astype(jnp.int32)
    lines = pl.ds(pl.multiple_of(upper * height, height), height)
    lane = lax.broadcasted_iota(jnp.int32, (height, LANES), 1)
    slot = lax.shift_right_logical(lane, REACH.bit_length() - 1)

    def widened(main, left, right, place):
        at_right = jnp.logical_and(slot == place, has_right)
        at_left = jnp.logical_and(slot == (place + 3) % 4, has_left)
        rim = jnp.where(at_right, right, jnp.where(at_left, left, 0.0))
        if place:
            rim = pltpu.roll(rim, LANES - REACH * place, 1)
        return jnp.concatenate([main.astype(F32), rim], 1)

    my_left, my_right = own_left[lines, :].astype(F32), own_right[lines, :].astype(F32)
    their_left, their_right = left[...].astype(F32), right[...].astype(F32)
    crossed = lax.rem(pairing[matching, 2 * group], 2)
    crossed = jnp.broadcast_to(crossed, (height, wide)) == 1
    ours, others = [
        [
            [widened(source(part, member), left, right, 2 * part + member) for part in range(2)]
            for member in range(2)
        ]
        for source, left, right in (
            (lambda part, member: images[part, member, lines, :], my_left, my_right),
            (lambda part, member: main[part, member], their_left, their_right),
        )
    ]
    fields = []
    for member in range(2):
        mine = ours[member]
        theirs = [
            jnp.where(crossed, others[1 - member][part], others[member][part])
            for part in range(2)
        ]
        fields.append(
            [
                mine[0] * theirs[0] + mine[1] * theirs[1],
                mine[1] * theirs[0] - mine[0] * theirs[1],
                theirs[0] * theirs[0] + theirs[1] * theirs[1],
            ]
            + ([] if known else [mine[0] * mine[0] + mine[1] * mine[1]])
        )

    smoothed = times_table(
        jnp.concatenate(fields[0] + fields[1], 0), range_band[0], range_band[1]
    )

    def spread(member):
        count_fields = len(fields[0])
        results = [
            table_times(
                azimuth_band[0],
                azimuth_band[1],
                smoothed[(count_fields * member + f) * height :][:height],
            )
            for f in range(count_fields)
        ]
        if known:
            results.append(power[member])
        else:
            power[member] = results[3]
        return results

    def finish(member, results):
        real, imag, theirs, mine = results
        coherence[member] = (real * real + imag * imag) / (mine * theirs + EPSILON)

    groups = breadth // LANES
    count = height // PATCH + 1
    high = count * PATCH
    shift = REACH - offsets[1, matching]

    def window(field):
        turned = [
            pltpu.roll(field[:, g * LANES : (g + 1) * LANES], shift, 1)
            for g in range(groups + 1)
        ]
        return [jnp.where(lane < shift, turned[g - 1], turned[g]) for g in range(groups + 1)]

    def unwindow(pieces):
        turned = [pltpu.roll(piece, LANES - shift, 1) for piece in pieces]
        return jnp.concatenate(
            [jnp.where(lane < LANES - shift, turned[g], turned[g + 1]) for g in range(groups)], 1
        )

    windows = [[window(fields[member][part]) for part in range(2)] for member in range(2)]
    cells = [
        jnp.concatenate([windows[member][part][block] for part in range(2)], 1)
        for member in range(2)
        for block in range(groups)
    ]
    cells.append(
        jnp.concatenate(
            [
                jnp.where(
                    lane < PATCH,
                    windows[0][part][groups],
                    pltpu.roll(windows[1][part][groups], PATCH, 1),
                )
                for part in range(2)
            ],
            1,
        )
    )
    rowwise = times_table(jnp.concatenate(cells, 0), columns[0], columns[1])

    there = (there_rows[matching, 0], there_rows[matching, 1])
    back_again = (back_rows[matching, 0], back_rows[matching, 1])

    def transformed(blocks):
        upright = jnp.concatenate(
            [
                jnp.concatenate(
                    [
                        rowwise[b * height : (b + 1) * height, :LANES],
                        rowwise[b * height : (b + 1) * height, LANES:],
                    ],
                    0,
                )
                for b in blocks
            ],
            1,
        )
        return table_times(*there, upright)

    def reweighted(frequency):
        blocks = frequency.shape[1] // LANES
        real, imag = frequency[:high], frequency[high:]
        magnitude = lax.rsqrt(lax.rsqrt(real * real + imag * imag + EPSILON))
        sums = [
            jnp.sum(magnitude[j * PATCH : (j + 1) * PATCH], axis=0, keepdims=True)
            for j in range(count)
        ]
        sums = [s[:, b * LANES : (b + 1) * LANES] for b in range(blocks) for s in sums]
        if len(sums) % 8:
            sums.append(jnp.zeros((-len(sums) % 8, LANES), F32))
        total = jnp.dot(
            jnp.concatenate(split(jnp.concatenate(sums, 0)), 1),
            ones[...],
            preferred_element_type=F32,
        )
        inverse = 1.0 / (total * (1.0 / (PATCH * PATCH)) + EPSILON)
        scaling = jnp.concatenate(
            [
                jnp.concatenate(
                    [
                        magnitude[j * PATCH : (j + 1) * PATCH, b * LANES : (b + 1) * LANES]
                        * inverse[b * count + j : b * count + j + 1]
                        for j in range(count)
                    ],
                    0,
                )
                for b in range(blocks)
            ],
            1,
        )
        return jnp.concatenate([real * scaling, imag * scaling], 0)

    def returned(weighted):
        back = table_times(*back_again, weighted)
        return [
            jnp.concatenate(
                [
                    back[:height, b * LANES : (b + 1) * LANES],
                    back[height:, b * LANES : (b + 1) * LANES],
                ],
                1,
            )
            for b in range(weighted.shape[1] // LANES)
        ]

    chains = [range(groups), range(groups, 2 * groups), range(2 * groups, 2 * groups + 1)]
    frequency = [transformed(chains[0]), transformed(chains[1])]
    results = spread(0)
    flat = returned(reweighted(frequency[0]))
    frequency.append(transformed(chains[2]))
    finish(0, results)
    flat += returned(reweighted(frequency[1]))
    results = spread(1)
    flat += returned(reweighted(frequency[2]))
    finish(1, results)
    stored()
    final = times_table(jnp.concatenate(flat, 0), columns[2], columns[3])
    for member in range(2):
        for part in range(2):
            pieces = [
                final[b * height : (b + 1) * height, part * LANES : (part + 1) * LANES]
                for b in [*chains[member], 2 * groups]
            ]
            if member:
                pieces[-1] = pltpu.roll(pieces[-1], LANES - PATCH, 1)
            filtered[part, member] = unwindow(pieces).astype(BF16)


def per_device(images, pairing, tile_offsets):
    height, breadth = images.shape[2] // 2, images.shape[3]
    tables = [range_table(breadth), column_tables(), azimuth_table(height), sum_table()]
    tables += row_tables(height)
    offsets = tile_offsets.T
    vmem, smem = pl.BlockSpec(memory_space=pltpu.VMEM), pl.BlockSpec(memory_space=pltpu.SMEM)
    anywhere = pl.BlockSpec(memory_space=pl.ANY)
    operands = [pairing, offsets, images] + [jnp.asarray(table) for table in tables]
    operands = [pltpu.with_memory_space_constraint(array, pltpu.HBM) for array in operands]
    slab, halo = (2, 2, height, breadth), (height, LANES)
    between = [
        pltpu.VMEM((MATCH - 1, 2, height, breadth), F32),
        pltpu.VMEM((2, MATCH - 1, 2, height, breadth), BF16),
        pltpu.VMEM((2, height, breadth), F32),
        pltpu.VMEM(images.shape, BF16),
        pltpu.VMEM((2 * height, LANES), BF16),
        pltpu.VMEM((2 * height, LANES), BF16),
        pltpu.VMEM(slab, BF16),
        pltpu.VMEM(halo, BF16),
        pltpu.VMEM(halo, BF16),
    ] + [pltpu.VMEM(table.shape, jnp.dtype(table.dtype)) for table in tables]
    deep, high = 2 * height, 2 * (height + PATCH)
    between += [pltpu.VMEM((MATCH, 2, high, deep), BF16), pltpu.VMEM((MATCH, 2, deep, high), BF16)]
    held = pl.pallas_call(
        first_kernel,
        in_specs=[anywhere] * len(operands),
        out_specs=[vmem] * len(between),
        out_shape=between,
        scratch_shapes=[
            pltpu.SMEM(pairing.shape, jnp.int32),
            pltpu.SMEM(offsets.shape, jnp.int32),
            pltpu.VMEM((MATCH - 1,) + slab, BF16),
            pltpu.VMEM((MATCH - 1,) + halo, BF16),
            pltpu.VMEM((MATCH - 1,) + halo, BF16),
            pltpu.VMEM((2 * height, LANES), BF16),
            pltpu.VMEM((2 * height, LANES), BF16),
            pltpu.SemaphoreType.DMA((11,)),
            pltpu.SemaphoreType.DMA((11,)),
            pltpu.SemaphoreType.DMA((len(operands),)),
        ],
        compiler_params=pltpu.CompilerParams(
            collective_id=0, has_side_effects=True, vmem_limit_bytes=40 * 2**20
        ),
        name="first",
    )(*operands)
    held = [pltpu.with_memory_space_constraint(array, pltpu.VMEM) for array in held]
    return pl.pallas_call(
        last_kernel,
        in_specs=[smem] * 2 + [vmem] * len(held),
        out_specs=[anywhere] * 2,
        out_shape=[
            jax.ShapeDtypeStruct((MATCH, 2, height, breadth), F32),
            jax.ShapeDtypeStruct((2, MATCH, 2, height, breadth), BF16),
        ],
        scratch_shapes=[
            pltpu.VMEM((2, height, breadth), F32),
            pltpu.VMEM(slab, BF16),
            pltpu.SemaphoreType.DMA((2, MATCH - 1)),
            pltpu.SemaphoreType.DMA((2,)),
        ],
        compiler_params=pltpu.CompilerParams(vmem_limit_bytes=40 * 2**20),
        name="last",
    )(*operands[:2], *held)


def solution(mesh):
    in_specs = (P(None, ("stack", "acq"), None, "rng"), P(), P())
    out_specs = (
        P(None, ("stack", "acq"), None, "rng"),
        P(None, None, ("stack", "acq"), None, "rng"),
    )
    return jax.shard_map(
        per_device, mesh=mesh, in_specs=in_specs, out_specs=out_specs, check_vma=False
    )
```
